32 devices in a mesh: fsdp: 32 (over z, y, x, core).
Axes of the slice: x: 2, y: 2, z: 4, core: 2. Of those that a mesh axis runs over, the one named last changes fastest.
Arguments:
- inputs: bfloat16 [2, 32, 384, 1024], P(None, 'fsdp'), may hold values from -6 to 6
- cotangent: bfloat16 [2, 32, 384, 1024], P(None, 'fsdp'), may hold values from -6 to 6
- lengths: int32 [2, 32], replicated, may hold values from 96 to 384, as said below
- owners: int32 [2, 32], replicated, may hold values from 0 to 31, each once within a row
- attn_gain: bfloat16 [1024], P('fsdp'), may hold values from 0.25 to 1.75
- query_weight: bfloat16 [1024, 1024], P('fsdp'), may hold values from -0.1875 to 0.1875
- key_weight: bfloat16 [1024, 1024], P('fsdp'), may hold values from -0.1875 to 0.1875
- value_weight: bfloat16 [1024, 1024], P('fsdp'), may hold values from -0.1875 to 0.1875
- beta_weight: bfloat16 [1024, 8], P('fsdp'), may hold values from -0.1875 to 0.1875
- query_conv: bfloat16 [4, 1024], P(None, 'fsdp'), may hold values from -3 to 3
- key_conv: bfloat16 [4, 1024], P(None, 'fsdp'), may hold values from -3 to 3
- value_conv: bfloat16 [4, 1024], P(None, 'fsdp'), may hold values from -3 to 3
- out_gain: bfloat16 [128], P('fsdp'), may hold values from 0.25 to 1.75
- out_weight: bfloat16 [1024, 1024], P(None, 'fsdp'), may hold values from -0.1875 to 0.1875
- mlp_gain: bfloat16 [1024], P('fsdp'), may hold values from 0.25 to 1.75
- gate_weight: bfloat16 [1024, 2816], P('fsdp'), may hold values from -0.1875 to 0.1875
- up_weight: bfloat16 [1024, 2816], P('fsdp'), may hold values from -0.1875 to 0.1875
- down_weight: bfloat16 [2816, 1024], P(None, 'fsdp'), may hold values from -0.109375 to 0.109375
Outputs:
- block_out: bfloat16 [2, 32, 384, 1024], P(None, 'fsdp')
- input_gradient_rows: bfloat16 [2, 32, 384, 1024], P(None, 'fsdp')
- attn_gain_grad: float32 [1024], P('fsdp')
- query_weight_grad: float32 [1024, 1024], P('fsdp')
- key_weight_grad: float32 [1024, 1024], P('fsdp')
- value_weight_grad: float32 [1024, 1024], P('fsdp')
- beta_weight_grad: float32 [1024, 8], P('fsdp')
- query_conv_grad: float32 [4, 1024], P(None, 'fsdp')
- key_conv_grad: float32 [4, 1024], P(None, 'fsdp')
- value_conv_grad: float32 [4, 1024], P(None, 'fsdp')
- out_gain_grad: float32 [128], P('fsdp')
- out_weight_grad: float32 [1024, 1024], P(None, 'fsdp')
- mlp_gain_grad: float32 [1024], P('fsdp')
- gate_weight_grad: float32 [1024, 2816], P('fsdp')
- up_weight_grad: float32 [1024, 2816], P('fsdp')
- down_weight_grad: float32 [2816, 1024], P(None, 'fsdp')
The draws below stay inside these ranges and needn't reach their ends.
Inputs may be any that keep to these rules, and one draw needn't show every extreme that they name: `lengths`: in every micro-batch one sequence has exactly 384 tokens. Each row of owners names every device once.
All inputs are finite; a program needn't handle non-finite values.
Results may differ from the reference program's by a relative error of at most 0.012.
Values may be sent and summed in bfloat16 or wider, within the bound.
A program may use at most 256 MiB of HBM per device.

```python
import math
import jax
import jax.numpy as jnp
from jax import lax

HEADS = 8
HEAD = 128
D = 1024
FF = 2816
CONV = 4
SPAN = 64
MICRO = 2
CAP = 384
SOURCES = 32


def draw_lengths(key, part):
    base_key, pick_key = jax.random.split(key)
    drawn = jax.random.randint(base_key, (MICRO, SOURCES), CAP // 4, CAP + 1)
    chosen = jax.random.randint(pick_key, (MICRO, 1), 0, SOURCES)
    column_ids = jnp.arange(SOURCES)[None, :]
    return jnp.where(column_ids == chosen, CAP, drawn).astype(jnp.int32)


def spiked(entries, key, source, target, shards_of, factor):
    owner, partner = [(jnp.arange(entries.shape[axis_at]) // (entries.shape[axis_at] // shards_of)).reshape([-1 if axis == axis_at else 1 for axis in range(entries.ndim)]) for axis_at in (source, target)]
    chosen = jax.random.permutation(key, shards_of)[partner]
    strong = (owner == chosen) | (owner == (partner + shards_of // 2) % shards_of)
    return jnp.where(strong, factor * entries, entries)


def block_levels(stream_key, shape, pieces, least, largest):
    factor_of, own = 1.0, jax.random.fold_in(stream_key, 6)
    for axis_at, blocks in pieces:
        draws = jnp.exp(jax.random.uniform(jax.random.fold_in(own, axis_at), (blocks,), jnp.float32, least / len(pieces), largest / len(pieces)))
        factor_of = factor_of * jnp.repeat(draws, shape[axis_at] // blocks).reshape([-1 if axis == axis_at else 1 for axis in range(len(shape))])
    return factor_of


def scatter_about(own_key, extent, deviation, limit, cuts=(), kind=jnp.bfloat16):
    level = block_levels(own_key, extent, cuts, -0.22, 0.18) if cuts else 1.0
    entries = jax.random.normal(own_key, extent, jnp.float32) * deviation * level
    return jnp.minimum(jnp.maximum(entries, -limit), limit).astype(kind)


def bell_draw_with(stream_key, shape, width, reach, cuts, heavy, kind=jnp.bfloat16):
    values = width * jax.random.normal(stream_key, shape, jnp.float32)
    if cuts:
        values = values * block_levels(stream_key, shape, cuts, -0.22, 0.18)
    return jnp.clip(spiked(values, jax.random.fold_in(stream_key, 3), *heavy), -reach, reach).astype(kind)


def setup_inputs(seed: int = 0) -> dict:
    streams_of = jax.random.split(jax.random.key(seed), 19)
    return {
        "inputs": scatter_about(streams_of[0], (MICRO, SOURCES, CAP, D), 1.0, 6.0, ((1, 32),)),
        "cotangent": bell_draw_with(streams_of[1], (MICRO, SOURCES, CAP, D), 1.0, 6.0, ((1, 32),), (1, 3, 32, 2.75)),
        "lengths": draw_lengths(jax.random.fold_in(streams_of[18], 71), 0),
        "owners": jax.vmap(lambda own: jax.random.permutation(own, SOURCES))(jax.random.split(streams_of[3], MICRO)).reshape((MICRO, SOURCES)).astype(jnp.int32),
        "attn_gain": jnp.clip(1.0 + 0.15 * jax.random.normal(streams_of[4], (D,), jnp.float32), 0.25, 1.75).astype(jnp.bfloat16),
        "query_weight": scatter_about(streams_of[5], (D, D), D ** -0.5, 0.1875, ((0, 32),)),
        "key_weight": scatter_about(streams_of[6], (D, D), D ** -0.5, 0.1875, ((0, 32),)),
        "value_weight": scatter_about(streams_of[7], (D, D), D ** -0.5, 0.1875, ((0, 32),)),
        "beta_weight": scatter_about(streams_of[8], (D, HEADS), D ** -0.5, 0.1875, ((0, 32),)),
        "query_conv": scatter_about(streams_of[9], (CONV, D), CONV ** -0.5, 3.0, ((1, 32),)),
        "key_conv": scatter_about(streams_of[10], (CONV, D), CONV ** -0.5, 3.0, ((1, 32),)),
        "value_conv": scatter_about(streams_of[11], (CONV, D), CONV ** -0.5, 3.0, ((1, 32),)),
        "out_gain": jnp.clip(1.0 + 0.15 * jax.random.normal(streams_of[12], (HEAD,), jnp.float32), 0.25, 1.75).astype(jnp.bfloat16),
        "out_weight": scatter_about(streams_of[13], (D, D), D ** -0.5, 0.1875, ((1, 32),)),
        "mlp_gain": jnp.clip(1.0 + 0.15 * jax.random.normal(streams_of[14], (D,), jnp.float32), 0.25, 1.75).astype(jnp.bfloat16),
        "gate_weight": scatter_about(streams_of[15], (D, FF), D ** -0.5, 0.1875, ((0, 32),)),
        "up_weight": scatter_about(streams_of[16], (D, FF), D ** -0.5, 0.1875, ((0, 32),)),
        "down_weight": scatter_about(streams_of[17], (FF, D), FF ** -0.5, 0.109375, ((1, 32),)),
    }


NORM_EPS = 1e-05
UNIT_EPS = 1e-06
HIGHEST = lax.Precision.HIGHEST

@jax.custom_vjp
def low(v):
    return lax.optimization_barrier(v.astype(jnp.bfloat16)).astype(jnp.float32)

@jax.custom_vjp
def low_back(v):
    return v

def low_keep(v):
    return (low(v), None)

def low_pass(kept, grad):
    return (grad,)

def back_keep(v):
    return (v, None)

def back_low(kept, grad):
    return (low(grad),)
low.defvjp(low_keep, low_pass)
low_back.defvjp(back_keep, back_low)

def rms_norm(values, norm_gain):
    return values * lax.rsqrt(lax.optimization_barrier(jnp.mean(values * values, axis=-1, keepdims=True)) + NORM_EPS) * norm_gain

def unit_heads(values):
    by_head = values.reshape(values.shape[0], HEADS, HEAD)
    scaled = by_head * lax.rsqrt(lax.optimization_barrier(jnp.sum(by_head * by_head, axis=-1, keepdims=True)) + UNIT_EPS)
    return scaled.reshape(values.shape)

def causal_conv(values, conv_taps):
    running = values * conv_taps[0]
    for offset in range(1, conv_taps.shape[0]):
        shifted = jnp.pad(values, ((offset, 0), (0, 0)))[:values.shape[0]]
        running = running + shifted * conv_taps[offset]
    return running

def inverse_unit_lower(strict):
    eye_mat = jnp.eye(strict.shape[-1], dtype=strict.dtype)
    result = eye_mat - strict
    power_mat = strict
    for doubling in range(strict.shape[-1].bit_length() - 2):
        power_mat = jnp.einsum('bij,bjk->bik', power_mat, power_mat, precision=HIGHEST)
        result = result + jnp.einsum('bij,bjk->bik', result, power_mat, precision=HIGHEST)
    return result

def delta_rule(queries, key_rows, value_rows, strength):
    batch_size, length, key_depth = queries.shape
    blocks = length // SPAN

    def by_block(values):
        return jnp.moveaxis(values.reshape((batch_size, blocks, SPAN) + values.shape[2:]), 1, 0)

    def span_step(state_mat, block_in):
        query_blk, key_blk, value_blk, beta_blk = block_in
        scaled_keys = key_blk * beta_blk[..., None]
        strict = jnp.tril(jnp.einsum('bid,bjd->bij', scaled_keys, key_blk, precision=HIGHEST), -1)
        inverse = inverse_unit_lower(strict)
        weight_rows = jnp.einsum('bij,bjd->bid', inverse, scaled_keys, precision=HIGHEST)
        update_rows = jnp.einsum('bij,bje->bie', inverse, value_blk * beta_blk[..., None], precision=HIGHEST)
        fresh_rows = update_rows - jnp.einsum('bcd,bde->bce', weight_rows, state_mat, precision=HIGHEST)
        scores = jnp.tril(jnp.einsum('bid,bjd->bij', query_blk, key_blk, precision=HIGHEST))
        output = jnp.einsum('bcd,bde->bce', query_blk, state_mat, precision=HIGHEST)
        output = output + jnp.einsum('bij,bje->bie', scores, fresh_rows, precision=HIGHEST)
        state_mat = state_mat + jnp.einsum('bcd,bce->bde', key_blk, fresh_rows, precision=HIGHEST)
        return (state_mat, output)
    initial = jnp.zeros((batch_size, key_depth, value_rows.shape[-1]), jnp.float32)
    final_state, outputs = lax.scan(jax.checkpoint(span_step), initial, (by_block(queries), by_block(key_rows), by_block(value_rows), by_block(strength)))
    return jnp.moveaxis(outputs, 0, 1).reshape(batch_size, length, -1)

def prepare(query_pre, key_pre, value_pre, beta_pre, query_taps, key_taps, value_taps):
    queries = unit_heads(jax.nn.silu(causal_conv(query_pre, query_taps)))
    key_rows = unit_heads(jax.nn.silu(causal_conv(key_pre, key_taps)))
    value_rows = jax.nn.silu(causal_conv(value_pre, value_taps))
    return (queries, key_rows, value_rows, jax.nn.sigmoid(beta_pre))

def token_mixer(queries, key_rows, value_rows, strength, norm_gain):
    length = queries.shape[0]

    def to_heads(values):
        return values.reshape(length, HEADS, HEAD).transpose(1, 0, 2)
    mixed_rows = delta_rule(to_heads(queries), to_heads(key_rows), to_heads(value_rows), strength.T)
    normed = rms_norm(mixed_rows.transpose(1, 0, 2), norm_gain)
    return normed.reshape(length, HEADS * HEAD)

def swiglu(gate_pre, up_pre):
    return jax.nn.silu(gate_pre) * up_pre

def matmul(left_mat, right_mat):
    return jnp.einsum('...d,de->...e', left_mat, right_mat, precision=HIGHEST)

def block_rows(rows_in, params):
    attn_gain, query_weight, key_weight, value_weight, beta_weight, query_conv, key_conv, value_conv, out_gain, out_weight, mlp_gain, gate_weight, up_weight, down_weight = params
    attn_in = low(rms_norm(rows_in, attn_gain))
    query_pre = low_back(matmul(attn_in, query_weight))
    key_pre = low_back(matmul(attn_in, key_weight))
    value_pre = low_back(matmul(attn_in, value_weight))
    beta_pre = low_back(matmul(attn_in, beta_weight))
    prepared = jax.vmap(prepare, in_axes=(0, 0, 0, 0, None, None, None))(query_pre, key_pre, value_pre, beta_pre, query_conv, key_conv, value_conv)
    queries = low(prepared[0])
    key_rows = low(prepared[1])
    value_rows = low(prepared[2])
    mixed_rows = jax.vmap(token_mixer, in_axes=(0, 0, 0, 0, None))(queries, key_rows, value_rows, prepared[3], out_gain)
    mixed_low = low(mixed_rows)
    hidden = rows_in + low_back(matmul(mixed_low, out_weight))
    mlp_in = low(rms_norm(hidden, mlp_gain))
    gate_pre = low_back(matmul(mlp_in, gate_weight))
    up_pre = low_back(matmul(mlp_in, up_weight))
    activated = low(swiglu(gate_pre, up_pre))
    return hidden + low_back(matmul(activated, down_weight))

def reference(inputs, cotangent, lengths, owners, attn_gain, query_weight, key_weight, value_weight, beta_weight, query_conv, key_conv, value_conv, out_gain, out_weight, mlp_gain, gate_weight, up_weight, down_weight):
    params = tuple((weight.astype(jnp.float32) for weight in (attn_gain, query_weight, key_weight, value_weight, beta_weight, query_conv, key_conv, value_conv, out_gain, out_weight, mlp_gain, gate_weight, up_weight, down_weight)))
    microbatch_count, partition_count, total_row_count, hidden_width = inputs.shape
    seq_ends = jnp.cumsum(lengths, axis=1)
    starts = seq_ends - lengths
    part_ids = jnp.arange(partition_count, dtype=jnp.int32)
    match_mat = (owners[:, None, :] == part_ids[None, :, None]).astype(jnp.int32)
    own_start = lax.optimization_barrier(jnp.sum(match_mat * starts[:, None, :], axis=2))
    own_len = lax.optimization_barrier(jnp.sum(match_mat * lengths[:, None, :], axis=2))
    positions = jnp.arange(total_row_count, dtype=jnp.int32)
    stream_pos = own_start[:, :, None] + positions[None, None, :]
    active_rows = positions[None, None, :] < own_len[:, :, None]
    flat_index = jnp.where(active_rows, stream_pos % partition_count * total_row_count + stream_pos // partition_count, 0).astype(jnp.int32)
    active_flags = active_rows.astype(jnp.float32)[..., None]
    sequences = microbatch_count * partition_count
    group_size = math.gcd(sequences, max(1, 4096 // total_row_count))

    def forward(stream_rows, weights):
        flat_rows = stream_rows.reshape(microbatch_count, partition_count * total_row_count, hidden_width)
        selected_rows = jax.vmap(lambda source_rows, row_index: jnp.take(source_rows, row_index.reshape(-1), axis=0))(flat_rows, flat_index)
        owned_rows = selected_rows.reshape(microbatch_count, partition_count, total_row_count, hidden_width) * active_flags
        grouped = owned_rows.reshape(sequences // group_size, group_size, total_row_count, hidden_width)
        step_outputs = lax.map(jax.checkpoint(lambda group_rows: block_rows(group_rows, weights)), grouped)
        return step_outputs.reshape(microbatch_count, partition_count, total_row_count, hidden_width) * active_flags
    out_rows, vector_jacobian = jax.vjp(forward, inputs.astype(jnp.float32), params)
    input_gradient_rows, weight_gradients = vector_jacobian(cotangent.astype(jnp.float32) * active_flags)
    attn_gain_grad, query_weight_grad, key_weight_grad, value_weight_grad, beta_weight_grad, query_conv_grad, key_conv_grad, value_conv_grad, out_gain_grad, out_weight_grad, mlp_gain_grad, gate_weight_grad, up_weight_grad, down_weight_grad = weight_gradients
    return (out_rows.astype(jnp.bfloat16), input_gradient_rows.astype(jnp.bfloat16), attn_gain_grad, query_weight_grad, key_weight_grad, value_weight_grad, beta_weight_grad, query_conv_grad, key_conv_grad, value_conv_grad, out_gain_grad, out_weight_grad, mlp_gain_grad, gate_weight_grad, up_weight_grad, down_weight_grad)
```

```python
import functools
import math

import jax
import jax.numpy as jnp
from jax import lax
from jax.experimental import pallas as pl
from jax.experimental.pallas import tpu as pltpu
from jax.sharding import PartitionSpec as P

HEADS = 8
HEAD = 128
SPAN = 128
NORM_EPS = 1e-05
UNIT_EPS = 1e-06
MESH = pl.DeviceIdType.MESH
F32, BF16 = jnp.float32, jnp.bfloat16
VMEM_LIMIT = 61440 * 1024
FFW = 256
Z, Y, X, C = 0, 1, 2, 3

ROW_CONV, ROW_ATTN, ROW_MLP, ROW_OUT, ROW_BETA, SMALL_ROWS = 0, 12, 13, 14, 16, 32


def grid_of(n):
    chips = n // 2
    a = 4 if chips % 4 == 0 else 1
    rest = chips // a
    b = 1
    while b * b < rest:
        b *= 2
    return (a, b, rest // b, 2)


def coords_of(dims, index):
    out = []
    for size in reversed(dims):
        out.append(lax.rem(index, size))
        index = index // size
    return out[::-1]


def index_of(dims, cs):
    total = 0
    for size, c in zip(dims, cs):
        total = total * size + c
    return total


def along(dims, cs, axis, delta):
    moved = list(cs)
    moved[axis] = lax.rem(cs[axis] + delta + dims[axis], dims[axis])
    return moved


def greet_all(n, me):
    barrier = pltpu.get_barrier_semaphore()

    def hello(d, carry):
        pl.semaphore_signal(
            barrier, inc=1, device_id=(lax.rem(me + d, n),), device_id_type=MESH
        )
        return carry

    lax.fori_loop(1, n, hello, 0)
    pl.semaphore_wait(barrier, n - 1)


def greet_axes(dims, cs):
    barrier = pltpu.get_barrier_semaphore()
    count = 0
    for axis in range(4):
        for delta in range(1, dims[axis]):
            to = index_of(dims, along(dims, cs, axis, delta))
            pl.semaphore_signal(barrier, inc=1, device_id=(to,), device_id_type=MESH)
            count += 1
    pl.semaphore_wait(barrier, count)


def hops(dims):
    return sum(d - 1 for d in dims)


class Gather:
    def __init__(self, dims, cs, shard, out, low, width, order, sems):
        self.dims, self.cs, self.order = dims, cs, order
        self.columns = pl.ds(low, width)
        self.shard, self.out = shard.at[:, self.columns], out
        self.send, self.recv, self.local = sems

    def slot(self, stage, delta):
        return sum(self.dims[a] - 1 for a in self.order[:stage]) + delta - 1

    def region(self, stage, cs):
        done = self.order[:stage]
        lead = tuple(slice(None) if k in done else cs[k] for k in range(4))
        return self.out.at[lead + (slice(None), self.columns)]

    def copies(self, stage, incoming):
        axis = self.order[stage]
        for delta in range(1, self.dims[axis]):
            frm = along(self.dims, self.cs, axis, -delta) if incoming else self.cs
            to = along(self.dims, self.cs, axis, delta)
            k = self.slot(stage, delta)
            yield pltpu.make_async_remote_copy(
                src_ref=self.shard if stage == 0 else self.region(stage, self.cs),
                dst_ref=self.region(stage, frm),
                send_sem=self.send.at[k],
                recv_sem=self.recv.at[k],
                device_id=(index_of(self.dims, to),),
                device_id_type=MESH,
            )

    def keep(self):
        return pltpu.make_async_copy(self.shard, self.region(0, self.cs), self.local)

    def step(self, stage):
        if stage == 0:
            self.keep().start()
        if stage == 1:
            self.keep().wait()
        if stage >= 1:
            for c in self.copies(stage - 1, True):
                c.wait_recv()
        if stage < 4:
            for c in self.copies(stage, False):
                c.start()

    def finish(self):
        for stage in range(4):
            for c in self.copies(stage, False):
                c.wait_send()


ZXY, ZYX, XYZ, YXZ = (Z, X, Y, C), (Z, Y, X, C), (X, Y, Z, C), (Y, X, Z, C)


def pipelined(jobs, stages, lag):
    for tick in range(len(jobs) + (stages - 1) * lag):
        for stage in range(stages):
            i = tick - stage * lag
            if 0 <= i < len(jobs):
                jobs[i].step(stage)


class Tokens:
    def __init__(self, n, me, a, b, send, recv, local):
        self.n, self.me, self.a, self.b = n, me, a, b
        self.send, self.recv, self.local = send, recv, local

    def copy(self, d, incoming):
        to = lax.rem(self.me + d, self.n)
        frm = lax.rem(self.me - d + self.n, self.n)
        return pltpu.make_async_remote_copy(
            src_ref=self.a.at[to],
            dst_ref=self.b.at[frm if incoming else self.me],
            send_sem=self.send.at[d],
            recv_sem=self.recv.at[d],
            device_id=(to,),
            device_id_type=MESH,
        )

    def keep(self):
        return pltpu.make_async_copy(self.a.at[self.me], self.b.at[self.me], self.local)

    def each(self, act):
        def body(d, carry):
            act(d)
            return carry

        lax.fori_loop(1, self.n, body, 0)

    def start(self):
        self.keep().start()
        self.each(lambda d: self.copy(d, False).start())

    def wait(self):
        self.keep().wait()
        self.each(lambda d: self.copy(d, True).wait_recv())
        self.each(lambda d: self.copy(d, False).wait_send())


def gather_kernel(dims, plan, lag, count, with_tokens, *refs):
    n = math.prod(dims)
    t = 1 if with_tokens else 0
    ins, outs, scr = refs[: count + t], refs[count + t : 2 * (count + t)], refs[2 * (count + t) :]
    send, recv, local = scr[:3]
    me = lax.axis_index("fsdp")
    cs = coords_of(dims, me)
    if with_tokens:
        greet_all(n, me)
        tokens = Tokens(n, me, ins[count], outs[count], *scr[3:])
        tokens.start()
    else:
        greet_axes(dims, cs)
    jobs = [
        Gather(dims, cs, ins[a], outs[a], low, width, order, (send.at[i], recv.at[i], local.at[i]))
        for i, (a, low, width, order) in enumerate(plan)
    ]
    pipelined(jobs, 5, lag)
    for j in jobs:
        j.finish()
    if with_tokens:
        tokens.wait()


def any_spec():
    return pl.BlockSpec(memory_space=pl.ANY)


def vmem_spec():
    return pl.BlockSpec(memory_space=pltpu.VMEM)


def token_sems(n):
    return [
        pltpu.SemaphoreType.DMA((n,)),
        pltpu.SemaphoreType.DMA((n,)),
        pltpu.SemaphoreType.DMA,
    ]


def gather_call(shards, tokens, plan, lag, collective_id):
    n = lax.axis_size("fsdp")
    dims = grid_of(n)
    k = hops(dims)
    ins = list(shards) + ([] if tokens is None else [tokens])
    outs = [jax.ShapeDtypeStruct(dims + s.shape, s.dtype) for s in shards]
    if tokens is not None:
        outs.append(jax.ShapeDtypeStruct(tokens.shape, tokens.dtype))
    m = len(plan)
    return pl.pallas_call(
        functools.partial(gather_kernel, dims, plan, lag, len(shards), tokens is not None),
        out_shape=outs,
        in_specs=[any_spec()] * len(ins),
        out_specs=[any_spec()] * len(outs),
        scratch_shapes=[
            pltpu.SemaphoreType.DMA((m, k)),
            pltpu.SemaphoreType.DMA((m, k)),
            pltpu.SemaphoreType.DMA((m,)),
        ]
        + ([] if tokens is None else token_sems(n)),
        compiler_params=pltpu.CompilerParams(
            collective_id=collective_id, has_side_effects=True, vmem_limit_bytes=VMEM_LIMIT
        ),
    )(*ins)


class Scatter:
    def __init__(self, dims, cs, terms, result, low, width, order, scratch, sems):
        self.dims, self.cs, self.order = dims, cs, order
        self.columns = pl.ds(low, width)
        self.terms, self.result = terms, result
        self.own, self.got = scratch[0], scratch[1:]
        self.send, self.recv, self.local = sems

    def slot(self, stage, delta):
        return sum(self.dims[a] - 1 for a in self.order[:stage]) + delta - 1

    def part(self, stage, at):
        axis = self.order[stage]
        if stage == 0:
            lead = tuple(at if k == axis else slice(None) for k in range(4))
            return self.terms.at[lead + (slice(None), self.columns)]
        left = [k for k in range(4) if k not in self.order[:stage]]
        return self.got[stage - 1].at[(0,) + tuple(at if k == axis else slice(None) for k in left)]

    def copies(self, stage):
        axis = self.order[stage]
        for delta in range(1, self.dims[axis]):
            to = along(self.dims, self.cs, axis, delta)
            k = self.slot(stage, delta)
            yield pltpu.make_async_remote_copy(
                src_ref=self.part(stage, to[axis]),
                dst_ref=self.got[stage].at[delta - 1],
                send_sem=self.send.at[k],
                recv_sem=self.recv.at[k],
                device_id=(index_of(self.dims, to),),
                device_id_type=MESH,
            )

    def keep(self):
        return pltpu.make_async_copy(self.part(0, self.cs[self.order[0]]), self.own, self.local)

    def total(self, stage):
        axis = self.order[stage]
        left = [k for k in range(4) if k not in self.order[: stage + 1]]
        shape = [self.dims[k] for k in left]
        got = self.got[stage]
        mine = self.own if stage == 0 else self.part(stage, self.cs[axis])

        def one(i, carry):
            at = tuple(coords_of(shape, i)) if shape else ()
            total = mine[at + (slice(None), slice(None))].astype(F32)
            for delta in range(1, self.dims[axis]):
                total += got[(delta - 1,) + at + (slice(None), slice(None))].astype(F32)
            if left:
                got[(0,) + at + (slice(None), slice(None))] = total.astype(got.dtype)
            else:
                self.result[:, self.columns] = total
            return carry

        lax.fori_loop(0, math.prod(shape), one, 0)

    def step(self, stage):
        if stage == 0:
            self.keep().start()
        if stage == 1:
            self.keep().wait()
        if stage >= 1:
            for c in self.copies(stage - 1):
                c.wait_recv()
            self.total(stage - 1)
        if stage < 4:
            for c in self.copies(stage):
                c.start()

    def finish(self):
        for stage in range(4):
            for c in self.copies(stage):
                c.wait_send()


CXYZ, CYXZ = (C, X, Y, Z), (C, Y, X, Z)


def scatter_scratch(dims, rows, width, order, dtype):
    left = list(dims)
    out = [pltpu.VMEM(tuple(d for k, d in enumerate(dims) if k != order[0]) + (rows, width), dtype)]
    for s, axis in enumerate(order):
        rest = tuple(dims[k] for k in range(4) if k not in order[: s + 1])
        out.append(pltpu.VMEM((dims[axis] - 1,) + rest + (rows, width), dtype))
    return out


def scatter_kernel(dims, plan, lag, count, with_tokens, *refs):
    n = math.prod(dims)
    t = 1 if with_tokens else 0
    ins, outs, scr = refs[: count + t], refs[count + t : 2 * (count + t)], refs[2 * (count + t) :]
    send, recv, local = scr[:3]
    scr = scr[3:]
    me = lax.axis_index("fsdp")
    cs = coords_of(dims, me)
    if with_tokens:
        greet_all(n, me)
        tokens = Tokens(n, me, ins[count], outs[count], *scr[:3])
        tokens.start()
        scr = scr[3:]
    else:
        greet_axes(dims, cs)
    jobs = [
        Scatter(
            dims, cs, ins[a], outs[a], low, width, order, scr[5 * i : 5 * i + 5],
            (send.at[i], recv.at[i], local.at[i]),
        )
        for i, (a, low, width, order) in enumerate(plan)
    ]
    pipelined(jobs, 5, lag)
    for j in jobs:
        j.finish()
    if with_tokens:
        tokens.wait()


def scatter_call(terms, tokens, plan, lag, collective_id):
    n = lax.axis_size("fsdp")
    dims = grid_of(n)
    k = hops(dims)
    ins = list(terms) + ([] if tokens is None else [tokens])
    outs = [jax.ShapeDtypeStruct(s.shape[4:], F32) for s in terms]
    out_specs = [vmem_spec()] * len(terms)
    if tokens is not None:
        outs.append(jax.ShapeDtypeStruct(tokens.shape, tokens.dtype))
        out_specs.append(any_spec())
    m = len(plan)
    scratch = []
    for a, low, width, order in plan:
        scratch += scatter_scratch(dims, terms[a].shape[4], width, order, terms[a].dtype)
    return pl.pallas_call(
        functools.partial(scatter_kernel, dims, plan, lag, len(terms), tokens is not None),
        out_shape=outs,
        in_specs=[any_spec()] * len(ins),
        out_specs=out_specs,
        scratch_shapes=[
            pltpu.SemaphoreType.DMA((m, k)),
            pltpu.SemaphoreType.DMA((m, k)),
            pltpu.SemaphoreType.DMA((m,)),
        ]
        + ([] if tokens is None else token_sems(n))
        + scratch,
        compiler_params=pltpu.CompilerParams(
            collective_id=collective_id, has_side_effects=True, vmem_limit_bytes=VMEM_LIMIT
        ),
    )(*ins)


def dot(a, b):
    return lax.dot_general(a, b, (((1,), (0,)), ((), ())), preferred_element_type=F32)


def dot_nt(a, b):
    return lax.dot_general(a, b, (((1,), (1,)), ((), ())), preferred_element_type=F32)


def dot_tn(a, b):
    return lax.dot_general(a, b, (((0,), (0,)), ((), ())), preferred_element_type=F32)


def low(v):
    return v.astype(BF16)


def lanes(i, width=HEAD):
    return slice(i * width, (i + 1) * width)


def shifted(values, by, row):
    if by == 0:
        return values
    rows = values.shape[0]
    moved = pltpu.roll(values, by % rows, 0)
    return jnp.where(row >= by if by > 0 else row < rows + by, moved, 0.0)


def conv(values, taps, row):
    total = values * taps[0:1]
    for c in range(1, taps.shape[0]):
        total += shifted(values, c, row) * taps[c : c + 1]
    return total


def head_sum(values):
    return jnp.sum(values, axis=-1, keepdims=True)


def iotas(shape):
    return lax.broadcasted_iota(jnp.int32, shape, 0), lax.broadcasted_iota(jnp.int32, shape, 1)


def level_masks():
    i, j = iotas((SPAN, SPAN))
    found = []
    for level in range(SPAN.bit_length() - 1):
        a, b = i >> level, j >> level
        found.append(((a >> 1) == (b >> 1)) & ((a & 1) == 1) & ((b & 1) == 0))
    return found


def project(own, small, weights, attn_low, pre, queries, keys, values, beta, micro, length):
    width = own.shape[1]
    row = lax.broadcasted_iota(jnp.int32, (length, 2 * HEAD), 0)
    gain = small[ROW_ATTN : ROW_ATTN + 1, :]
    beta_rows = low(small[ROW_BETA : ROW_BETA + 16, :])

    def one(m, carry):
        rows = pl.ds(m * length, length)
        v = own[rows, :].astype(F32)
        r = lax.rsqrt(jnp.mean(v * v, axis=-1, keepdims=True) + NORM_EPS)
        attn_low[rows, :] = low(v * r * gain)
        a = attn_low[rows, :]
        beta[rows, :] = jax.nn.sigmoid(dot_nt(a, beta_rows))
        for kind, out in enumerate((queries, keys, values)):
            for b in range(width // (2 * HEAD)):
                cols = lanes(b, 2 * HEAD)
                wide = slice(kind * width + cols.start, kind * width + cols.stop)
                x = dot(a, weights[:, wide])
                pre[rows, wide] = low(x)
                c = conv(x, small[4 * kind : 4 * kind + 4, cols], row)
                u = c * jax.nn.sigmoid(c)
                if kind == 2:
                    out[rows, cols] = low(u)
                    continue
                for h in range(2):
                    part = u[:, lanes(h)]
                    n = lax.rsqrt(head_sum(part * part) + UNIT_EPS)
                    out[rows, slice(cols.start + h * HEAD, cols.start + (h + 1) * HEAD)] = low(part * n)
        return carry

    lax.fori_loop(0, micro, one, 0)


def delta_block(base, first, refs, gain):
    queries, keys, values, beta, state, states, inverses, scores, fresh, mix, mixed, at = refs
    rows = pl.ds(base, SPAN)
    i, j = iotas((SPAN, SPAN))
    masks = level_masks()
    eye = jnp.where(i == j, 1.0, 0.0).astype(F32)
    heads = range(HEADS)

    @pl.when(first)
    def _():
        state[...] = jnp.zeros_like(state)

    strength = beta[rows, :]
    k = [keys[rows, lanes(h)] for h in heads]
    q = [queries[rows, lanes(h)] for h in heads]
    b = [strength[:, h : h + 1] for h in heads]
    strict = [low(jnp.where(i > j, dot_nt(k[h], k[h]) * b[h], 0.0)) for h in heads]
    for h in heads:
        scores[at, h] = low(jnp.where(i >= j, dot_nt(q[h], k[h]), 0.0))
    zero = jnp.zeros((), BF16)
    inv = [eye - jnp.where(masks[0], strict[h], zero).astype(F32) for h in heads]
    for level in range(1, len(masks)):
        t = [low(inv[h]) for h in heads]
        f = [low(dot(jnp.where(masks[level], strict[h], zero), t[h])) for h in heads]
        inv = [inv[h] - dot(t[h], f[h]) for h in heads]
    for h in heads:
        inverses[at, h] = low(inv[h])
    s = [low(state[h]) for h in heads]
    for h in heads:
        states[at, h] = s[h]
    rest = [low((values[rows, lanes(h)].astype(F32) - dot(k[h], s[h])) * b[h]) for h in heads]
    new = [low(dot(inverses[at, h], rest[h])) for h in heads]
    out = [dot(q[h], s[h]) + dot(scores[at, h], new[h]) for h in heads]
    for h in heads:
        fresh[rows, lanes(h)] = new[h]
        state[h] += dot_tn(k[h], new[h])
        r = lax.rsqrt(jnp.mean(out[h] * out[h], axis=-1, keepdims=True) + NORM_EPS)
        mix[rows, lanes(h)] = low(out[h])
        mixed[rows, lanes(h)] = low(out[h] * r * gain)


def forward_kernel(micro, length, *refs):
    (own, small, weights, out_weight, hidden, attn_low, pre, queries, keys, values, beta,
     states, inverses, scores, fresh, mix, mixed, state) = refs
    project(own, small, weights, attn_low, pre, queries, keys, values, beta, micro, length)
    gain = small[ROW_OUT : ROW_OUT + 1, :HEAD]
    blocks = length // SPAN

    def one(t, carry):
        delta_block(
            pl.multiple_of(t * SPAN, SPAN), lax.rem(t, blocks) == 0,
            (queries, keys, values, beta, state, states, inverses, scores, fresh, mix, mixed, t), gain,
        )
        rows = pl.ds(pl.multiple_of(t * SPAN, SPAN), SPAN)
        hidden[rows, :] = own[rows, :].astype(F32) + dot_nt(mixed[rows, :], out_weight[...])
        return carry

    lax.fori_loop(0, micro * blocks, one, 0)


def forward_call(own, small, weights, out_weight, micro):
    rows, width = own.shape
    length = rows // micro
    blocks = rows // SPAN
    square = jax.ShapeDtypeStruct((blocks, HEADS, SPAN, SPAN), BF16)
    wide = jax.ShapeDtypeStruct((rows, width), BF16)
    outs = [
        jax.ShapeDtypeStruct((rows, width), F32), wide, jax.ShapeDtypeStruct((rows, 3 * width), BF16),
        wide, wide, wide, jax.ShapeDtypeStruct((rows, 16), F32),
        jax.ShapeDtypeStruct((blocks, HEADS, HEAD, HEAD), BF16), square, square, wide, wide, wide,
    ]
    return pl.pallas_call(
        functools.partial(forward_kernel, micro, length),
        out_shape=outs,
        in_specs=[vmem_spec()] * 4,
        out_specs=[vmem_spec()] * len(outs),
        scratch_shapes=[pltpu.VMEM((HEADS, HEAD, HEAD), F32)],
        compiler_params=pltpu.CompilerParams(vmem_limit_bytes=VMEM_LIMIT),
    )(own, small, weights, out_weight)


def feed_kernel(steps, hidden, grad, small, active, w_ref, result, terms, d_hidden, gain_grad, norm, total, d_norm):
    t = pl.program_id(0)
    gain = small[ROW_MLP : ROW_MLP + 1, :]

    @pl.when(t == 0)
    def _():
        v = hidden[...]
        r = lax.rsqrt(jnp.mean(v * v, axis=-1, keepdims=True) + NORM_EPS)
        norm[...] = low(v * r * gain)
        total[...] = v
        d_norm[...] = jnp.zeros_like(d_norm)

    x, g = norm[...], grad[...]
    gw, uw, dw = (w_ref[:, lanes(i, FFW)] for i in range(3))
    gate, up = dot(x, gw), dot(x, uw)
    d_act = dot(g, dw)
    s = jax.nn.sigmoid(gate)
    silu = gate * s
    act = low(silu * up)
    d_gate = low(d_act * up * (s + silu * (1.0 - s)))
    d_up = low(d_act * silu)
    total[...] += dot_nt(act, dw)
    d_norm[...] += dot_nt(d_gate, gw) + dot_nt(d_up, uw)
    terms[:, lanes(0, FFW)] = low(dot_tn(x, d_gate))
    terms[:, lanes(1, FFW)] = low(dot_tn(x, d_up))
    terms[:, lanes(2, FFW)] = low(dot_tn(g, act))

    @pl.when(t == steps - 1)
    def _():
        result[...] = low(jnp.where(active[...] > 0.0, total[...], 0.0))
        v, d = hidden[...], d_norm[...]
        n = v.shape[1]
        r = lax.rsqrt(jnp.mean(v * v, axis=-1, keepdims=True) + NORM_EPS)
        vr = v * r
        gain_grad[...] = jnp.sum(d * vr, axis=0, keepdims=True)
        gd = d * gain
        d_hidden[...] = g.astype(F32) + r * (gd - vr * (jnp.sum(vr * gd, axis=-1, keepdims=True) / n))


def feed_call(hidden, grad, small, active, weights):
    rows, width = hidden.shape
    steps = weights.shape[1] // (3 * FFW)
    whole = lambda *shape: pl.BlockSpec(shape, lambda t: (0,) * len(shape))
    block = pl.BlockSpec((width, 3 * FFW), lambda t: (0, t))
    return pl.pallas_call(
        functools.partial(feed_kernel, steps),
        grid=(steps,),
        out_shape=[
            jax.ShapeDtypeStruct((rows, width), BF16),
            jax.ShapeDtypeStruct(weights.shape, BF16),
            jax.ShapeDtypeStruct((rows, width), F32),
            jax.ShapeDtypeStruct((1, width), F32),
        ],
        in_specs=[whole(rows, width), whole(rows, width), whole(*small.shape), whole(rows, 1), block],
        out_specs=[whole(rows, width), block, whole(rows, width), whole(1, width)],
        scratch_shapes=[
            pltpu.VMEM((rows, width), BF16),
            pltpu.VMEM((rows, width), F32),
            pltpu.VMEM((rows, width), F32),
        ],
        compiler_params=pltpu.CompilerParams(
            vmem_limit_bytes=VMEM_LIMIT, dimension_semantics=("arbitrary",)
        ),
    )(hidden, grad, small, active, weights)


def delta_back(base, last, refs, gain):
    (queries, keys, values, beta, states, inverses, scores, fresh, mix, d_mixed,
     d_state, d_out, d_q, d_k, d_v, d_beta, gain_grad, at) = refs
    rows = pl.ds(base, SPAN)
    i, j = iotas((SPAN, SPAN))
    lane = lax.broadcasted_iota(jnp.int32, (SPAN, 16), 1)
    heads = range(HEADS)

    @pl.when(last)
    def _():
        d_state[...] = jnp.zeros_like(d_state)

    strength = beta[rows, :]
    k = [keys[rows, lanes(h)] for h in heads]
    q = [queries[rows, lanes(h)] for h in heads]
    e = [fresh[rows, lanes(h)] for h in heads]
    b = [strength[:, h : h + 1] for h in heads]
    kb = [low(k[h].astype(F32) * b[h]) for h in heads]
    do = []
    for h in heads:
        v, d = mix[rows, lanes(h)].astype(F32), d_mixed[:, lanes(h)]
        r = lax.rsqrt(jnp.mean(v * v, axis=-1, keepdims=True) + NORM_EPS)
        vr, gd = v * r, d * gain
        gain_grad[...] += jnp.sum(d * vr, axis=0, keepdims=True)
        do.append(low(r * (gd - vr * jnp.mean(vr * gd, axis=-1, keepdims=True))))
    s = [states[at, h] for h in heads]
    p = [scores[at, h] for h in heads]
    ds = [low(d_state[h]) for h in heads]
    de = [low(dot_tn(p[h], do[h]) + dot(k[h], ds[h])) for h in heads]
    dx = [dot_tn(inverses[at, h], de[h]) for h in heads]
    dxl = [low(dx[h]) for h in heads]
    dp = [low(jnp.where(i >= j, dot_nt(do[h], e[h]), 0.0)) for h in heads]
    da = [low(jnp.where(i > j, -dot_nt(dxl[h], e[h]), 0.0)) for h in heads]
    dkb = [dot(da[h], k[h]) - dot_nt(dxl[h], s[h]) for h in heads]
    beta_grad = jnp.zeros((SPAN, 16), F32)
    for h in heads:
        d_q[rows, lanes(h)] = low(dot_nt(do[h], s[h]) + dot(dp[h], k[h]))
        d_k[rows, lanes(h)] = low(
            dkb[h] * b[h] + dot_tn(da[h], kb[h]) + dot_tn(dp[h], q[h]) + dot_nt(e[h], ds[h])
        )
        d_v[rows, lanes(h)] = low(dx[h] * b[h])
        d_state[h] += dot_tn(q[h], do[h]) - dot_tn(kb[h], dxl[h])
        db = head_sum(dkb[h] * k[h].astype(F32) + dx[h] * values[rows, lanes(h)].astype(F32))
        beta_grad += jnp.where(lane == h, db, 0.0)
    d_beta[rows, :] = low(beta_grad * strength * (1.0 - strength))


def backward_kernel(micro, length, *refs):
    (d_hidden, own, small, weights, out_weight, attn_low, pre, queries, keys, values, beta,
     states, inverses, scores, fresh, mix, mixed,
     d_own, qkv_grad, out_grad, small_grad,
     d_state, d_out, d_q, d_k, d_v, d_beta, d_pre, d_attn, gain_grad) = refs
    width = own.shape[1]
    blocks = length // SPAN
    total = micro * blocks
    gain = small[ROW_OUT : ROW_OUT + 1, :HEAD]
    gain_grad[...] = jnp.zeros_like(gain_grad)
    small_grad[...] = jnp.zeros_like(small_grad)
    d_attn[...] = low(d_hidden[...])

    def one(step, carry):
        t = total - 1 - step
        base = pl.multiple_of(t * SPAN, SPAN)
        d_out[...] = dot(d_attn[pl.ds(base, SPAN), :], out_weight[...])
        delta_back(
            base, lax.rem(step, blocks) == 0,
            (queries, keys, values, beta, states, inverses, scores, fresh, mix, d_out,
             d_state, None, d_q, d_k, d_v, d_beta, gain_grad, t), gain,
        )
        return carry

    lax.fori_loop(0, total, one, 0)
    row = lax.broadcasted_iota(jnp.int32, (length, HEAD), 0)

    def conv_back(m, carry):
        rows = pl.ds(m * length, length)
        for kind, grads in enumerate((d_q, d_k, d_v)):
            for h in range(width // HEAD):
                cols = lanes(h)
                wide = slice(kind * width + cols.start, kind * width + cols.stop)
                taps = small[4 * kind : 4 * kind + 4, cols]
                x = pre[rows, wide].astype(F32)
                moved = [shifted(x, c, row) for c in range(4)]
                c = moved[0] * taps[0:1]
                for o in range(1, 4):
                    c += moved[o] * taps[o : o + 1]
                s = jax.nn.sigmoid(c)
                u = c * s
                d = grads[rows, cols].astype(F32)
                if kind < 2:
                    n = lax.rsqrt(head_sum(u * u) + UNIT_EPS)
                    un = u * n
                    d = (d - un * head_sum(un * d)) * n
                d = d * (s + u * (1.0 - s))
                for o in range(4):
                    at = slice(4 * kind + o, 4 * kind + o + 1)
                    small_grad[at, cols] += jnp.sum(moved[o] * d, axis=0, keepdims=True)
                back = d * taps[0:1]
                for o in range(1, 4):
                    back += shifted(d, -o, row) * taps[o : o + 1]
                d_pre[rows, wide] = low(back)
        return carry

    lax.fori_loop(0, micro, conv_back, 0)
    for b in range(width // 256):
        cols = lanes(b, 256)
        out_grad[:, cols] = low(dot_tn(d_attn[...], mixed[:, cols]))
    for b in range(3 * width // 256):
        cols = lanes(b, 256)
        qkv_grad[:, cols] = low(dot_tn(attn_low[...], d_pre[:, cols]))
    beta_rows = low(small[ROW_BETA : ROW_BETA + 16, :])
    small_grad[ROW_BETA : ROW_BETA + 16, :] = dot_tn(d_beta[...], attn_low[...])
    small_grad[ROW_OUT : ROW_OUT + 1, :HEAD] = gain_grad[...]
    attn_gain = small[ROW_ATTN : ROW_ATTN + 1, :]

    def finish(t, carry):
        rows = pl.ds(pl.multiple_of(t * SPAN, SPAN), SPAN)
        d = dot_nt(d_pre[rows, :], weights[...]) + dot(d_beta[rows, :], beta_rows)
        v = own[rows, :].astype(F32)
        r = lax.rsqrt(jnp.mean(v * v, axis=-1, keepdims=True) + NORM_EPS)
        vr, gd = v * r, d * attn_gain
        small_grad[ROW_ATTN : ROW_ATTN + 1, :] += jnp.sum(d * vr, axis=0, keepdims=True)
        d_own[rows, :] = low(d_hidden[rows, :] + r * (gd - vr * jnp.mean(vr * gd, axis=-1, keepdims=True)))
        return carry

    lax.fori_loop(0, total, finish, 0)


def backward_call(d_hidden, own, small, weights, out_weight, saved, micro):
    rows, width = own.shape
    length = rows // micro
    return pl.pallas_call(
        functools.partial(backward_kernel, micro, length),
        out_shape=[
            jax.ShapeDtypeStruct((rows, width), BF16),
            jax.ShapeDtypeStruct((width, 3 * width), BF16),
            jax.ShapeDtypeStruct((width, width), BF16),
            jax.ShapeDtypeStruct((SMALL_ROWS, width), F32),
        ],
        in_specs=[vmem_spec()] * (5 + len(saved)),
        out_specs=[vmem_spec()] * 4,
        scratch_shapes=[
            pltpu.VMEM((HEADS, HEAD, HEAD), F32),
            pltpu.VMEM((SPAN, width), F32),
            pltpu.VMEM((rows, width), BF16),
            pltpu.VMEM((rows, width), BF16),
            pltpu.VMEM((rows, width), BF16),
            pltpu.VMEM((rows, 16), BF16),
            pltpu.VMEM((rows, 3 * width), BF16),
            pltpu.VMEM((rows, width), BF16),
            pltpu.VMEM((1, HEAD), F32),
        ],
        compiler_params=pltpu.CompilerParams(vmem_limit_bytes=VMEM_LIMIT),
    )(d_hidden, own, small, weights, out_weight, *saved)


def picked(index, source):
    hot = index[:, None] == jnp.arange(source.shape[0], dtype=jnp.int32)[None, :]
    return jnp.dot(low(hot), source, preferred_element_type=F32).astype(BF16)


def split_rows(values, parts):
    cut = values.reshape(values.shape[:-1] + (parts, values.shape[-1] // parts))
    return jnp.moveaxis(cut, -2, 0)


def spans(width, size):
    at = 0
    while at < width:
        yield at, min(size, width - at)
        at += size


def local(
    inputs, cotangent, lengths, owners, attn_gain, query_weight, key_weight, value_weight, beta_weight,
    query_conv, key_conv, value_conv, out_gain, out_weight, mlp_gain, gate_weight, up_weight, down_weight,
):
    n = lax.axis_size("fsdp")
    dims = grid_of(n)
    me = lax.axis_index("fsdp")
    micro, _, length, width = inputs.shape
    hidden_units = gate_weight.shape[1]
    share = width // n
    slots = length // n
    per = micro * slots
    parts = 16 // math.gcd(per, 16)
    thin = width // parts
    i32 = jnp.int32
    devices = jnp.arange(n, dtype=i32)
    slot_ids = jnp.arange(slots, dtype=i32)
    row_ids = jnp.arange(length, dtype=i32)
    micros = jnp.arange(micro, dtype=i32)
    part_ids = jnp.arange(parts, dtype=i32)

    before = devices[:, None] < devices[None, :]
    starts = jnp.sum(jnp.where(before[None], lengths[:, :, None], 0), axis=1)
    match = owners[:, None, :] == devices[None, :, None]
    own_start = jnp.sum(jnp.where(match, starts[:, None, :], 0), axis=2)
    own_len = jnp.sum(jnp.where(match, lengths[:, None, :], 0), axis=2)
    mine = devices == me
    my_start = jnp.sum(jnp.where(mine, own_start, 0), axis=1)
    my_len = jnp.sum(jnp.where(mine, own_len, 0), axis=1)

    first = own_start + (me - own_start) % n
    pos = first[:, :, None] + n * slot_ids
    live = pos < (own_start + own_len)[:, :, None]
    send = jnp.where(live, micros[:, None, None] * length + pos // n, -1)
    send = jnp.moveaxis(send, 0, 1)[:, None] + jnp.zeros((1, parts, 1, 1), i32)
    send = jnp.where(send >= 0, send + (part_ids * micro * length)[None, :, None, None], -1)
    rows_in = split_rows(inputs[:, 0].reshape(micro * length, width), parts).reshape(-1, thin)
    outgoing = picked(send.reshape(-1), rows_in).reshape(n, parts * per, thin)

    def row_of(v):
        return jnp.pad(v, ((0, 0), (0, share - v.shape[1])))

    packed = jnp.concatenate([
        query_conv, key_conv, value_conv, attn_gain[None], mlp_gain[None], row_of(out_gain[None]),
        jnp.zeros((1, share), BF16), beta_weight.T, jnp.zeros((SMALL_ROWS - 16 - HEADS, share), BF16),
    ])
    count = SMALL_ROWS * share // HEAD
    packed = jnp.pad(packed.reshape(count, HEAD), ((0, -count % 16), (0, 0)))

    attn_shard = jnp.concatenate([query_weight, key_weight, value_weight, out_weight.T], axis=1)
    steps = hidden_units // FFW
    feed_shard = jnp.stack(
        [w.reshape(share, steps, FFW) for w in (gate_weight, up_weight, down_weight.T)], axis=2
    ).reshape(share, 3 * hidden_units)

    plan = [(0, 0, HEAD, ZXY)]
    for a, (w, size) in enumerate(((4 * width, 512), (3 * hidden_units, 768)), 1):
        for at, wide in spans(w, size):
            plan.append((a, at, wide, (ZXY, ZYX)[len(plan) % 2]))
    small_all, attn_all, feed_all, incoming = gather_call(
        [packed, attn_shard, feed_shard], outgoing, tuple(plan), 2, 1
    )
    small = small_all.reshape(n, -1)[:, : SMALL_ROWS * share].reshape(n, SMALL_ROWS, share)
    small = jnp.moveaxis(small, 1, 0)
    gain_row = small[ROW_OUT, :, : HEAD // n].reshape(1, HEAD)
    small = small.reshape(SMALL_ROWS, width).astype(F32)
    small = lax.dynamic_update_slice(small, gain_row.astype(F32), (ROW_OUT, 0))
    attn_all = attn_all.reshape(width, 4 * width)
    feed_all = feed_all.reshape(width, 3 * hidden_units)
    qkv, out_t = attn_all[:, : 3 * width], attn_all[:, 3 * width :]

    active = row_ids[None] < my_len[:, None]
    block = (my_start[:, None] + row_ids) % n
    at = block * (parts * per) + micros[:, None] * slots + row_ids // n
    take = jnp.where(active, at, -1).reshape(-1)
    flat = incoming.reshape(n * parts * per, thin)
    own = jnp.concatenate(
        [picked(jnp.where(take >= 0, take + p * per, -1), flat) for p in range(parts)], axis=1
    )
    active = active.reshape(-1, 1)
    grad = jnp.where(active, cotangent[:, 0].reshape(-1, width), jnp.zeros((), BF16))

    hidden, *saved = forward_call(own, small, qkv, out_t, micro)
    result, feed_terms, d_hidden, mlp_gain_grad = feed_call(
        hidden, grad, small, active.astype(F32), feed_all
    )
    d_own, qkv_terms, out_terms, small_terms = backward_call(
        d_hidden, own, small, qkv, out_t, saved, micro
    )

    back = slot_ids * n + (devices[:, None, None] - my_start[None, :, None]) % n
    back = jnp.where(back < my_len[None, :, None], back + (micros * length)[None, :, None], -1)
    back = back[:, None] + jnp.zeros((1, parts, 1, 1), i32)
    back = jnp.where(back >= 0, back + (part_ids * micro * length)[None, :, None, None], -1)
    returning = picked(back.reshape(-1), split_rows(d_own, parts).reshape(-1, thin))
    returning = returning.reshape(n, parts * per, thin)

    small_terms = lax.dynamic_update_slice(small_terms, mlp_gain_grad, (ROW_MLP, 0))
    out_gain_terms = jnp.pad(small_terms[ROW_OUT, :HEAD].reshape(n, -1), ((0, 0), (0, share - HEAD // n)))
    small_terms = jnp.concatenate(
        [small_terms[:ROW_OUT].reshape(ROW_OUT, n, share), out_gain_terms[None],
         small_terms[ROW_OUT + 1 :].reshape(SMALL_ROWS - ROW_OUT - 1, n, share)]
    )
    small_terms = jnp.moveaxis(small_terms, 1, 0).reshape(n, count, HEAD)
    small_terms = jnp.pad(small_terms, ((0, 0), (0, -count % 16), (0, 0)))
    terms = [
        small_terms.reshape(dims + small_terms.shape[1:]),
        qkv_terms.reshape(dims + (share, 3 * width)),
        out_terms.reshape(dims + (share, width)),
        feed_terms.reshape(dims + (share, 3 * hidden_units)),
    ]
    plan = []
    for a, size in ((3, 768), (2, 512), (1, 512), (0, HEAD)):
        for lo, wide in spans(terms[a].shape[5], size):
            plan.append((a, lo, wide, (CXYZ, CYXZ)[len(plan) % 2]))
    small_grad, qkv_grad, out_grad, feed_grad, returned = scatter_call(
        terms, returning, tuple(plan), 2, 2
    )

    place = row_ids * n + me
    inside = (place[None, :, None] >= own_start[:, None, :]) & (
        place[None, :, None] < (own_start + own_len)[:, None, :]
    )
    at = devices * (parts * per) + micros[:, None, None] * slots + (place[None, :, None] - first[:, None, :]) // n
    take = (jnp.sum(jnp.where(inside, at + 1, 0), axis=2) - 1).reshape(-1)
    flat = returned.reshape(n * parts * per, thin)
    input_rows = jnp.concatenate(
        [picked(jnp.where(take >= 0, take + p * per, -1), flat) for p in range(parts)], axis=1
    )

    small_grad = small_grad.reshape(-1)[: SMALL_ROWS * share].reshape(SMALL_ROWS, share)
    feed_grad = feed_grad.reshape(share, steps, 3, FFW)
    gate_grad, up_grad, down_grad = (
        feed_grad[:, :, i].reshape(share, hidden_units) for i in range(3)
    )
    return (
        result.reshape(micro, 1, length, width),
        input_rows.reshape(micro, 1, length, width),
        small_grad[ROW_ATTN],
        qkv_grad[:, :width],
        qkv_grad[:, width : 2 * width],
        qkv_grad[:, 2 * width :],
        small_grad[ROW_BETA : ROW_BETA + HEADS].T,
        small_grad[0:4],
        small_grad[4:8],
        small_grad[8:12],
        small_grad[ROW_OUT, : HEAD // n],
        out_grad.T,
        small_grad[ROW_MLP],
        gate_grad,
        up_grad,
        down_grad.T,
    )


def solution(mesh):
    rows, cols, flat = P("fsdp", None), P(None, "fsdp"), P("fsdp")
    data = P(None, "fsdp", None, None)
    return jax.shard_map(
        local,
        mesh=mesh,
        in_specs=(
            data, data, P(), P(), flat, rows, rows, rows, rows, cols, cols, cols, flat, cols, flat, rows, rows, cols,
        ),
        out_specs=(
            data, data, flat, rows, rows, rows, rows, cols, cols, cols, flat, cols, flat, rows, rows, cols,
        ),
        check_vma=False,
    )
```

```python
import functools
import math

import jax
import jax.numpy as jnp
from jax import lax
from jax.experimental import pallas as pl
from jax.experimental.pallas import tpu as pltpu
from jax.sharding import PartitionSpec as P

HEADS = 8
HEAD = 128
SPAN = 128
NORM_EPS = 1e-05
UNIT_EPS = 1e-06
MESH = pl.DeviceIdType.MESH
F32, BF16 = jnp.float32, jnp.bfloat16
VMEM_LIMIT = 61440 * 1024
FFW = 256
Z, Y, X, C = 0, 1, 2, 3

ROW_CONV, ROW_ATTN, ROW_MLP, ROW_OUT, ROW_BETA, SMALL_ROWS = 0, 12, 13, 14, 16, 32


def grid_of(n):
    chips = n // 2
    a = 4 if chips % 4 == 0 else 1
    rest = chips // a
    b = 1
    while b * b < rest:
        b *= 2
    return (a, b, rest // b, 2)


def coords_of(dims, index):
    out = []
    for size in reversed(dims):
        out.append(lax.rem(index, size))
        index = index // size
    return out[::-1]


def index_of(dims, cs):
    total = 0
    for size, c in zip(dims, cs):
        total = total * size + c
    return total


def along(dims, cs, axis, delta):
    moved = list(cs)
    moved[axis] = lax.rem(cs[axis] + delta + dims[axis], dims[axis])
    return moved


def greet_all(n, me):
    barrier = pltpu.get_barrier_semaphore()

    def hello(d, carry):
        pl.semaphore_signal(
            barrier, inc=1, device_id=(lax.rem(me + d, n),), device_id_type=MESH
        )
        return carry

    lax.fori_loop(1, n, hello, 0)
    pl.semaphore_wait(barrier, n - 1)


def greet_axes(dims, cs):
    barrier = pltpu.get_barrier_semaphore()
    count = 0
    for axis in range(4):
        for delta in range(1, dims[axis]):
            to = index_of(dims, along(dims, cs, axis, delta))
            pl.semaphore_signal(barrier, inc=1, device_id=(to,), device_id_type=MESH)
            count += 1
    pl.semaphore_wait(barrier, count)


def hops(dims):
    return sum(d - 1 for d in dims)


class Gather:
    def __init__(self, dims, cs, shard, out, low, width, order, sems):
        self.dims, self.cs, self.order = dims, cs, order
        self.columns = pl.ds(low, width)
        self.shard, self.out = shard.at[:, self.columns], out
        self.send, self.recv, self.local = sems

    def slot(self, stage, delta):
        return sum(self.dims[a] - 1 for a in self.order[:stage]) + delta - 1

    def region(self, stage, cs):
        done = self.order[:stage]
        lead = tuple(slice(None) if k in done else cs[k] for k in range(4))
        return self.out.at[lead + (slice(None), self.columns)]

    def copies(self, stage, incoming):
        axis = self.order[stage]
        for delta in range(1, self.dims[axis]):
            frm = along(self.dims, self.cs, axis, -delta) if incoming else self.cs
            to = along(self.dims, self.cs, axis, delta)
            k = self.slot(stage, delta)
            yield pltpu.make_async_remote_copy(
                src_ref=self.shard if stage == 0 else self.region(stage, self.cs),
                dst_ref=self.region(stage, frm),
                send_sem=self.send.at[k],
                recv_sem=self.recv.at[k],
                device_id=(index_of(self.dims, to),),
                device_id_type=MESH,
            )

    def keep(self):
        return pltpu.make_async_copy(self.shard, self.region(0, self.cs), self.local)

    def step(self, stage):
        if stage == 0:
            self.keep().start()
        if stage == 1:
            self.keep().wait()
        if stage >= 1:
            for c in self.copies(stage - 1, True):
                c.wait_recv()
        if stage < 4:
            for c in self.copies(stage, False):
                c.start()

    def finish(self):
        for stage in range(4):
            for c in self.copies(stage, False):
                c.wait_send()


ZXY, ZYX, XYZ, YXZ = (Z, X, Y, C), (Z, Y, X, C), (X, Y, Z, C), (Y, X, Z, C)


def pipelined(jobs, stages, lag):
    for tick in range(len(jobs) + (stages - 1) * lag):
        run_tick(jobs, stages, lag, tick)


def run_tick(jobs, stages, lag, tick):
    for stage in reversed(range(stages)):
        i = tick - stage * lag
        if 0 <= i < len(jobs):
            jobs[i].step(stage)


def loop_tick(make, count, stages, lag, tick):
    for stage in reversed(range(stages)):
        i = tick - stage * lag

        @pl.when((i >= 0) & (i < count))
        def _(i=i, stage=stage):
            for job in make(i):
                job.step(stage)


class Tokens:
    def __init__(self, n, me, a, b, send, recv, local):
        self.n, self.me, self.a, self.b = n, me, a, b
        self.send, self.recv, self.local = send, recv, local

    def copy(self, d, incoming):
        to = lax.rem(self.me + d, self.n)
        frm = lax.rem(self.me - d + self.n, self.n)
        return pltpu.make_async_remote_copy(
            src_ref=self.a.at[to],
            dst_ref=self.b.at[frm if incoming else self.me],
            send_sem=self.send.at[d],
            recv_sem=self.recv.at[d],
            device_id=(to,),
            device_id_type=MESH,
        )

    def keep(self):
        return pltpu.make_async_copy(self.a.at[self.me], self.b.at[self.me], self.local)

    def each(self, act):
        def body(d, carry):
            act(d)
            return carry

        lax.fori_loop(1, self.n, body, 0)

    def start(self):
        self.keep().start()
        self.each(lambda d: self.copy(d, False).start())

    def wait(self):
        self.keep().wait()
        self.each(lambda d: self.copy(d, True).wait_recv())
        self.each(lambda d: self.copy(d, False).wait_send())


def gather_kernel(dims, plan, lag, count, with_tokens, *refs):
    n = math.prod(dims)
    t = 1 if with_tokens else 0
    ins, outs, scr = refs[: count + t], refs[count + t : 2 * (count + t)], refs[2 * (count + t) :]
    send, recv, local = scr[:3]
    me = lax.axis_index("fsdp")
    cs = coords_of(dims, me)
    if with_tokens:
        greet_all(n, me)
        tokens = Tokens(n, me, ins[count], outs[count], *scr[3:])
        tokens.start()
    else:
        greet_axes(dims, cs)
    jobs = [
        Gather(dims, cs, ins[a], outs[a], low, width, order, (send.at[i], recv.at[i], local.at[i]))
        for i, (a, low, width, order) in enumerate(plan)
    ]
    pipelined(jobs, 5, lag)
    for j in jobs:
        j.finish()
    if with_tokens:
        tokens.wait()


def any_spec():
    return pl.BlockSpec(memory_space=pl.ANY)


def vmem_spec():
    return pl.BlockSpec(memory_space=pltpu.VMEM)


def token_sems(n):
    return [
        pltpu.SemaphoreType.DMA((n,)),
        pltpu.SemaphoreType.DMA((n,)),
        pltpu.SemaphoreType.DMA,
    ]


def gather_call(shards, tokens, plan, lag, collective_id):
    n = lax.axis_size("fsdp")
    dims = grid_of(n)
    k = hops(dims)
    ins = list(shards) + ([] if tokens is None else [tokens])
    outs = [jax.ShapeDtypeStruct(dims + s.shape, s.dtype) for s in shards]
    if tokens is not None:
        outs.append(jax.ShapeDtypeStruct(tokens.shape, tokens.dtype))
    m = len(plan)
    return pl.pallas_call(
        functools.partial(gather_kernel, dims, plan, lag, len(shards), tokens is not None),
        out_shape=outs,
        in_specs=[any_spec()] * len(ins),
        out_specs=[any_spec()] * len(outs),
        scratch_shapes=[
            pltpu.SemaphoreType.DMA((m, k)),
            pltpu.SemaphoreType.DMA((m, k)),
            pltpu.SemaphoreType.DMA((m,)),
        ]
        + ([] if tokens is None else token_sems(n)),
        compiler_params=pltpu.CompilerParams(
            collective_id=collective_id, has_side_effects=True, vmem_limit_bytes=VMEM_LIMIT
        ),
    )(*ins)


class Scatter:
    def __init__(self, dims, cs, terms, term_columns, result, columns, order, own, got, sems):
        self.dims, self.cs, self.order = dims, cs, order
        self.term_columns, self.columns = term_columns, columns
        self.terms, self.result = terms, result
        self.own, self.got = own, got
        self.send, self.recv, self.local = sems

    def slot(self, stage, delta):
        return sum(self.dims[a] - 1 for a in self.order[:stage]) + delta - 1

    def part(self, stage, at):
        axis = self.order[stage]
        if stage == 0:
            lead = tuple(at if k == axis else slice(None) for k in range(4))
            return self.terms.at[lead + (slice(None), self.term_columns)]
        left = [k for k in range(4) if k not in self.order[:stage]]
        return self.got[stage - 1].at[(0,) + tuple(at if k == axis else slice(None) for k in left)]

    def copies(self, stage):
        axis = self.order[stage]
        for delta in range(1, self.dims[axis]):
            to = along(self.dims, self.cs, axis, delta)
            k = self.slot(stage, delta)
            yield pltpu.make_async_remote_copy(
                src_ref=self.part(stage, to[axis]),
                dst_ref=self.got[stage].at[delta - 1],
                send_sem=self.send.at[k],
                recv_sem=self.recv.at[k],
                device_id=(index_of(self.dims, to),),
                device_id_type=MESH,
            )

    def keep(self):
        return pltpu.make_async_copy(self.part(0, self.cs[self.order[0]]), self.own, self.local)

    def total(self, stage):
        axis = self.order[stage]
        left = [k for k in range(4) if k not in self.order[: stage + 1]]
        shape = [self.dims[k] for k in left]
        got = self.got[stage]
        whole = stage or self.own is None
        mine = self.part(stage, self.cs[axis]) if whole else self.own

        def one(i, carry):
            at = tuple(coords_of(shape, i)) if shape else ()
            total = mine[at + (slice(None), slice(None))].astype(F32)
            for delta in range(1, self.dims[axis]):
                total += got[(delta - 1,) + at + (slice(None), slice(None))].astype(F32)
            if left:
                got[(0,) + at + (slice(None), slice(None))] = total.astype(got.dtype)
            else:
                self.result[:, self.columns] = total
            return carry

        lax.fori_loop(0, math.prod(shape), one, 0)

    def step(self, stage):
        if self.own is not None:
            if stage == 0:
                self.keep().start()
            if stage == 1:
                self.keep().wait()
        if stage >= 1:
            for c in self.copies(stage - 1):
                c.wait()
            self.total(stage - 1)
        if stage < 4:
            for c in self.copies(stage):
                c.start()


CXYZ, CYXZ = (C, X, Y, Z), (C, Y, X, Z)


def scatter_scratch(dims, rows, width, order, dtype, lead=(), keep=True):
    out = []
    if keep:
        rest = tuple(d for k, d in enumerate(dims) if k != order[0])
        out.append(pltpu.VMEM(lead + rest + (rows, width), dtype))
    for s, axis in enumerate(order):
        rest = tuple(dims[k] for k in range(4) if k not in order[: s + 1])
        out.append(pltpu.VMEM(lead + (dims[axis] - 1,) + rest + (rows, width), dtype))
    return out


def dot(a, b):
    return lax.dot_general(a, b, (((1,), (0,)), ((), ())), preferred_element_type=F32)


def dot_nt(a, b):
    return lax.dot_general(a, b, (((1,), (1,)), ((), ())), preferred_element_type=F32)


def dot_tn(a, b):
    return lax.dot_general(a, b, (((0,), (0,)), ((), ())), preferred_element_type=F32)


def low(v):
    return v.astype(BF16)


def lanes(i, width=HEAD):
    return slice(i * width, (i + 1) * width)


def shifted(values, by, row):
    if by == 0:
        return values
    rows = values.shape[0]
    moved = pltpu.roll(values, by % rows, 0)
    return jnp.where(row >= by if by > 0 else row < rows + by, moved, 0.0)


def conv(values, taps, row):
    total = values * taps[0:1]
    for c in range(1, taps.shape[0]):
        total += shifted(values, c, row) * taps[c : c + 1]
    return total


def head_sum(values):
    return jnp.sum(values, axis=-1, keepdims=True)


def iotas(shape):
    return lax.broadcasted_iota(jnp.int32, shape, 0), lax.broadcasted_iota(jnp.int32, shape, 1)


def level_masks():
    i, j = iotas((SPAN, SPAN))
    found = []
    for level in range(SPAN.bit_length() - 1):
        a, b = i >> level, j >> level
        found.append(((a >> 1) == (b >> 1)) & ((a & 1) == 1) & ((b & 1) == 0))
    return found


def project(own, small, weights, attn_low, pre, queries, keys, values, beta, micro, length, tick):
    width = own.shape[1]
    row = lax.broadcasted_iota(jnp.int32, (length, 2 * HEAD), 0)
    gain = small[ROW_ATTN : ROW_ATTN + 1, :]
    beta_rows = low(small[ROW_BETA : ROW_BETA + 16, :])

    def one(m, carry):
        tick(m + 1)
        rows = pl.ds(m * length, length)
        v = own[rows, :].astype(F32)
        r = lax.rsqrt(jnp.mean(v * v, axis=-1, keepdims=True) + NORM_EPS)
        attn_low[rows, :] = low(v * r * gain)
        a = attn_low[rows, :]
        beta[rows, :] = jax.nn.sigmoid(dot_nt(a, beta_rows))
        for kind, out in enumerate((queries, keys, values)):
            for b in range(width // (2 * HEAD)):
                cols = lanes(b, 2 * HEAD)
                wide = slice(kind * width + cols.start, kind * width + cols.stop)
                x = dot(a, weights[:, wide])
                pre[rows, wide] = low(x)
                c = conv(x, small[4 * kind : 4 * kind + 4, cols], row)
                u = c * jax.nn.sigmoid(c)
                if kind == 2:
                    out[rows, cols] = low(u)
                    continue
                for h in range(2):
                    part = u[:, lanes(h)]
                    n = lax.rsqrt(head_sum(part * part) + UNIT_EPS)
                    out[rows, slice(cols.start + h * HEAD, cols.start + (h + 1) * HEAD)] = low(part * n)
        return carry

    lax.fori_loop(0, micro, one, 0)


def delta_block(base, first, refs, gain):
    queries, keys, values, beta, state, states, inverses, scores, fresh, mix, mixed, at = refs
    rows = pl.ds(base, SPAN)
    i, j = iotas((SPAN, SPAN))
    masks = level_masks()
    eye = jnp.where(i == j, 1.0, 0.0).astype(F32)
    heads = range(HEADS)

    @pl.when(first)
    def _():
        state[...] = jnp.zeros_like(state)

    strength = beta[rows, :]
    k = [keys[rows, lanes(h)] for h in heads]
    q = [queries[rows, lanes(h)] for h in heads]
    b = [strength[:, h : h + 1] for h in heads]
    strict = [low(jnp.where(i > j, dot_nt(k[h], k[h]) * b[h], 0.0)) for h in heads]
    for h in heads:
        scores[at, h] = low(jnp.where(i >= j, dot_nt(q[h], k[h]), 0.0))
    zero = jnp.zeros((), BF16)
    inv = [eye - jnp.where(masks[0], strict[h], zero).astype(F32) for h in heads]
    for level in range(1, len(masks)):
        t = [low(inv[h]) for h in heads]
        f = [low(dot(jnp.where(masks[level], strict[h], zero), t[h])) for h in heads]
        inv = [inv[h] - dot(t[h], f[h]) for h in heads]
    for h in heads:
        inverses[at, h] = low(inv[h])
    s = [low(state[h]) for h in heads]
    for h in heads:
        states[at, h] = s[h]
    rest = [low((values[rows, lanes(h)].astype(F32) - dot(k[h], s[h])) * b[h]) for h in heads]
    new = [low(dot(inverses[at, h], rest[h])) for h in heads]
    out = [dot(q[h], s[h]) + dot(scores[at, h], new[h]) for h in heads]
    for h in heads:
        fresh[rows, lanes(h)] = new[h]
        state[h] += dot_tn(k[h], new[h])
        r = lax.rsqrt(jnp.mean(out[h] * out[h], axis=-1, keepdims=True) + NORM_EPS)
        mix[rows, lanes(h)] = low(out[h])
        mixed[rows, lanes(h)] = low(out[h] * r * gain)


def square_rms(v):
    return lax.rsqrt(jnp.mean(v * v, axis=-1, keepdims=True) + NORM_EPS)


def forward_kernel(dims, micro, length, steps, *refs):
    (own, small, weights, out_weight, grad, active, feed_shard,
     result, d_hidden, d_attn, gain_grad, terms, feed, attn_low, pre, queries, keys, values, beta,
     states, inverses, scores, fresh, mix, mixed,
     state, hidden, norm, total, w_buf, t_buf, send, recv, local, w_sem, t_sem) = refs
    me = lax.axis_index("fsdp")
    cs = coords_of(dims, me)
    greet_axes(dims, cs)
    half = 3 * FFW // 2

    def jobs(i):
        for p, order in enumerate((ZXY, ZYX)):
            at = pl.multiple_of(i * (3 * FFW) + p * half, half)
            k = 2 * i + p
            yield Gather(
                dims, cs, feed_shard, feed, at, half, order, (send.at[k], recv.at[k], local.at[k])
            )

    def tick(t):
        loop_tick(jobs, steps, 5, 2, t)

    tick(0)
    project(own, small, weights, attn_low, pre, queries, keys, values, beta, micro, length, tick)
    gain = small[ROW_OUT : ROW_OUT + 1, :HEAD]
    blocks = length // SPAN

    def one(t, carry):
        tick(micro + 1 + t)
        delta_block(
            pl.multiple_of(t * SPAN, SPAN), lax.rem(t, blocks) == 0,
            (queries, keys, values, beta, state, states, inverses, scores, fresh, mix, mixed, t), gain,
        )
        rows = pl.ds(pl.multiple_of(t * SPAN, SPAN), SPAN)
        hidden[rows, :] = own[rows, :].astype(F32) + dot_nt(mixed[rows, :], out_weight[...])
        return carry

    lax.fori_loop(0, micro * blocks, one, 0)
    begun = micro + 1 + micro * blocks

    def columns(t):
        return pl.ds(pl.multiple_of(t * (3 * FFW), 3 * FFW), 3 * FFW)

    def load(t):
        slot = lax.rem(t, 2)
        return pltpu.make_async_copy(
            feed.at[:, :, :, :, :, columns(t)], w_buf.at[slot], w_sem.at[slot]
        )

    def store(t):
        slot = lax.rem(t, 2)
        return pltpu.make_async_copy(t_buf.at[slot], terms.at[:, columns(t)], t_sem.at[slot])

    load(0).start()
    gain_mlp = small[ROW_MLP : ROW_MLP + 1, :]
    v = hidden[...]
    norm[...] = low(v * square_rms(v) * gain_mlp)
    total[...] = jnp.zeros_like(total)
    d_hidden[...] = jnp.zeros_like(d_hidden)

    def feed_step(t, carry):
        tick(begun + t)

        @pl.when(t + 1 < steps)
        def _():
            load(t + 1).start()

        load(t).wait()

        @pl.when(t >= 2)
        def _():
            store(t - 2).wait()

        slot = lax.rem(t, 2)
        w = w_buf[slot].reshape(norm.shape[1], 3 * FFW)
        feed_part(w, norm, grad, total, d_hidden, t_buf.at[slot])
        store(t).start()
        return carry

    lax.fori_loop(0, steps, feed_step, 0)
    store(steps - 2).wait()
    store(steps - 1).wait()
    n = norm.shape[1]

    def close(t, carry):
        rows = pl.ds(pl.multiple_of(t * SPAN, SPAN), SPAN)
        v, d = hidden[rows, :], d_hidden[rows, :]
        result[rows, :] = low(jnp.where(active[rows, :] > 0.0, v + total[rows, :], 0.0))
        r = square_rms(v)
        vr, gd = v * r, d * gain_mlp
        gain_grad[...] += jnp.sum(d * vr, axis=0, keepdims=True)
        whole = grad[rows, :].astype(F32) + r * (gd - vr * jnp.mean(vr * gd, axis=-1, keepdims=True))
        d_hidden[rows, :] = whole
        d_attn[rows, :] = low(whole)
        return carry

    gain_grad[...] = jnp.zeros_like(gain_grad)
    lax.fori_loop(0, micro * blocks, close, 0)

    def finish(i, carry):
        for job in jobs(i):
            job.finish()
        return carry

    lax.fori_loop(0, steps, finish, 0)


def feed_part(w, norm, grad, total, d_norm, terms):
    x, g = norm[...], grad[...]
    gw, uw, dw = (w[:, lanes(i, FFW)] for i in range(3))
    gate, up = dot(x, gw), dot(x, uw)
    d_act = dot(g, dw)
    s = jax.nn.sigmoid(gate)
    silu = gate * s
    act = low(silu * up)
    d_gate = low(d_act * up * (s + silu * (1.0 - s)))
    d_up = low(d_act * silu)
    total[...] += dot_nt(act, dw)
    d_norm[...] += dot_nt(d_gate, gw) + dot_nt(d_up, uw)
    terms[:, lanes(0, FFW)] = low(dot_tn(x, d_gate))
    terms[:, lanes(1, FFW)] = low(dot_tn(x, d_up))
    terms[:, lanes(2, FFW)] = low(dot_tn(g, act))


def forward_call(own, small, weights, out_weight, grad, active, feed_shard, micro, collective_id):
    rows, width = own.shape
    length = rows // micro
    blocks = rows // SPAN
    n = lax.axis_size("fsdp")
    dims = grid_of(n)
    k = hops(dims)
    steps = feed_shard.shape[1] // (3 * FFW)
    square = jax.ShapeDtypeStruct((blocks, HEADS, SPAN, SPAN), BF16)
    wide = jax.ShapeDtypeStruct((rows, width), BF16)
    outs = [
        wide, jax.ShapeDtypeStruct((rows, width), F32), wide, jax.ShapeDtypeStruct((1, width), F32),
        jax.ShapeDtypeStruct((width, feed_shard.shape[1]), BF16),
        jax.ShapeDtypeStruct(dims + feed_shard.shape, BF16),
        wide, jax.ShapeDtypeStruct((rows, 3 * width), BF16),
        wide, wide, wide, jax.ShapeDtypeStruct((rows, 16), F32),
        jax.ShapeDtypeStruct((blocks, HEADS, HEAD, HEAD), BF16), square, square, wide, wide, wide,
    ]
    return pl.pallas_call(
        functools.partial(forward_kernel, dims, micro, length, steps),
        out_shape=outs,
        in_specs=[vmem_spec()] * 6 + [any_spec()],
        out_specs=[vmem_spec()] * 4 + [any_spec()] * 2 + [vmem_spec()] * (len(outs) - 6),
        scratch_shapes=[
            pltpu.VMEM((HEADS, HEAD, HEAD), F32),
            pltpu.VMEM((rows, width), F32),
            pltpu.VMEM((rows, width), BF16),
            pltpu.VMEM((rows, width), F32),
            pltpu.VMEM((2,) + dims + (width // n, 3 * FFW), BF16),
            pltpu.VMEM((2, width, 3 * FFW), BF16),
            pltpu.SemaphoreType.DMA((2 * steps, k)),
            pltpu.SemaphoreType.DMA((2 * steps, k)),
            pltpu.SemaphoreType.DMA((2 * steps,)),
            pltpu.SemaphoreType.DMA((2,)),
            pltpu.SemaphoreType.DMA((2,)),
        ],
        compiler_params=pltpu.CompilerParams(
            collective_id=collective_id, has_side_effects=True, vmem_limit_bytes=VMEM_LIMIT
        ),
    )(own, small, weights, out_weight, grad, active, feed_shard)


def delta_back(base, last, refs, gain):
    (queries, keys, values, beta, states, inverses, scores, fresh, mix, d_mixed,
     d_state, d_out, d_q, d_k, d_v, d_beta, gain_grad, at) = refs
    rows = pl.ds(base, SPAN)
    i, j = iotas((SPAN, SPAN))
    lane = lax.broadcasted_iota(jnp.int32, (SPAN, 16), 1)
    heads = range(HEADS)

    @pl.when(last)
    def _():
        d_state[...] = jnp.zeros_like(d_state)

    strength = beta[rows, :]
    k = [keys[rows, lanes(h)] for h in heads]
    q = [queries[rows, lanes(h)] for h in heads]
    e = [fresh[rows, lanes(h)] for h in heads]
    b = [strength[:, h : h + 1] for h in heads]
    kb = [low(k[h].astype(F32) * b[h]) for h in heads]
    do = []
    for h in heads:
        v, d = mix[rows, lanes(h)].astype(F32), d_mixed[:, lanes(h)]
        r = lax.rsqrt(jnp.mean(v * v, axis=-1, keepdims=True) + NORM_EPS)
        vr, gd = v * r, d * gain
        gain_grad[...] += jnp.sum(d * vr, axis=0, keepdims=True)
        do.append(low(r * (gd - vr * jnp.mean(vr * gd, axis=-1, keepdims=True))))
    s = [states[at, h] for h in heads]
    p = [scores[at, h] for h in heads]
    ds = [low(d_state[h]) for h in heads]
    de = [low(dot_tn(p[h], do[h]) + dot(k[h], ds[h])) for h in heads]
    dx = [dot_tn(inverses[at, h], de[h]) for h in heads]
    dxl = [low(dx[h]) for h in heads]
    dp = [low(jnp.where(i >= j, dot_nt(do[h], e[h]), 0.0)) for h in heads]
    da = [low(jnp.where(i > j, -dot_nt(dxl[h], e[h]), 0.0)) for h in heads]
    dkb = [dot(da[h], k[h]) - dot_nt(dxl[h], s[h]) for h in heads]
    beta_grad = jnp.zeros((SPAN, 16), F32)
    for h in heads:
        d_q[rows, lanes(h)] = (dot_nt(do[h], s[h]) + dot(dp[h], k[h])).astype(d_q.dtype)
        d_k[rows, lanes(h)] = (
            dkb[h] * b[h] + dot_tn(da[h], kb[h]) + dot_tn(dp[h], q[h]) + dot_nt(e[h], ds[h])
        ).astype(d_k.dtype)
        d_v[rows, lanes(h)] = (dx[h] * b[h]).astype(d_v.dtype)
        d_state[h] += dot_tn(q[h], do[h]) - dot_tn(kb[h], dxl[h])
        db = head_sum(dkb[h] * k[h].astype(F32) + dx[h] * values[rows, lanes(h)].astype(F32))
        beta_grad += jnp.where(lane == h, db, 0.0)
    d_beta[rows, :] = low(beta_grad * strength * (1.0 - strength))


SLOTS = 6


def backward_kernel(dims, micro, length, steps, *refs):
    (d_attn, small, out_weight, pre, queries, keys, values, beta,
     states, inverses, scores, fresh, mix, mixed, feed_terms,
     d_pre, d_beta, out_grad, small_grad, feed_grad,
     d_state, d_out, d_q, d_k, d_v, gain_grad, send, recv, local, *slots) = refs
    me = lax.axis_index("fsdp")
    cs = coords_of(dims, me)
    greet_axes(dims, cs)
    half = 3 * FFW // 2

    def jobs(i):
        slot = lax.rem(i, SLOTS)
        for p, order in enumerate((CXYZ, CYXZ)):
            columns = pl.ds(pl.multiple_of(i * (3 * FFW) + p * half, half), half)
            k = 2 * i + p
            own, *got = [ref.at[slot] for ref in slots[5 * p : 5 * p + 5]]
            yield Scatter(
                dims, cs, feed_terms, columns, feed_grad, columns, order, own, got,
                (send.at[k], recv.at[k], local.at[k]),
            )

    def tick(t):
        loop_tick(jobs, steps, 5, 2, t)

    tick(0)
    width = d_attn.shape[1]
    blocks = length // SPAN
    total = micro * blocks
    gain = small[ROW_OUT : ROW_OUT + 1, :HEAD]
    gain_grad[...] = jnp.zeros_like(gain_grad)
    small_grad[...] = jnp.zeros_like(small_grad)

    def one(step, carry):
        tick(2 * step + 1)
        t = total - 1 - step
        base = pl.multiple_of(t * SPAN, SPAN)
        d_out[...] = dot(d_attn[pl.ds(base, SPAN), :], out_weight[...])
        tick(2 * step + 2)
        delta_back(
            base, lax.rem(step, blocks) == 0,
            (queries, keys, values, beta, states, inverses, scores, fresh, mix, d_out,
             d_state, None, d_q, d_k, d_v, d_beta, gain_grad, t), gain,
        )
        return carry

    lax.fori_loop(0, total, one, 0)
    row = lax.broadcasted_iota(jnp.int32, (length, HEAD), 0)

    def conv_back(m, carry):
        tick(2 * total + 1 + m)
        rows = pl.ds(m * length, length)
        for kind, grads in enumerate((d_q, d_k, d_v)):
            for h in range(width // HEAD):
                cols = lanes(h)
                wide = slice(kind * width + cols.start, kind * width + cols.stop)
                taps = small[4 * kind : 4 * kind + 4, cols]
                x = pre[rows, wide].astype(F32)
                moved = [shifted(x, c, row) for c in range(4)]
                c = moved[0] * taps[0:1]
                for o in range(1, 4):
                    c += moved[o] * taps[o : o + 1]
                s = jax.nn.sigmoid(c)
                u = c * s
                d = grads[rows, cols]
                if kind < 2:
                    n = lax.rsqrt(head_sum(u * u) + UNIT_EPS)
                    un = u * n
                    d = (d - un * head_sum(un * d)) * n
                d = d * (s + u * (1.0 - s))
                for o in range(4):
                    at = slice(4 * kind + o, 4 * kind + o + 1)
                    small_grad[at, cols] += jnp.sum(moved[o] * d, axis=0, keepdims=True)
                back = d * taps[0:1]
                for o in range(1, 4):
                    back += shifted(d, -o, row) * taps[o : o + 1]
                d_pre[rows, wide] = low(back)
        return carry

    lax.fori_loop(0, micro, conv_back, 0)
    for b in range(width // 256):
        cols = lanes(b, 256)
        out_grad[:, cols] = low(dot_tn(d_attn[...], mixed[:, cols]))
    small_grad[ROW_OUT : ROW_OUT + 1, :HEAD] = gain_grad[...]

    def rest(t, carry):
        tick(t)
        return carry

    lax.fori_loop(2 * total + 1 + micro, steps + 8, rest, 0)


def backward_call(d_attn, small, out_weight, saved, feed_terms, micro, collective_id):
    rows, width = d_attn.shape
    length = rows // micro
    n = lax.axis_size("fsdp")
    dims = grid_of(n)
    k = hops(dims)
    share = width // n
    steps = feed_terms.shape[5] // (3 * FFW)
    scratch = []
    for order in (CXYZ, CYXZ):
        scratch += scatter_scratch(dims, share, 3 * FFW // 2, order, BF16, (SLOTS,))
    return pl.pallas_call(
        functools.partial(backward_kernel, dims, micro, length, steps),
        out_shape=[
            jax.ShapeDtypeStruct((rows, 3 * width), BF16),
            jax.ShapeDtypeStruct((rows, 16), BF16),
            jax.ShapeDtypeStruct((width, width), BF16),
            jax.ShapeDtypeStruct((SMALL_ROWS, width), F32),
            jax.ShapeDtypeStruct((share, feed_terms.shape[5]), F32),
        ],
        in_specs=[vmem_spec()] * (3 + len(saved)) + [any_spec()],
        out_specs=[vmem_spec()] * 5,
        scratch_shapes=[
            pltpu.VMEM((HEADS, HEAD, HEAD), F32),
            pltpu.VMEM((SPAN, width), F32),
            pltpu.VMEM((rows, width), F32),
            pltpu.VMEM((rows, width), F32),
            pltpu.VMEM((rows, width), F32),
            pltpu.VMEM((1, HEAD), F32),
            pltpu.SemaphoreType.DMA((2 * steps, k)),
            pltpu.SemaphoreType.DMA((2 * steps, k)),
            pltpu.SemaphoreType.DMA((2 * steps,)),
        ]
        + scratch,
        compiler_params=pltpu.CompilerParams(
            collective_id=collective_id, has_side_effects=True, vmem_limit_bytes=VMEM_LIMIT
        ),
    )(d_attn, small, out_weight, *saved, feed_terms)


TAIL = 512


def tail_kernel(dims, micro, length, *refs):
    n = math.prod(dims)
    (d_hidden, own, small, weights, attn_low, d_pre, d_beta, back, out_terms, small_terms, gain_mlp,
     qkv_grad, out_grad, small_grad, returned,
     d_rows, outgoing, row_sum, small_buf, tok_send, tok_recv, tok_local, send, recv, local,
     *scr) = refs
    me = lax.axis_index("fsdp")
    cs = coords_of(dims, me)
    greet_all(n, me)
    width = own.shape[1]
    share = width // n
    rows = micro * length
    tokens = Tokens(n, me, outgoing, returned, tok_send, tok_recv, tok_local)
    pieces = 3 * width // TAIL
    job_list, at = [], 0
    sems = lambda i: (send.at[i], recv.at[i], local.at[i])
    buffers = []
    for i in range(width // TAIL):
        own_buf, *got = scr[at : at + 5]
        at += 5
        job_list.append(Scatter(
            dims, cs, out_terms, pl.ds(i * TAIL, TAIL), out_grad, pl.ds(i * TAIL, TAIL),
            (CXYZ, CYXZ)[i % 2], own_buf, got, sems(len(job_list)),
        ))
    for i in range(pieces):
        term, *got = scr[at : at + 5]
        at += 5
        buffers.append(term)
        job_list.append(Scatter(
            dims, cs, term, pl.ds(0, TAIL), qkv_grad, pl.ds(i * TAIL, TAIL),
            (CXYZ, CYXZ)[i % 2], None, got, sems(len(job_list)),
        ))
    job_list.append(Scatter(
        dims, cs, small_buf, pl.ds(0, HEAD), small_grad, pl.ds(0, HEAD), CXYZ, None, scr[at : at + 4],
        sems(len(job_list)),
    ))
    lead = width // TAIL
    tick = lambda t: run_tick(job_list, 5, 2, t)
    for t in range(lead):
        tick(t)
    beta_rows = low(small[ROW_BETA : ROW_BETA + 16, :])
    attn_gain = small[ROW_ATTN : ROW_ATTN + 1, :]
    row_sum[...] = jnp.zeros_like(row_sum)
    parts = outgoing.shape[1] * n * own.shape[1] // outgoing.shape[2] // rows
    thin = outgoing.shape[2]

    def block(t, carry):
        at = pl.ds(pl.multiple_of(t * SPAN, SPAN), SPAN)
        d = dot_nt(d_pre[at, :], weights[...]) + dot(d_beta[at, :], beta_rows)
        v = own[at, :].astype(F32)
        r = square_rms(v)
        vr, gd = v * r, d * attn_gain
        row_sum[...] += jnp.sum(d * vr, axis=0, keepdims=True)
        d_rows[at, :] = low(d_hidden[at, :] + r * (gd - vr * jnp.mean(vr * gd, axis=-1, keepdims=True)))
        return carry

    lax.fori_loop(0, rows // SPAN, block, 0)
    place_tokens(back, d_rows, outgoing)
    tokens.start()
    for i in range(pieces):
        cols = lanes(i, TAIL)
        grads = low(dot_tn(attn_low[...], d_pre[:, cols]))
        buffers[i][...] = grads.reshape(dims + (share, TAIL))
        tick(lead + i)
    small_part(n, small_terms, gain_mlp, row_sum, dot_tn(d_beta[...], attn_low[...]), small_buf, dims)
    for t in range(lead + pieces, len(job_list) + 8):
        tick(t)
    tokens.wait()


def place_tokens(back, rows, outgoing):
    n, count, thin = outgoing.shape
    for p in range(rows.shape[1] // thin):
        hot = lax.broadcasted_iota(jnp.int32, (n * count, rows.shape[0]), 1) == back[:, p : p + 1]
        pick = dot(low(jnp.where(hot, 1.0, 0.0)), rows[:, lanes(p, thin)])
        if p == 0:
            held = pick
        else:
            held = held + pick
    outgoing[...] = low(held).reshape(n, count, thin)


def small_part(n, terms, gain_mlp, gain_attn, beta_grad, out, dims):
    width = terms.shape[1]
    share, few = width // n, HEAD // n
    i = lax.broadcasted_iota(jnp.int32, (HEAD, width), 0)
    c = lax.broadcasted_iota(jnp.int32, (HEAD, width), 1)
    spread = (lax.rem(c, share) < few) & (i == (c // share) * few + lax.rem(c, share))
    wide = jnp.broadcast_to(terms[ROW_OUT : ROW_OUT + 1, :HEAD], (HEAD, HEAD)).T[:, 0:1]
    gain_out = jnp.sum(jnp.where(spread, wide, 0.0), axis=0, keepdims=True)
    block = jnp.concatenate(
        [terms[:ROW_ATTN, :], gain_attn[...], gain_mlp[...], gain_out, jnp.zeros((1, width), F32), beta_grad,
         jnp.zeros((HEAD - SMALL_ROWS, width), F32)], axis=0,
    )
    out[...] = block.T.reshape(dims + (share, HEAD))


def tail_call(d_hidden, own, small, weights, attn_low, d_pre, d_beta, back, out_terms, small_terms,
              gain_mlp, token_shape, micro, collective_id):
    rows, width = own.shape
    n = lax.axis_size("fsdp")
    dims = grid_of(n)
    k = hops(dims)
    share = width // n
    scratch = []
    for i in range(width // TAIL):
        scratch += scatter_scratch(dims, share, TAIL, (CXYZ, CYXZ)[i % 2], BF16)
    for i in range(3 * width // TAIL):
        scratch.append(pltpu.VMEM(dims + (share, TAIL), BF16))
        scratch += scatter_scratch(dims, share, TAIL, (CXYZ, CYXZ)[i % 2], BF16, keep=False)
    scratch += scatter_scratch(dims, share, HEAD, CXYZ, F32, keep=False)
    m = 4 * width // TAIL + 1
    return pl.pallas_call(
        functools.partial(tail_kernel, dims, micro, rows // micro),
        out_shape=[
            jax.ShapeDtypeStruct((share, 3 * width), F32),
            jax.ShapeDtypeStruct((share, width), F32),
            jax.ShapeDtypeStruct((share, HEAD), F32),
            jax.ShapeDtypeStruct(token_shape, BF16),
        ],
        in_specs=[vmem_spec()] * 8 + [any_spec()] + [vmem_spec()] * 2,
        out_specs=[vmem_spec()] * 3 + [any_spec()],
        scratch_shapes=[
            pltpu.VMEM((rows, width), BF16),
            pltpu.VMEM(token_shape, BF16),
            pltpu.VMEM((1, width), F32),
            pltpu.VMEM(dims + (share, HEAD), F32),
        ]
        + token_sems(n)
        + [
            pltpu.SemaphoreType.DMA((m, k)),
            pltpu.SemaphoreType.DMA((m, k)),
            pltpu.SemaphoreType.DMA((m,)),
        ]
        + scratch,
        compiler_params=pltpu.CompilerParams(
            collective_id=collective_id, has_side_effects=True, vmem_limit_bytes=VMEM_LIMIT
        ),
    )(d_hidden, own, small, weights, attn_low, d_pre, d_beta, back, out_terms, small_terms, gain_mlp)


def picked(index, source):
    hot = index[:, None] == jnp.arange(source.shape[0], dtype=jnp.int32)[None, :]
    return jnp.dot(low(hot), source, preferred_element_type=F32).astype(BF16)


def split_rows(values, parts):
    cut = values.reshape(values.shape[:-1] + (parts, values.shape[-1] // parts))
    return jnp.moveaxis(cut, -2, 0)


def spans(width, size):
    at = 0
    while at < width:
        yield at, min(size, width - at)
        at += size


def local(
    inputs, cotangent, lengths, owners, attn_gain, query_weight, key_weight, value_weight, beta_weight,
    query_conv, key_conv, value_conv, out_gain, out_weight, mlp_gain, gate_weight, up_weight, down_weight,
):
    n = lax.axis_size("fsdp")
    dims = grid_of(n)
    me = lax.axis_index("fsdp")
    micro, _, length, width = inputs.shape
    hidden_units = gate_weight.shape[1]
    share = width // n
    if share % 16:
        return local_thin(
            inputs, cotangent, lengths, owners, attn_gain, query_weight, key_weight, value_weight, beta_weight,
            query_conv, key_conv, value_conv, out_gain, out_weight, mlp_gain, gate_weight, up_weight, down_weight,
        )
    slots = length // n
    per = micro * slots
    parts = 16 // math.gcd(per, 16)
    thin = width // parts
    i32 = jnp.int32
    devices = jnp.arange(n, dtype=i32)
    slot_ids = jnp.arange(slots, dtype=i32)
    row_ids = jnp.arange(length, dtype=i32)
    micros = jnp.arange(micro, dtype=i32)
    part_ids = jnp.arange(parts, dtype=i32)

    before = devices[:, None] < devices[None, :]
    starts = jnp.sum(jnp.where(before[None], lengths[:, :, None], 0), axis=1)
    match = owners[:, None, :] == devices[None, :, None]
    own_start = jnp.sum(jnp.where(match, starts[:, None, :], 0), axis=2)
    own_len = jnp.sum(jnp.where(match, lengths[:, None, :], 0), axis=2)
    mine = devices == me
    my_start = jnp.sum(jnp.where(mine, own_start, 0), axis=1)
    my_len = jnp.sum(jnp.where(mine, own_len, 0), axis=1)

    first = own_start + (me - own_start) % n
    pos = first[:, :, None] + n * slot_ids
    live = pos < (own_start + own_len)[:, :, None]
    send = jnp.where(live, micros[:, None, None] * length + pos // n, -1)
    send = jnp.moveaxis(send, 0, 1)[:, None] + jnp.zeros((1, parts, 1, 1), i32)
    send = jnp.where(send >= 0, send + (part_ids * micro * length)[None, :, None, None], -1)
    rows_in = split_rows(inputs[:, 0].reshape(micro * length, width), parts).reshape(-1, thin)
    outgoing = picked(send.reshape(-1), rows_in).reshape(n, parts * per, thin)

    def row_of(v):
        return jnp.pad(v, ((0, 0), (0, share - v.shape[1])))

    packed = jnp.concatenate([
        query_conv, key_conv, value_conv, attn_gain[None], mlp_gain[None], row_of(out_gain[None]),
        jnp.zeros((1, share), BF16), beta_weight.T, jnp.zeros((SMALL_ROWS - 16 - HEADS, share), BF16),
    ])
    count = SMALL_ROWS * share // HEAD
    packed = jnp.pad(packed.reshape(count, HEAD), ((0, -count % 16), (0, 0)))

    attn_shard = jnp.concatenate([query_weight, key_weight, value_weight], axis=1)
    steps = hidden_units // FFW
    feed_shard = jnp.stack(
        [w.reshape(share, steps, FFW) for w in (gate_weight, up_weight, down_weight.T)], axis=2
    ).reshape(share, 3 * hidden_units)

    plan = [(0, 0, HEAD, ZXY)]
    for a, w in ((1, 3 * width), (2, width)):
        for at, wide in spans(w, 512):
            plan.append((a, at, wide, (ZXY, ZYX)[len(plan) % 2]))
    small_all, qkv, out_t, incoming = gather_call(
        [packed, attn_shard, out_weight.T], outgoing, tuple(plan), 2, 1
    )
    small = small_all.reshape(n, -1)[:, : SMALL_ROWS * share].reshape(n, SMALL_ROWS, share)
    small = jnp.moveaxis(small, 1, 0)
    gain_row = small[ROW_OUT, :, : HEAD // n].reshape(1, HEAD)
    small = small.reshape(SMALL_ROWS, width).astype(F32)
    small = lax.dynamic_update_slice(small, gain_row.astype(F32), (ROW_OUT, 0))
    qkv, out_t = qkv.reshape(width, 3 * width), out_t.reshape(width, width)

    active = row_ids[None] < my_len[:, None]
    block = (my_start[:, None] + row_ids) % n
    at = block * (parts * per) + micros[:, None] * slots + row_ids // n
    take = jnp.where(active, at, -1).reshape(-1)
    flat = incoming.reshape(n * parts * per, thin)
    own = jnp.concatenate(
        [picked(jnp.where(take >= 0, take + p * per, -1), flat) for p in range(parts)], axis=1
    )
    active = active.reshape(-1, 1)
    grad = jnp.where(active, cotangent[:, 0].reshape(-1, width), jnp.zeros((), BF16))

    result, d_hidden, d_attn, mlp_gain_terms, feed_terms, _, attn_low, *saved = forward_call(
        own, small, qkv, out_t, grad, active.astype(F32), feed_shard, micro, 2
    )
    feed_terms = feed_terms.reshape(dims + (share, 3 * hidden_units))
    d_pre, d_beta, out_terms, small_terms, feed_grad = backward_call(
        d_attn, small, out_t, saved, feed_terms, micro, 3
    )

    back = slot_ids * n + (devices[:, None, None] - my_start[None, :, None]) % n
    back = jnp.where(back < my_len[None, :, None], back + (micros * length)[None, :, None], -1)
    back = jnp.where(
        (part_ids[:, None] == part_ids[None, :])[None, :, None, None, :], back[:, None, :, :, None], -1
    )
    back = back.reshape(n * parts * per, parts)
    qkv_grad, out_grad, small_grad, returned = tail_call(
        d_hidden, own, small, qkv, attn_low, d_pre, d_beta, back,
        out_terms.reshape(dims + (share, width)), small_terms, mlp_gain_terms,
        (n, parts * per, thin), micro, 4,
    )

    place = row_ids * n + me
    inside = (place[None, :, None] >= own_start[:, None, :]) & (
        place[None, :, None] < (own_start + own_len)[:, None, :]
    )
    at = devices * (parts * per) + micros[:, None, None] * slots + (place[None, :, None] - first[:, None, :]) // n
    take = (jnp.sum(jnp.where(inside, at + 1, 0), axis=2) - 1).reshape(-1)
    flat = returned.reshape(n * parts * per, thin)
    input_rows = jnp.concatenate(
        [picked(jnp.where(take >= 0, take + p * per, -1), flat) for p in range(parts)], axis=1
    )

    small_grad = small_grad.T
    feed_grad = feed_grad.reshape(share, steps, 3, FFW)
    gate_grad, up_grad, down_grad = (
        feed_grad[:, :, i].reshape(share, hidden_units) for i in range(3)
    )
    return (
        result.reshape(micro, 1, length, width),
        input_rows.reshape(micro, 1, length, width),
        small_grad[ROW_ATTN],
        qkv_grad[:, :width],
        qkv_grad[:, width : 2 * width],
        qkv_grad[:, 2 * width :],
        small_grad[ROW_BETA : ROW_BETA + HEADS].T,
        small_grad[0:4],
        small_grad[4:8],
        small_grad[8:12],
        small_grad[ROW_OUT, : HEAD // n],
        out_grad.T,
        small_grad[ROW_MLP],
        gate_grad,
        up_grad,
        down_grad.T,
    )


class GatherThin:
    def __init__(self, dims, cs, shard, out, low, width, order, sems):
        self.dims, self.cs, self.order = dims, cs, order
        self.columns = pl.ds(low, width)
        self.shard, self.out = shard.at[:, self.columns], out
        self.send, self.recv, self.local_thin = sems

    def slot(self, stage, delta):
        return sum(self.dims[a] - 1 for a in self.order[:stage]) + delta - 1

    def region(self, stage, cs):
        done = self.order[:stage]
        lead = tuple(slice(None) if k in done else cs[k] for k in range(4))
        return self.out.at[lead + (slice(None), self.columns)]

    def copies(self, stage, incoming):
        axis = self.order[stage]
        for delta in range(1, self.dims[axis]):
            frm = along(self.dims, self.cs, axis, -delta) if incoming else self.cs
            to = along(self.dims, self.cs, axis, delta)
            k = self.slot(stage, delta)
            yield pltpu.make_async_remote_copy(
                src_ref=self.shard if stage == 0 else self.region(stage, self.cs),
                dst_ref=self.region(stage, frm),
                send_sem=self.send.at[k],
                recv_sem=self.recv.at[k],
                device_id=(index_of(self.dims, to),),
                device_id_type=MESH,
            )

    def keep(self):
        return pltpu.make_async_copy(self.shard, self.region(0, self.cs), self.local_thin)

    def step(self, stage):
        if stage == 0:
            self.keep().start()
        if stage == 1:
            self.keep().wait()
        if stage >= 1:
            for c in self.copies(stage - 1, True):
                c.wait_recv()
        if stage < 4:
            for c in self.copies(stage, False):
                c.start()

    def finish(self):
        for stage in range(4):
            for c in self.copies(stage, False):
                c.wait_send()


def pipelined_thin(jobs, stages, lag):
    for tick in range(len(jobs) + (stages - 1) * lag):
        for stage in range(stages):
            i = tick - stage * lag
            if 0 <= i < len(jobs):
                jobs[i].step(stage)


def gather_kernel_thin(dims, plan, lag, count, with_tokens, *refs):
    n = math.prod(dims)
    t = 1 if with_tokens else 0
    ins, outs, scr = refs[: count + t], refs[count + t : 2 * (count + t)], refs[2 * (count + t) :]
    send, recv, local_thin = scr[:3]
    me = lax.axis_index("fsdp")
    cs = coords_of(dims, me)
    if with_tokens:
        greet_all(n, me)
        tokens = Tokens(n, me, ins[count], outs[count], *scr[3:])
        tokens.start()
    else:
        greet_axes(dims, cs)
    jobs = [
        GatherThin(dims, cs, ins[a], outs[a], low, width, order, (send.at[i], recv.at[i], local_thin.at[i]))
        for i, (a, low, width, order) in enumerate(plan)
    ]
    pipelined_thin(jobs, 5, lag)
    for j in jobs:
        j.finish()
    if with_tokens:
        tokens.wait()


def gather_call_thin(shards, tokens, plan, lag, collective_id):
    n = lax.axis_size("fsdp")
    dims = grid_of(n)
    k = hops(dims)
    ins = list(shards) + ([] if tokens is None else [tokens])
    outs = [jax.ShapeDtypeStruct(dims + s.shape, s.dtype) for s in shards]
    if tokens is not None:
        outs.append(jax.ShapeDtypeStruct(tokens.shape, tokens.dtype))
    m = len(plan)
    return pl.pallas_call(
        functools.partial(gather_kernel_thin, dims, plan, lag, len(shards), tokens is not None),
        out_shape=outs,
        in_specs=[any_spec()] * len(ins),
        out_specs=[any_spec()] * len(outs),
        scratch_shapes=[
            pltpu.SemaphoreType.DMA((m, k)),
            pltpu.SemaphoreType.DMA((m, k)),
            pltpu.SemaphoreType.DMA((m,)),
        ]
        + ([] if tokens is None else token_sems(n)),
        compiler_params=pltpu.CompilerParams(
            collective_id=collective_id, has_side_effects=True, vmem_limit_bytes=VMEM_LIMIT
        ),
    )(*ins)


class ScatterThin:
    def __init__(self, dims, cs, terms, result, low, width, order, scratch, sems):
        self.dims, self.cs, self.order = dims, cs, order
        self.columns = pl.ds(low, width)
        self.terms, self.result = terms, result
        self.own, self.got = scratch[0], scratch[1:]
        self.send, self.recv, self.local_thin = sems

    def slot(self, stage, delta):
        return sum(self.dims[a] - 1 for a in self.order[:stage]) + delta - 1

    def part(self, stage, at):
        axis = self.order[stage]
        if stage == 0:
            lead = tuple(at if k == axis else slice(None) for k in range(4))
            return self.terms.at[lead + (slice(None), self.columns)]
        left = [k for k in range(4) if k not in self.order[:stage]]
        return self.got[stage - 1].at[(0,) + tuple(at if k == axis else slice(None) for k in left)]

    def copies(self, stage):
        axis = self.order[stage]
        for delta in range(1, self.dims[axis]):
            to = along(self.dims, self.cs, axis, delta)
            k = self.slot(stage, delta)
            yield pltpu.make_async_remote_copy(
                src_ref=self.part(stage, to[axis]),
                dst_ref=self.got[stage].at[delta - 1],
                send_sem=self.send.at[k],
                recv_sem=self.recv.at[k],
                device_id=(index_of(self.dims, to),),
                device_id_type=MESH,
            )

    def keep(self):
        return pltpu.make_async_copy(self.part(0, self.cs[self.order[0]]), self.own, self.local_thin)

    def total(self, stage):
        axis = self.order[stage]
        left = [k for k in range(4) if k not in self.order[: stage + 1]]
        shape = [self.dims[k] for k in left]
        got = self.got[stage]
        mine = self.own if stage == 0 else self.part(stage, self.cs[axis])

        def one(i, carry):
            at = tuple(coords_of(shape, i)) if shape else ()
            total = mine[at + (slice(None), slice(None))].astype(F32)
            for delta in range(1, self.dims[axis]):
                total += got[(delta - 1,) + at + (slice(None), slice(None))].astype(F32)
            if left:
                got[(0,) + at + (slice(None), slice(None))] = total.astype(got.dtype)
            else:
                self.result[:, self.columns] = total
            return carry

        lax.fori_loop(0, math.prod(shape), one, 0)

    def step(self, stage):
        if stage == 0:
            self.keep().start()
        if stage == 1:
            self.keep().wait()
        if stage >= 1:
            for c in self.copies(stage - 1):
                c.wait_recv()
            self.total(stage - 1)
        if stage < 4:
            for c in self.copies(stage):
                c.start()

    def finish(self):
        for stage in range(4):
            for c in self.copies(stage):
                c.wait_send()


def scatter_scratch_thin(dims, rows, width, order, dtype):
    left = list(dims)
    out = [pltpu.VMEM(tuple(d for k, d in enumerate(dims) if k != order[0]) + (rows, width), dtype)]
    for s, axis in enumerate(order):
        rest = tuple(dims[k] for k in range(4) if k not in order[: s + 1])
        out.append(pltpu.VMEM((dims[axis] - 1,) + rest + (rows, width), dtype))
    return out


def scatter_kernel_thin(dims, plan, lag, count, with_tokens, *refs):
    n = math.prod(dims)
    t = 1 if with_tokens else 0
    ins, outs, scr = refs[: count + t], refs[count + t : 2 * (count + t)], refs[2 * (count + t) :]
    send, recv, local_thin = scr[:3]
    scr = scr[3:]
    me = lax.axis_index("fsdp")
    cs = coords_of(dims, me)
    if with_tokens:
        greet_all(n, me)
        tokens = Tokens(n, me, ins[count], outs[count], *scr[:3])
        tokens.start()
        scr = scr[3:]
    else:
        greet_axes(dims, cs)
    jobs = [
        ScatterThin(
            dims, cs, ins[a], outs[a], low, width, order, scr[5 * i : 5 * i + 5],
            (send.at[i], recv.at[i], local_thin.at[i]),
        )
        for i, (a, low, width, order) in enumerate(plan)
    ]
    pipelined_thin(jobs, 5, lag)
    for j in jobs:
        j.finish()
    if with_tokens:
        tokens.wait()


def scatter_call_thin(terms, tokens, plan, lag, collective_id):
    n = lax.axis_size("fsdp")
    dims = grid_of(n)
    k = hops(dims)
    ins = list(terms) + ([] if tokens is None else [tokens])
    outs = [jax.ShapeDtypeStruct(s.shape[4:], F32) for s in terms]
    out_specs = [vmem_spec()] * len(terms)
    if tokens is not None:
        outs.append(jax.ShapeDtypeStruct(tokens.shape, tokens.dtype))
        out_specs.append(any_spec())
    m = len(plan)
    scratch = []
    for a, low, width, order in plan:
        scratch += scatter_scratch_thin(dims, terms[a].shape[4], width, order, terms[a].dtype)
    return pl.pallas_call(
        functools.partial(scatter_kernel_thin, dims, plan, lag, len(terms), tokens is not None),
        out_shape=outs,
        in_specs=[any_spec()] * len(ins),
        out_specs=out_specs,
        scratch_shapes=[
            pltpu.SemaphoreType.DMA((m, k)),
            pltpu.SemaphoreType.DMA((m, k)),
            pltpu.SemaphoreType.DMA((m,)),
        ]
        + ([] if tokens is None else token_sems(n))
        + scratch,
        compiler_params=pltpu.CompilerParams(
            collective_id=collective_id, has_side_effects=True, vmem_limit_bytes=VMEM_LIMIT
        ),
    )(*ins)


def project_thin(own, small, weights, attn_low, pre, queries, keys, values, beta, micro, length):
    width = own.shape[1]
    row = lax.broadcasted_iota(jnp.int32, (length, 2 * HEAD), 0)
    gain = small[ROW_ATTN : ROW_ATTN + 1, :]
    beta_rows = low(small[ROW_BETA : ROW_BETA + 16, :])

    def one(m, carry):
        rows = pl.ds(m * length, length)
        v = own[rows, :].astype(F32)
        r = lax.rsqrt(jnp.mean(v * v, axis=-1, keepdims=True) + NORM_EPS)
        attn_low[rows, :] = low(v * r * gain)
        a = attn_low[rows, :]
        beta[rows, :] = jax.nn.sigmoid(dot_nt(a, beta_rows))
        for kind, out in enumerate((queries, keys, values)):
            for b in range(width // (2 * HEAD)):
                cols = lanes(b, 2 * HEAD)
                wide = slice(kind * width + cols.start, kind * width + cols.stop)
                x = dot(a, weights[:, wide])
                pre[rows, wide] = low(x)
                c = conv(x, small[4 * kind : 4 * kind + 4, cols], row)
                u = c * jax.nn.sigmoid(c)
                if kind == 2:
                    out[rows, cols] = low(u)
                    continue
                for h in range(2):
                    part = u[:, lanes(h)]
                    n = lax.rsqrt(head_sum(part * part) + UNIT_EPS)
                    out[rows, slice(cols.start + h * HEAD, cols.start + (h + 1) * HEAD)] = low(part * n)
        return carry

    lax.fori_loop(0, micro, one, 0)


def forward_kernel_thin(micro, length, *refs):
    (own, small, weights, out_weight, hidden, attn_low, pre, queries, keys, values, beta,
     states, inverses, scores, fresh, mix, mixed, state) = refs
    project_thin(own, small, weights, attn_low, pre, queries, keys, values, beta, micro, length)
    gain = small[ROW_OUT : ROW_OUT + 1, :HEAD]
    blocks = length // SPAN

    def one(t, carry):
        delta_block(
            pl.multiple_of(t * SPAN, SPAN), lax.rem(t, blocks) == 0,
            (queries, keys, values, beta, state, states, inverses, scores, fresh, mix, mixed, t), gain,
        )
        rows = pl.ds(pl.multiple_of(t * SPAN, SPAN), SPAN)
        hidden[rows, :] = own[rows, :].astype(F32) + dot_nt(mixed[rows, :], out_weight[...])
        return carry

    lax.fori_loop(0, micro * blocks, one, 0)


def forward_call_thin(own, small, weights, out_weight, micro):
    rows, width = own.shape
    length = rows // micro
    blocks = rows // SPAN
    square = jax.ShapeDtypeStruct((blocks, HEADS, SPAN, SPAN), BF16)
    wide = jax.ShapeDtypeStruct((rows, width), BF16)
    outs = [
        jax.ShapeDtypeStruct((rows, width), F32), wide, jax.ShapeDtypeStruct((rows, 3 * width), BF16),
        wide, wide, wide, jax.ShapeDtypeStruct((rows, 16), F32),
        jax.ShapeDtypeStruct((blocks, HEADS, HEAD, HEAD), BF16), square, square, wide, wide, wide,
    ]
    return pl.pallas_call(
        functools.partial(forward_kernel_thin, micro, length),
        out_shape=outs,
        in_specs=[vmem_spec()] * 4,
        out_specs=[vmem_spec()] * len(outs),
        scratch_shapes=[pltpu.VMEM((HEADS, HEAD, HEAD), F32)],
        compiler_params=pltpu.CompilerParams(vmem_limit_bytes=VMEM_LIMIT),
    )(own, small, weights, out_weight)


def feed_kernel_thin(steps, hidden, grad, small, active, w_ref, result, terms, d_hidden, gain_grad, norm, total, d_norm):
    t = pl.program_id(0)
    gain = small[ROW_MLP : ROW_MLP + 1, :]

    @pl.when(t == 0)
    def _():
        v = hidden[...]
        r = lax.rsqrt(jnp.mean(v * v, axis=-1, keepdims=True) + NORM_EPS)
        norm[...] = low(v * r * gain)
        total[...] = v
        d_norm[...] = jnp.zeros_like(d_norm)

    x, g = norm[...], grad[...]
    gw, uw, dw = (w_ref[:, lanes(i, FFW)] for i in range(3))
    gate, up = dot(x, gw), dot(x, uw)
    d_act = dot(g, dw)
    s = jax.nn.sigmoid(gate)
    silu = gate * s
    act = low(silu * up)
    d_gate = low(d_act * up * (s + silu * (1.0 - s)))
    d_up = low(d_act * silu)
    total[...] += dot_nt(act, dw)
    d_norm[...] += dot_nt(d_gate, gw) + dot_nt(d_up, uw)
    terms[:, lanes(0, FFW)] = low(dot_tn(x, d_gate))
    terms[:, lanes(1, FFW)] = low(dot_tn(x, d_up))
    terms[:, lanes(2, FFW)] = low(dot_tn(g, act))

    @pl.when(t == steps - 1)
    def _():
        result[...] = low(jnp.where(active[...] > 0.0, total[...], 0.0))
        v, d = hidden[...], d_norm[...]
        n = v.shape[1]
        r = lax.rsqrt(jnp.mean(v * v, axis=-1, keepdims=True) + NORM_EPS)
        vr = v * r
        gain_grad[...] = jnp.sum(d * vr, axis=0, keepdims=True)
        gd = d * gain
        d_hidden[...] = g.astype(F32) + r * (gd - vr * (jnp.sum(vr * gd, axis=-1, keepdims=True) / n))


def feed_call_thin(hidden, grad, small, active, weights):
    rows, width = hidden.shape
    steps = weights.shape[1] // (3 * FFW)
    whole = lambda *shape: pl.BlockSpec(shape, lambda t: (0,) * len(shape))
    block = pl.BlockSpec((width, 3 * FFW), lambda t: (0, t))
    return pl.pallas_call(
        functools.partial(feed_kernel_thin, steps),
        grid=(steps,),
        out_shape=[
            jax.ShapeDtypeStruct((rows, width), BF16),
            jax.ShapeDtypeStruct(weights.shape, BF16),
            jax.ShapeDtypeStruct((rows, width), F32),
            jax.ShapeDtypeStruct((1, width), F32),
        ],
        in_specs=[whole(rows, width), whole(rows, width), whole(*small.shape), whole(rows, 1), block],
        out_specs=[whole(rows, width), block, whole(rows, width), whole(1, width)],
        scratch_shapes=[
            pltpu.VMEM((rows, width), BF16),
            pltpu.VMEM((rows, width), F32),
            pltpu.VMEM((rows, width), F32),
        ],
        compiler_params=pltpu.CompilerParams(
            vmem_limit_bytes=VMEM_LIMIT, dimension_semantics=("arbitrary",)
        ),
    )(hidden, grad, small, active, weights)


def backward_kernel_thin(micro, length, *refs):
    (d_hidden, own, small, weights, out_weight, attn_low, pre, queries, keys, values, beta,
     states, inverses, scores, fresh, mix, mixed,
     d_own, qkv_grad, out_grad, small_grad,
     d_state, d_out, d_q, d_k, d_v, d_beta, d_pre, d_attn, gain_grad) = refs
    width = own.shape[1]
    blocks = length // SPAN
    total = micro * blocks
    gain = small[ROW_OUT : ROW_OUT + 1, :HEAD]
    gain_grad[...] = jnp.zeros_like(gain_grad)
    small_grad[...] = jnp.zeros_like(small_grad)
    d_attn[...] = low(d_hidden[...])

    def one(step, carry):
        t = total - 1 - step
        base = pl.multiple_of(t * SPAN, SPAN)
        d_out[...] = dot(d_attn[pl.ds(base, SPAN), :], out_weight[...])
        delta_back(
            base, lax.rem(step, blocks) == 0,
            (queries, keys, values, beta, states, inverses, scores, fresh, mix, d_out,
             d_state, None, d_q, d_k, d_v, d_beta, gain_grad, t), gain,
        )
        return carry

    lax.fori_loop(0, total, one, 0)
    row = lax.broadcasted_iota(jnp.int32, (length, HEAD), 0)

    def conv_back(m, carry):
        rows = pl.ds(m * length, length)
        for kind, grads in enumerate((d_q, d_k, d_v)):
            for h in range(width // HEAD):
                cols = lanes(h)
                wide = slice(kind * width + cols.start, kind * width + cols.stop)
                taps = small[4 * kind : 4 * kind + 4, cols]
                x = pre[rows, wide].astype(F32)
                moved = [shifted(x, c, row) for c in range(4)]
                c = moved[0] * taps[0:1]
                for o in range(1, 4):
                    c += moved[o] * taps[o : o + 1]
                s = jax.nn.sigmoid(c)
                u = c * s
                d = grads[rows, cols].astype(F32)
                if kind < 2:
                    n = lax.rsqrt(head_sum(u * u) + UNIT_EPS)
                    un = u * n
                    d = (d - un * head_sum(un * d)) * n
                d = d * (s + u * (1.0 - s))
                for o in range(4):
                    at = slice(4 * kind + o, 4 * kind + o + 1)
                    small_grad[at, cols] += jnp.sum(moved[o] * d, axis=0, keepdims=True)
                back = d * taps[0:1]
                for o in range(1, 4):
                    back += shifted(d, -o, row) * taps[o : o + 1]
                d_pre[rows, wide] = low(back)
        return carry

    lax.fori_loop(0, micro, conv_back, 0)
    for b in range(width // 256):
        cols = lanes(b, 256)
        out_grad[:, cols] = low(dot_tn(d_attn[...], mixed[:, cols]))
    for b in range(3 * width // 256):
        cols = lanes(b, 256)
        qkv_grad[:, cols] = low(dot_tn(attn_low[...], d_pre[:, cols]))
    beta_rows = low(small[ROW_BETA : ROW_BETA + 16, :])
    small_grad[ROW_BETA : ROW_BETA + 16, :] = dot_tn(d_beta[...], attn_low[...])
    small_grad[ROW_OUT : ROW_OUT + 1, :HEAD] = gain_grad[...]
    attn_gain = small[ROW_ATTN : ROW_ATTN + 1, :]

    def finish(t, carry):
        rows = pl.ds(pl.multiple_of(t * SPAN, SPAN), SPAN)
        d = dot_nt(d_pre[rows, :], weights[...]) + dot(d_beta[rows, :], beta_rows)
        v = own[rows, :].astype(F32)
        r = lax.rsqrt(jnp.mean(v * v, axis=-1, keepdims=True) + NORM_EPS)
        vr, gd = v * r, d * attn_gain
        small_grad[ROW_ATTN : ROW_ATTN + 1, :] += jnp.sum(d * vr, axis=0, keepdims=True)
        d_own[rows, :] = low(d_hidden[rows, :] + r * (gd - vr * jnp.mean(vr * gd, axis=-1, keepdims=True)))
        return carry

    lax.fori_loop(0, total, finish, 0)


def backward_call_thin(d_hidden, own, small, weights, out_weight, saved, micro):
    rows, width = own.shape
    length = rows // micro
    return pl.pallas_call(
        functools.partial(backward_kernel_thin, micro, length),
        out_shape=[
            jax.ShapeDtypeStruct((rows, width), BF16),
            jax.ShapeDtypeStruct((width, 3 * width), BF16),
            jax.ShapeDtypeStruct((width, width), BF16),
            jax.ShapeDtypeStruct((SMALL_ROWS, width), F32),
        ],
        in_specs=[vmem_spec()] * (5 + len(saved)),
        out_specs=[vmem_spec()] * 4,
        scratch_shapes=[
            pltpu.VMEM((HEADS, HEAD, HEAD), F32),
            pltpu.VMEM((SPAN, width), F32),
            pltpu.VMEM((rows, width), BF16),
            pltpu.VMEM((rows, width), BF16),
            pltpu.VMEM((rows, width), BF16),
            pltpu.VMEM((rows, 16), BF16),
            pltpu.VMEM((rows, 3 * width), BF16),
            pltpu.VMEM((rows, width), BF16),
            pltpu.VMEM((1, HEAD), F32),
        ],
        compiler_params=pltpu.CompilerParams(vmem_limit_bytes=VMEM_LIMIT),
    )(d_hidden, own, small, weights, out_weight, *saved)


def local_thin(
    inputs, cotangent, lengths, owners, attn_gain, query_weight, key_weight, value_weight, beta_weight,
    query_conv, key_conv, value_conv, out_gain, out_weight, mlp_gain, gate_weight, up_weight, down_weight,
):
    n = lax.axis_size("fsdp")
    dims = grid_of(n)
    me = lax.axis_index("fsdp")
    micro, _, length, width = inputs.shape
    hidden_units = gate_weight.shape[1]
    share = width // n
    slots = length // n
    per = micro * slots
    parts = 16 // math.gcd(per, 16)
    thin = width // parts
    i32 = jnp.int32
    devices = jnp.arange(n, dtype=i32)
    slot_ids = jnp.arange(slots, dtype=i32)
    row_ids = jnp.arange(length, dtype=i32)
    micros = jnp.arange(micro, dtype=i32)
    part_ids = jnp.arange(parts, dtype=i32)

    before = devices[:, None] < devices[None, :]
    starts = jnp.sum(jnp.where(before[None], lengths[:, :, None], 0), axis=1)
    match = owners[:, None, :] == devices[None, :, None]
    own_start = jnp.sum(jnp.where(match, starts[:, None, :], 0), axis=2)
    own_len = jnp.sum(jnp.where(match, lengths[:, None, :], 0), axis=2)
    mine = devices == me
    my_start = jnp.sum(jnp.where(mine, own_start, 0), axis=1)
    my_len = jnp.sum(jnp.where(mine, own_len, 0), axis=1)

    first = own_start + (me - own_start) % n
    pos = first[:, :, None] + n * slot_ids
    live = pos < (own_start + own_len)[:, :, None]
    send = jnp.where(live, micros[:, None, None] * length + pos // n, -1)
    send = jnp.moveaxis(send, 0, 1)[:, None] + jnp.zeros((1, parts, 1, 1), i32)
    send = jnp.where(send >= 0, send + (part_ids * micro * length)[None, :, None, None], -1)
    rows_in = split_rows(inputs[:, 0].reshape(micro * length, width), parts).reshape(-1, thin)
    outgoing = picked(send.reshape(-1), rows_in).reshape(n, parts * per, thin)

    def row_of(v):
        return jnp.pad(v, ((0, 0), (0, share - v.shape[1])))

    packed = jnp.concatenate([
        query_conv, key_conv, value_conv, attn_gain[None], mlp_gain[None], row_of(out_gain[None]),
        jnp.zeros((1, share), BF16), beta_weight.T, jnp.zeros((SMALL_ROWS - 16 - HEADS, share), BF16),
    ])
    count = SMALL_ROWS * share // HEAD
    packed = jnp.pad(packed.reshape(count, HEAD), ((0, -count % 16), (0, 0)))

    attn_shard = jnp.concatenate([query_weight, key_weight, value_weight, out_weight.T], axis=1)
    steps = hidden_units // FFW
    feed_shard = jnp.stack(
        [w.reshape(share, steps, FFW) for w in (gate_weight, up_weight, down_weight.T)], axis=2
    ).reshape(share, 3 * hidden_units)

    plan = [(0, 0, HEAD, ZXY)]
    for a, (w, size) in enumerate(((4 * width, 512), (3 * hidden_units, 768)), 1):
        for at, wide in spans(w, size):
            plan.append((a, at, wide, (ZXY, ZYX)[len(plan) % 2]))
    small_all, attn_all, feed_all, incoming = gather_call_thin(
        [packed, attn_shard, feed_shard], outgoing, tuple(plan), 2, 1
    )
    small = small_all.reshape(n, -1)[:, : SMALL_ROWS * share].reshape(n, SMALL_ROWS, share)
    small = jnp.moveaxis(small, 1, 0)
    gain_row = small[ROW_OUT, :, : HEAD // n].reshape(1, HEAD)
    small = small.reshape(SMALL_ROWS, width).astype(F32)
    small = lax.dynamic_update_slice(small, gain_row.astype(F32), (ROW_OUT, 0))
    attn_all = attn_all.reshape(width, 4 * width)
    feed_all = feed_all.reshape(width, 3 * hidden_units)
    qkv, out_t = attn_all[:, : 3 * width], attn_all[:, 3 * width :]

    active = row_ids[None] < my_len[:, None]
    block = (my_start[:, None] + row_ids) % n
    at = block * (parts * per) + micros[:, None] * slots + row_ids // n
    take = jnp.where(active, at, -1).reshape(-1)
    flat = incoming.reshape(n * parts * per, thin)
    own = jnp.concatenate(
        [picked(jnp.where(take >= 0, take + p * per, -1), flat) for p in range(parts)], axis=1
    )
    active = active.reshape(-1, 1)
    grad = jnp.where(active, cotangent[:, 0].reshape(-1, width), jnp.zeros((), BF16))

    hidden, *saved = forward_call_thin(own, small, qkv, out_t, micro)
    result, feed_terms, d_hidden, mlp_gain_grad = feed_call_thin(
        hidden, grad, small, active.astype(F32), feed_all
    )
    d_own, qkv_terms, out_terms, small_terms = backward_call_thin(
        d_hidden, own, small, qkv, out_t, saved, micro
    )

    back = slot_ids * n + (devices[:, None, None] - my_start[None, :, None]) % n
    back = jnp.where(back < my_len[None, :, None], back + (micros * length)[None, :, None], -1)
    back = back[:, None] + jnp.zeros((1, parts, 1, 1), i32)
    back = jnp.where(back >= 0, back + (part_ids * micro * length)[None, :, None, None], -1)
    returning = picked(back.reshape(-1), split_rows(d_own, parts).reshape(-1, thin))
    returning = returning.reshape(n, parts * per, thin)

    small_terms = lax.dynamic_update_slice(small_terms, mlp_gain_grad, (ROW_MLP, 0))
    out_gain_terms = jnp.pad(small_terms[ROW_OUT, :HEAD].reshape(n, -1), ((0, 0), (0, share - HEAD // n)))
    small_terms = jnp.concatenate(
        [small_terms[:ROW_OUT].reshape(ROW_OUT, n, share), out_gain_terms[None],
         small_terms[ROW_OUT + 1 :].reshape(SMALL_ROWS - ROW_OUT - 1, n, share)]
    )
    small_terms = jnp.moveaxis(small_terms, 1, 0).reshape(n, count, HEAD)
    small_terms = jnp.pad(small_terms, ((0, 0), (0, -count % 16), (0, 0)))
    terms = [
        small_terms.reshape(dims + small_terms.shape[1:]),
        qkv_terms.reshape(dims + (share, 3 * width)),
        out_terms.reshape(dims + (share, width)),
        feed_terms.reshape(dims + (share, 3 * hidden_units)),
    ]
    plan = []
    for a, size in ((3, 768), (2, 512), (1, 512), (0, HEAD)):
        for lo, wide in spans(terms[a].shape[5], size):
            plan.append((a, lo, wide, (CXYZ, CYXZ)[len(plan) % 2]))
    small_grad, qkv_grad, out_grad, feed_grad, returned = scatter_call_thin(
        terms, returning, tuple(plan), 2, 2
    )

    place = row_ids * n + me
    inside = (place[None, :, None] >= own_start[:, None, :]) & (
        place[None, :, None] < (own_start + own_len)[:, None, :]
    )
    at = devices * (parts * per) + micros[:, None, None] * slots + (place[None, :, None] - first[:, None, :]) // n
    take = (jnp.sum(jnp.where(inside, at + 1, 0), axis=2) - 1).reshape(-1)
    flat = returned.reshape(n * parts * per, thin)
    input_rows = jnp.concatenate(
        [picked(jnp.where(take >= 0, take + p * per, -1), flat) for p in range(parts)], axis=1
    )

    small_grad = small_grad.reshape(-1)[: SMALL_ROWS * share].reshape(SMALL_ROWS, share)
    feed_grad = feed_grad.reshape(share, steps, 3, FFW)
    gate_grad, up_grad, down_grad = (
        feed_grad[:, :, i].reshape(share, hidden_units) for i in range(3)
    )
    return (
        result.reshape(micro, 1, length, width),
        input_rows.reshape(micro, 1, length, width),
        small_grad[ROW_ATTN],
        qkv_grad[:, :width],
        qkv_grad[:, width : 2 * width],
        qkv_grad[:, 2 * width :],
        small_grad[ROW_BETA : ROW_BETA + HEADS].T,
        small_grad[0:4],
        small_grad[4:8],
        small_grad[8:12],
        small_grad[ROW_OUT, : HEAD // n],
        out_grad.T,
        small_grad[ROW_MLP],
        gate_grad,
        up_grad,
        down_grad.T,
    )


def solution(mesh):
    rows, cols, flat = P("fsdp", None), P(None, "fsdp"), P("fsdp")
    data = P(None, "fsdp", None, None)
    return jax.shard_map(
        local,
        mesh=mesh,
        in_specs=(
            data, data, P(), P(), flat, rows, rows, rows, rows, cols, cols, cols, flat, cols, flat, rows, rows, cols,
        ),
        out_specs=(
            data, data, flat, rows, rows, rows, rows, cols, cols, cols, flat, cols, flat, rows, rows, cols,
        ),
        check_vma=False,
    )
```

```python
import functools
import math

import jax
import jax.numpy as jnp
from jax import lax
from jax.experimental import pallas as pl
from jax.experimental.pallas import tpu as pltpu
from jax.sharding import PartitionSpec as P

HEADS = 8
HEAD = 128
SPAN = 128
NORM_EPS = 1e-05
UNIT_EPS = 1e-06
MESH = pl.DeviceIdType.MESH
F32, BF16 = jnp.float32, jnp.bfloat16
VMEM_LIMIT = 62 * 1024 * 1024
FFW = 256
WIDE = 3 * FFW
HALF = WIDE // 2
Z, Y, X, C = 0, 1, 2, 3
ZXY, ZYX = (Z, X, Y, C), (Z, Y, X, C)
CXYZ, CYXZ = (C, X, Y, Z), (C, Y, X, Z)
GATHER_TICKS = (0, 2, 4, 6, 8)
SCATTER_TICKS = (0, 1, 3, 5, 7)
SLOTS = (4, 6, 6, 4)

ROW_CONV, ROW_ATTN, ROW_MLP, ROW_OUT, ROW_BETA, SMALL_ROWS = 0, 12, 13, 14, 16, 32


def grid_of(n):
    chips = n // 2
    a = 4 if chips % 4 == 0 else 1
    rest = chips // a
    b = 1
    while b * b < rest:
        b *= 2
    return (a, b, rest // b, 2)


def coords_of(dims, index):
    out = []
    for size in reversed(dims):
        out.append(lax.rem(index, size))
        index = index // size
    return out[::-1]


def index_of(dims, cs):
    total = 0
    for size, c in zip(dims, cs):
        total = total * size + c
    return total


def along(dims, cs, axis, delta):
    moved = list(cs)
    moved[axis] = lax.rem(cs[axis] + delta + dims[axis], dims[axis])
    return moved


def axis_peers(dims, cs):
    return [index_of(dims, along(dims, cs, a, d)) for a in range(4) for d in range(1, dims[a])]


def greet_all(n, me):
    barrier = pltpu.get_barrier_semaphore()

    def hello(d, carry):
        pl.semaphore_signal(
            barrier, inc=1, device_id=(lax.rem(me + d, n),), device_id_type=MESH
        )
        return carry

    lax.fori_loop(1, n, hello, 0)
    pl.semaphore_wait(barrier, n - 1)


def hops(dims):
    return sum(d - 1 for d in dims)


def guard(condition, act):
    if isinstance(condition, bool):
        if condition:
            act()
    else:
        pl.when(condition)(act)


def run_tick(segments, ticks, tick):
    for stage in reversed(range(len(ticks))):
        i = tick - ticks[stage]
        for make, first, end in segments:
            inside = (first <= i < end) if isinstance(i, int) else (i >= first) & (i < end)

            def act(make=make, i=i, stage=stage):
                for job in make(i):
                    job.step(stage)

            guard(inside, act)


class Gather:
    def __init__(self, dims, cs, shard, out, columns, order, sems):
        self.dims, self.cs, self.order, self.columns = dims, cs, order, columns
        self.shard, self.out = shard.at[:, columns], out
        self.send, self.recv, self.local = sems

    def slot(self, stage, delta):
        return sum(self.dims[a] - 1 for a in self.order[:stage]) + delta - 1

    def region(self, stage, cs):
        done = self.order[:stage]
        lead = tuple(slice(None) if k in done else cs[k] for k in range(4))
        return self.out.at[lead + (slice(None), self.columns)]

    def copies(self, stage, incoming):
        axis = self.order[stage]
        for delta in range(1, self.dims[axis]):
            frm = along(self.dims, self.cs, axis, -delta) if incoming else self.cs
            to = along(self.dims, self.cs, axis, delta)
            k = self.slot(stage, delta)
            yield pltpu.make_async_remote_copy(
                src_ref=self.shard if stage == 0 else self.region(stage, self.cs),
                dst_ref=self.region(stage, frm),
                send_sem=self.send.at[k],
                recv_sem=self.recv.at[k],
                device_id=(index_of(self.dims, to),),
                device_id_type=MESH,
            )

    def keep(self):
        return pltpu.make_async_copy(self.shard, self.region(0, self.cs), self.local)

    def step(self, stage):
        if stage == 0:
            self.keep().start()
        if stage == 1:
            self.keep().wait()
        if stage >= 1:
            for c in self.copies(stage - 1, True):
                c.wait_recv()
        if stage < 4:
            for c in self.copies(stage, False):
                c.start()

    def finish(self):
        for stage in range(4):
            for c in self.copies(stage, False):
                c.wait_send()


class Scatter:
    def __init__(self, dims, cs, terms, term_columns, result, columns, order, got, sems):
        self.dims, self.cs, self.order = dims, cs, order
        self.term_columns, self.columns = term_columns, columns
        self.terms, self.result, self.got = terms, result, got
        self.send, self.recv = sems

    def slot(self, stage, delta):
        return sum(self.dims[a] - 1 for a in self.order[:stage]) + delta - 1

    def part(self, stage, at):
        axis = self.order[stage]
        if stage == 0:
            lead = tuple(at if k == axis else slice(None) for k in range(4))
            return self.terms.at[lead + (slice(None), self.term_columns)]
        left = [k for k in range(4) if k not in self.order[:stage]]
        return self.got[stage - 1].at[(0,) + tuple(at if k == axis else slice(None) for k in left)]

    def copies(self, stage):
        axis = self.order[stage]
        for delta in range(1, self.dims[axis]):
            to = along(self.dims, self.cs, axis, delta)
            k = self.slot(stage, delta)
            yield pltpu.make_async_remote_copy(
                src_ref=self.part(stage, to[axis]),
                dst_ref=self.got[stage].at[delta - 1],
                send_sem=self.send.at[k],
                recv_sem=self.recv.at[k],
                device_id=(index_of(self.dims, to),),
                device_id_type=MESH,
            )

    def total(self, stage):
        axis = self.order[stage]
        left = [k for k in range(4) if k not in self.order[: stage + 1]]
        shape = [self.dims[k] for k in left]
        got = self.got[stage]
        mine = self.part(stage, self.cs[axis])

        def one(i, carry):
            at = tuple(coords_of(shape, i)) if shape else ()
            total = mine[at + (slice(None), slice(None))].astype(F32)
            for delta in range(1, self.dims[axis]):
                total += got[(delta - 1,) + at + (slice(None), slice(None))].astype(F32)
            if left:
                got[(0,) + at + (slice(None), slice(None))] = total.astype(got.dtype)
            else:
                self.result[:, self.columns] = total
            return carry

        lax.fori_loop(0, math.prod(shape), one, 0)

    def step(self, stage):
        if stage >= 1:
            for c in self.copies(stage - 1):
                c.wait()
            self.total(stage - 1)
        if stage < 4:
            for c in self.copies(stage):
                c.start()


def scatter_scratch(dims, rows, width, order, dtype, slots=None):
    out = []
    for s, axis in enumerate(order):
        rest = tuple(dims[k] for k in range(4) if k not in order[: s + 1])
        lead = () if slots is None else (slots[s],)
        out.append(pltpu.VMEM(lead + (dims[axis] - 1,) + rest + (rows, width), dtype))
    return out


class Tokens:
    def __init__(self, n, me, rows, a, b, send, recv, local):
        self.n, self.me, self.rows, self.a, self.b = n, me, rows, a, b
        self.send, self.recv, self.local = send, recv, local

    def block(self, d):
        return pl.ds(pl.multiple_of(d * self.rows, self.rows), self.rows)

    def copy(self, d, incoming):
        to = lax.rem(self.me + d, self.n)
        frm = lax.rem(self.me - d + self.n, self.n)
        return pltpu.make_async_remote_copy(
            src_ref=self.a.at[self.block(to)],
            dst_ref=self.b.at[self.block(frm if incoming else self.me)],
            send_sem=self.send.at[d],
            recv_sem=self.recv.at[d],
            device_id=(to,),
            device_id_type=MESH,
        )

    def keep(self):
        at = self.block(self.me)
        return pltpu.make_async_copy(self.a.at[at], self.b.at[at], self.local)

    def each(self, act):
        def body(d, carry):
            act(d)
            return carry

        lax.fori_loop(1, self.n, body, 0)

    def start(self):
        self.keep().start()
        self.each(lambda d: self.copy(d, False).start())

    def wait(self):
        self.keep().wait()
        self.each(lambda d: self.copy(d, True).wait_recv())
        self.each(lambda d: self.copy(d, False).wait_send())


def any_spec():
    return pl.BlockSpec(memory_space=pl.ANY)


def vmem_spec():
    return pl.BlockSpec(memory_space=pltpu.VMEM)


def dot(a, b):
    return lax.dot_general(a, b, (((1,), (0,)), ((), ())), preferred_element_type=F32)


def dot_nt(a, b):
    return lax.dot_general(a, b, (((1,), (1,)), ((), ())), preferred_element_type=F32)


def dot_tn(a, b):
    return lax.dot_general(a, b, (((0,), (0,)), ((), ())), preferred_element_type=F32)


def low(v):
    return v.astype(BF16)


def lanes(i, width=HEAD):
    return slice(i * width, (i + 1) * width)


def place(kind, h):
    at = (h // 2) * WIDE + kind * 2 * HEAD + (h % 2) * HEAD
    return slice(at, at + HEAD)


def shifted(values, by, row):
    if by == 0:
        return values
    rows = values.shape[0]
    moved = pltpu.roll(values, by % rows, 0)
    return jnp.where(row >= by if by > 0 else row < rows + by, moved, 0.0)


def head_sum(values):
    return jnp.sum(values, axis=-1, keepdims=True)


def rms(v):
    return lax.rsqrt(jnp.mean(v * v, axis=-1, keepdims=True) + NORM_EPS)


def rms_back(d, v, r, gain):
    vr, gd = v * r, d * gain
    return r * (gd - vr * jnp.mean(vr * gd, axis=-1, keepdims=True)), d * vr


def iotas(shape):
    return lax.broadcasted_iota(jnp.int32, shape, 0), lax.broadcasted_iota(jnp.int32, shape, 1)


def level_masks():
    i, j = iotas((SPAN, SPAN))
    found = []
    for level in range(SPAN.bit_length() - 1):
        a, b = i >> level, j >> level
        found.append(((a >> 1) == (b >> 1)) & ((a & 1) == 1) & ((b & 1) == 0))
    return found


def column(row):
    return jnp.broadcast_to(row, (HEAD, HEAD)).T


def hot(index, count):
    lane = lax.broadcasted_iota(jnp.int32, (HEAD, HEAD), 1).astype(F32)
    return jnp.concatenate(
        [low(jnp.where(lane + float(HEAD * b) == index, 1.0, 0.0)) for b in range(count // HEAD)], axis=1
    )


def prepare(x, taps, unit, row):
    c = x * taps[0:1]
    for o in range(1, taps.shape[0]):
        c += shifted(x, o, row) * taps[o : o + 1]
    u = c * jax.nn.sigmoid(c)
    if unit:
        u = jnp.concatenate(
            [
                u[:, lanes(h)] * lax.rsqrt(head_sum(u[:, lanes(h)] * u[:, lanes(h)]) + UNIT_EPS)
                for h in range(x.shape[1] // HEAD)
            ],
            axis=1,
        )
    return u


def prepare_back(x, d, taps, unit, row):
    moved = [shifted(x, o, row) for o in range(taps.shape[0])]
    c = moved[0] * taps[0:1]
    for o in range(1, taps.shape[0]):
        c += moved[o] * taps[o : o + 1]
    s = jax.nn.sigmoid(c)
    u = c * s
    if unit:
        n = lax.rsqrt(head_sum(u * u) + UNIT_EPS)
        un = u * n
        d = (d - un * head_sum(un * d)) * n
    d = d * (s + u * (1.0 - s))
    grads = [jnp.sum(m * d, axis=0, keepdims=True) for m in moved]
    back = d * taps[0:1]
    for o in range(1, taps.shape[0]):
        back += shifted(d, -o, row) * taps[o : o + 1]
    return back, grads


def delta_block(base, first, refs, gain):
    qkv, beta, state, states, inverses, scores, fresh, mix, mixed, at = refs
    rows = pl.ds(base, SPAN)
    i, j = iotas((SPAN, SPAN))
    masks = level_masks()
    eye = jnp.where(i == j, 1.0, 0.0).astype(F32)
    heads = range(HEADS)

    @pl.when(first)
    def _():
        state[...] = jnp.zeros_like(state)

    strength = beta[rows, :]
    q, k = ([qkv[rows, place(kind, h)] for h in heads] for kind in range(2))
    b = [strength[:, h : h + 1] for h in heads]
    strict = [low(jnp.where(i > j, dot_nt(k[h], k[h]) * b[h], 0.0)) for h in heads]
    for h in heads:
        scores[at, h] = low(jnp.where(i >= j, dot_nt(q[h], k[h]), 0.0))
    zero = jnp.zeros((), BF16)
    inv = [eye - jnp.where(masks[0], strict[h], zero).astype(F32) for h in heads]
    for level in range(1, len(masks)):
        t = [low(inv[h]) for h in heads]
        f = [low(dot(jnp.where(masks[level], strict[h], zero), t[h])) for h in heads]
        inv = [inv[h] - dot(t[h], f[h]) for h in heads]
    for h in heads:
        inverses[at, h] = low(inv[h])
    s = [low(state[h]) for h in heads]
    for h in heads:
        states[at, h] = s[h]
    rest = [low((qkv[rows, place(2, h)].astype(F32) - dot(k[h], s[h])) * b[h]) for h in heads]
    new = [low(dot(inverses[at, h], rest[h])) for h in heads]
    out = [dot(q[h], s[h]) + dot(scores[at, h], new[h]) for h in heads]
    for h in heads:
        fresh[rows, lanes(h)] = new[h]
        state[h] += dot_tn(k[h], new[h])
        mix[rows, lanes(h)] = low(out[h])
        mixed[rows, lanes(h)] = low(out[h] * rms(out[h]) * gain)


def delta_back(base, last, refs, gain):
    (qkv, beta, states, inverses, scores, fresh, mix, d_mixed,
     d_state, d_q, d_k, d_v, d_beta, gain_grad, at) = refs
    rows = pl.ds(base, SPAN)
    i, j = iotas((SPAN, SPAN))
    lane = lax.broadcasted_iota(jnp.int32, (SPAN, 16), 1)
    heads = range(HEADS)

    @pl.when(last)
    def _():
        d_state[...] = jnp.zeros_like(d_state)

    strength = beta[rows, :]
    q, k = ([qkv[rows, place(kind, h)] for h in heads] for kind in range(2))
    e = [fresh[rows, lanes(h)] for h in heads]
    b = [strength[:, h : h + 1] for h in heads]
    kb = [low(k[h].astype(F32) * b[h]) for h in heads]
    do = []
    for h in heads:
        v = mix[rows, lanes(h)].astype(F32)
        d, terms = rms_back(d_mixed[:, lanes(h)], v, rms(v), gain)
        gain_grad[...] += jnp.sum(terms, axis=0, keepdims=True)
        do.append(low(d))
    s = [states[at, h] for h in heads]
    p = [scores[at, h] for h in heads]
    ds = [low(d_state[h]) for h in heads]
    de = [low(dot_tn(p[h], do[h]) + dot(k[h], ds[h])) for h in heads]
    dx = [dot_tn(inverses[at, h], de[h]) for h in heads]
    dxl = [low(dx[h]) for h in heads]
    dp = [low(jnp.where(i >= j, dot_nt(do[h], e[h]), 0.0)) for h in heads]
    da = [low(jnp.where(i > j, -dot_nt(dxl[h], e[h]), 0.0)) for h in heads]
    dkb = [dot(da[h], k[h]) - dot_nt(dxl[h], s[h]) for h in heads]
    beta_grad = jnp.zeros((SPAN, 16), F32)
    for h in heads:
        d_q[rows, lanes(h)] = dot_nt(do[h], s[h]) + dot(dp[h], k[h])
        d_k[rows, lanes(h)] = (
            dkb[h] * b[h] + dot_tn(da[h], kb[h]) + dot_tn(dp[h], q[h]) + dot_nt(e[h], ds[h])
        )
        d_v[rows, lanes(h)] = low(dx[h] * b[h])
        d_state[h] += dot_tn(q[h], do[h]) - dot_tn(kb[h], dxl[h])
        v = qkv[rows, place(2, h)].astype(F32)
        db = head_sum(dkb[h] * k[h].astype(F32) + dx[h] * v)
        beta_grad += jnp.where(lane == h, db, 0.0)
    d_beta[rows, :] = low(beta_grad * strength * (1.0 - strength))


def block_kernel(dims, micro, length, steps, token_rows, *refs):
    (tokens_in, take, back, grad_in, small_shard, qkv_shard, out_shard, feed_shard,
     result, returned, feed_grad, qkv_grad, out_grad, small_grad,
     small_all, qkv_all, out_all, feed_all,
     own, attn_low, pre, qkv, beta, states, inverses, scores, fresh, mix, mixed,
     hidden, total, d_hidden, norm, grad, bufs, w_out, state, d_out, tok_buf, small_buf, small, small_terms,
     gain_out, d_beta, small_out,
     g_send, g_recv, g_local, s_send, s_recv, t_send, t_recv, t_local, load_sem, ready, *got) = refs
    n = math.prod(dims)
    me = lax.axis_index("fsdp")
    cs = coords_of(dims, me)
    width = own.shape[1]
    share = width // n
    thin = tok_buf.shape[2]
    parts = width // thin
    slots = token_rows // parts
    pieces = 3 * width // WIDE
    blocks = length // SPAN
    rows_total = micro * length
    flat = dims + (share,)

    def g_sems(i):
        return g_send.at[i], g_recv.at[i], g_local.at[i]

    def s_sems(i):
        return s_send.at[i], s_recv.at[i]

    def feed_columns(i, p=0, wide=WIDE):
        return pl.ds(pl.multiple_of(i * WIDE + p * HALF, HALF), wide)

    def feed_gather(i):
        for p, order in enumerate((ZXY, ZYX)):
            yield Gather(dims, cs, feed_shard, feed_all, feed_columns(i, p, HALF), order, g_sems(2 * i + p))

    first_gather = 2 * steps
    attn_gather = [Gather(dims, cs, small_shard, small_all, pl.ds(0, HEAD), ZXY, g_sems(first_gather))]
    for i in range(2 * pieces):
        attn_gather.append(Gather(
            dims, cs, qkv_shard, qkv_all, pl.ds(i * HALF, HALF), (ZXY, ZYX)[i % 2],
            g_sems(first_gather + 1 + i),
        ))
    half_out = width // 2
    out_gather = [
        Gather(dims, cs, out_shard, out_all, pl.ds(i * half_out, half_out), (ZXY, ZYX)[i],
               g_sems(first_gather + 1 + 2 * pieces + i))
        for i in range(2)
    ]
    gathers = [(feed_gather, 0, steps)]

    def slot_views(i, p, wide):
        for s in range(4):
            ref = got[4 * p + s]
            lead = (lax.rem(i, SLOTS[s]),) + (slice(None),) * (len(ref.shape) - 2)
            yield ref.at[lead + (pl.ds(0, wide),)]

    def scatter(i, source, source_at, target, at, wide, sem):
        for p, order in enumerate((CXYZ, CYXZ)):
            yield Scatter(
                dims, cs, source, pl.ds(source_at + p * wide, wide), target,
                pl.ds(pl.multiple_of(at + p * wide, HEAD), wide), order,
                list(slot_views(i, p, wide)), s_sems(sem + p),
            )

    def feed_scatter(i):
        return scatter(i, bufs.at[lax.rem(i, 2)], 0, feed_grad, i * WIDE, HALF, 2 * i)

    rest = width - WIDE
    first_out = 2 * steps

    def out_scatter(i):
        return scatter(steps, bufs.at[steps % 2], 0, out_grad, 0, HALF, first_out)

    def out_scatter_rest(i):
        return scatter(steps + 1, bufs.at[(steps + 1) % 2], 0, out_grad, WIDE, rest // 2, first_out + 2)

    scatters = [
        (feed_scatter, 0, steps), (out_scatter, steps, steps + 1), (out_scatter_rest, steps + 1, steps + 2)
    ]
    first_qkv = first_out + 4

    def qkv_scatter(i):
        yield from scatter(i, bufs.at[i], 0, qkv_grad, i * WIDE, HALF, first_qkv + 2 * i)

    def small_scatter(i):
        yield Scatter(
            dims, cs, small_out, pl.ds(0, HEAD), small_grad, pl.ds(0, HEAD), CXYZ, got[8:12],
            s_sems(first_qkv + 2 * pieces),
        )

    tail_scatters = [(qkv_scatter, 0, pieces), (small_scatter, pieces, pieces + 1)]

    def tokens_to(m):
        return Tokens(n, me, token_rows, tokens_in.at[m], tok_buf.at[m], t_send.at[m], t_recv.at[m], t_local.at[m])

    def tokens_back(m):
        k = micro + m
        return Tokens(n, me, token_rows, tok_buf.at[m], returned.at[m], t_send.at[k], t_recv.at[k], t_local.at[k])

    def load_qkv(i):
        return pltpu.make_async_copy(
            qkv_all.at[:, :, :, :, :, pl.ds(i * WIDE, WIDE)], bufs.at[i], load_sem.at[i]
        )

    load_out = pltpu.make_async_copy(out_all, w_out, load_sem.at[pieces])
    load_small = pltpu.make_async_copy(small_all, small_buf, load_sem.at[pieces + 1])
    load_grad = pltpu.make_async_copy(grad_in, grad, load_sem.at[pieces + 2])
    store_result = pltpu.make_async_copy(grad, result, load_sem.at[pieces + 2])

    def load_feed(t):
        slot = lax.rem(t, 2)
        return pltpu.make_async_copy(
            feed_all.at[:, :, :, :, :, feed_columns(t)], bufs.at[2 + slot], load_sem.at[pieces + 3 + slot]
        )

    load_grad.start()
    greet_all(n, me)
    tokens_to(0).start()
    segment = [(lambda i: [attn_gather[i]], 0, len(attn_gather))]
    last = len(attn_gather) + GATHER_TICKS[-1]
    early = 0
    for t in range(last):
        run_tick(segment, GATHER_TICKS, t)
        if t == len(attn_gather) - 1:
            for m in range(1, micro):
                tokens_to(m).start()
        if t >= len(attn_gather) and (last - 1 - t) % 2 == 0 and early < EARLY:
            run_tick(gathers, GATHER_TICKS, early)
            early += 1
        if t == GATHER_TICKS[-1]:
            load_small.start()
        for i in range(pieces):
            if t == 2 * i + 2 + GATHER_TICKS[-1]:
                load_qkv(i).start()
    load_small.wait()
    blockwise = small_buf[...].reshape(width, HEAD).astype(F32)
    small[...] = blockwise.T[:SMALL_ROWS]
    i, j = iotas((width, HEAD))
    few = HEAD // n
    mine = (lax.rem(i, share) < few) & ((i // share) * few + lax.rem(i, share) == j)
    gain_out[...] = jnp.sum(
        jnp.where(mine, blockwise[:, ROW_OUT : ROW_OUT + 1], 0.0), axis=0, keepdims=True
    )
    for i in range(pieces):
        load_qkv(i).wait()

    gain_attn = small[ROW_ATTN : ROW_ATTN + 1, :]
    gain_mlp = small[ROW_MLP : ROW_MLP + 1, :]
    beta_rows = low(small[ROW_BETA : ROW_BETA + 16, :])
    row2 = lax.broadcasted_iota(jnp.int32, (length, 2 * HEAD), 0)
    row1 = lax.broadcasted_iota(jnp.int32, (length, HEAD), 0)

    def project(m, carry):
        run_tick(gathers, GATHER_TICKS, early + m)
        tokens_to(m).wait()

        def arrive(t, carry):
            at = pl.ds(pl.multiple_of(t * SPAN, SPAN), SPAN)
            index = column(take[pl.ds(t, 1), :])
            for p in range(parts):
                cols = lanes(p, thin)
                pick = hot(jnp.where(index >= 0.0, index + float(p * slots), -1.0), n * token_rows)
                own[at, cols] = low(dot(pick, tok_buf[m]))
            v = own[at, :].astype(F32)
            attn_low[at, :] = low(v * rms(v) * gain_attn)
            return carry

        lax.fori_loop(m * blocks, (m + 1) * blocks, arrive, 0)
        rows = pl.ds(pl.multiple_of(m * length, SPAN), length)
        a = attn_low[rows, :]
        beta[rows, :] = jax.nn.sigmoid(dot_nt(a, beta_rows))
        for b in range(pieces):
            for kind in range(3):
                cols = lanes(kind, 2 * HEAD)
                wide = slice(b * WIDE + cols.start, b * WIDE + cols.stop)
                x = dot(a, bufs[b, :, :, :, :, :, cols].reshape(width, 2 * HEAD))
                pre[rows, wide] = low(x)
                taps = small[4 * kind : 4 * kind + 4, lanes(b, 2 * HEAD)]
                qkv[rows, wide] = low(prepare(x, taps, kind < 2, row2))
        return carry

    lax.fori_loop(0, micro, project, 0)

    def forward(t, carry):
        run_tick(gathers, GATHER_TICKS, early + micro + t)
        for s in range(5):

            @pl.when(t == s)
            def _(s=s):
                for g in out_gather:
                    g.step(s)

        base = pl.multiple_of(t * SPAN, SPAN)
        delta_block(
            base, lax.rem(t, blocks) == 0,
            (qkv, beta, state, states, inverses, scores, fresh, mix, mixed, t), gain_out[...],
        )
        return carry

    lax.fori_loop(0, micro * blocks, forward, 0)
    load_out.start()
    begun = early + micro + micro * blocks
    load_feed(0).start()
    load_out.wait()

    def enter(t, carry):
        at = pl.ds(pl.multiple_of(t * SPAN, SPAN), SPAN)
        v = own[at, :].astype(F32) + dot_nt(mixed[at, :], w_out[...].reshape(width, width))
        hidden[at, :] = v
        norm[at, :] = low(v * rms(v) * gain_mlp)
        return carry

    lax.fori_loop(0, micro * blocks, enter, 0)
    load_grad.wait()
    total[...] = jnp.zeros_like(total)
    d_hidden[...] = jnp.zeros_like(d_hidden)

    def feed(t, carry):
        run_tick(gathers, GATHER_TICKS, begun + t)

        @pl.when(t + 1 < steps)
        def _():
            load_feed(t + 1).start()

        load_feed(t).wait()
        w = bufs.at[2 + lax.rem(t, 2)]
        terms = bufs.at[lax.rem(t, 2)]
        gw, uw, dw = (w[:, :, :, :, :, lanes(i, FFW)].reshape(width, FFW) for i in range(3))
        x, g = norm[...], grad[...]
        gate, up = dot(x, gw), dot(x, uw)
        d_act = dot(g, dw)
        s = jax.nn.sigmoid(gate)
        silu = gate * s
        act = low(silu * up)
        d_gate = low(d_act * up * (s + silu * (1.0 - s)))
        d_up = low(d_act * silu)
        for b in range(width // FFW):
            cols = lanes(b, FFW)
            total[:, cols] += dot_nt(act, dw[cols])
            d_hidden[:, cols] += dot_nt(d_gate, gw[cols]) + dot_nt(d_up, uw[cols])
        for i, (left, right) in enumerate(((x, d_gate), (x, d_up), (g, act))):
            terms[:, :, :, :, :, lanes(i, FFW)] = low(dot_tn(left, right)).reshape(flat + (FFW,))
        run_tick(scatters, SCATTER_TICKS, t)
        return carry

    lax.fori_loop(0, steps, feed, 0)
    small_terms[...] = jnp.zeros_like(small_terms)

    def leave(t, carry):
        at = pl.ds(pl.multiple_of(t * SPAN, SPAN), SPAN)
        v, g = hidden[at, :], grad[at, :].astype(F32)
        grad[at, :] = low(v + total[at, :])
        d, terms = rms_back(d_hidden[at, :], v, rms(v), gain_mlp)
        small_terms[ROW_MLP : ROW_MLP + 1, :] += jnp.sum(terms, axis=0, keepdims=True)
        d_hidden[at, :] = g + d
        norm[at, :] = low(g + d)
        return carry

    lax.fori_loop(0, micro * blocks, leave, 0)
    store_result.start()
    d_attn = d_v = norm

    for b in range(width // 256):
        slot, at = (steps + b * 256 // WIDE) % 2, b * 256 % WIDE
        grads = low(dot_tn(d_attn[...], mixed[:, lanes(b, 256)]))
        bufs[slot, :, :, :, :, :, at : at + 256] = grads.reshape(flat + (256,))
        if b == WIDE // 256 - 1:
            run_tick(scatters, SCATTER_TICKS, steps)
    run_tick(scatters, SCATTER_TICKS, steps + 1)
    d_q, d_k = hidden, total
    begun_back = steps + 2

    def backward(turn, carry):
        m = micro - 1 - turn

        def one(b, carry):
            run_tick(scatters, SCATTER_TICKS, begun_back + turn * (blocks + 1) + b)
            t = m * blocks + blocks - 1 - b
            base = pl.multiple_of(t * SPAN, SPAN)
            d_out[...] = dot(d_attn[pl.ds(base, SPAN), :], w_out[...].reshape(width, width))
            delta_back(
                base, b == 0,
                (qkv, beta, states, inverses, scores, fresh, mix, d_out,
                 state, d_q, d_k, d_v, d_beta, small_terms.at[ROW_OUT : ROW_OUT + 1, 0:HEAD], t),
                gain_out[...],
            )
            return carry

        lax.fori_loop(0, blocks, one, 0)
        run_tick(scatters, SCATTER_TICKS, begun_back + turn * (blocks + 1) + blocks)

        @pl.when(turn == 0)
        def _():
            for i in range(pieces):
                load_qkv(i).start()

        rows = pl.ds(pl.multiple_of(m * length, SPAN), length)
        for kind, grads in enumerate((d_q, d_k, d_v)):
            for h in range(HEADS):
                at = place(kind, h)
                back_rows, taps = prepare_back(
                    pre[rows, at].astype(F32), grads[rows, lanes(h)].astype(F32),
                    small[4 * kind : 4 * kind + 4, lanes(h)], kind < 2, row1,
                )
                qkv[rows, at] = low(back_rows)
                for o, terms in enumerate(taps):
                    small_terms[4 * kind + o : 4 * kind + o + 1, lanes(h)] += terms

        @pl.when(turn == 0)
        def _():
            for i in range(pieces):
                load_qkv(i).wait()

        def depart(b, carry):
            at = pl.ds(pl.multiple_of(m * length + b * SPAN, SPAN), SPAN)
            d = dot(d_beta[at, :], beta_rows)
            for i in range(pieces):
                d += dot_nt(qkv[at, lanes(i, WIDE)], bufs[i].reshape(width, WIDE))
            v = own[at, :].astype(F32)
            d, terms = rms_back(d, v, rms(v), gain_attn)
            small_terms[ROW_ATTN : ROW_ATTN + 1, :] += jnp.sum(terms, axis=0, keepdims=True)
            own[at, :] = low(d_hidden[at, :] + d)
            return carry

        lax.fori_loop(0, blocks, depart, 0)
        line = lax.broadcasted_iota(jnp.int32, (HEAD, length), 0)

        def pack(b, carry):
            pick = hot(column(back[pl.ds(m * (n * token_rows // HEAD) + b, 1), :]), length)
            part = lax.rem(line + b * HEAD, token_rows) // slots
            held = jnp.zeros((HEAD, thin), F32)
            for p in range(parts):
                held += dot(jnp.where(part == p, pick, jnp.zeros((), BF16)), own[rows, lanes(p, thin)])
            tok_buf[m, pl.ds(pl.multiple_of(b * HEAD, HEAD), HEAD), :] = low(held)
            return carry

        lax.fori_loop(0, n * token_rows // HEAD, pack, 0)
        tokens_back(m).start()
        return carry

    lax.fori_loop(0, micro, backward, 0)

    for peer in axis_peers(dims, cs):
        pl.semaphore_signal(ready, inc=1, device_id=(peer,), device_id_type=MESH)
    for i in range(pieces):
        for kind in range(3):
            cols = lanes(kind, FFW)
            grads = low(dot_tn(attn_low[...], qkv[:, i * WIDE + cols.start : i * WIDE + cols.stop]))
            bufs[i, :, :, :, :, :, cols] = grads.reshape(flat + (FFW,))
        if i == 0:
            pl.semaphore_wait(ready, hops(dims))
        run_tick(tail_scatters, SCATTER_TICKS, i)
    i, j = iotas((HEAD, width))
    mine = (lax.rem(j, share) < few) & ((j // share) * few + lax.rem(j, share) == i)
    gain_column = column(small_terms[ROW_OUT : ROW_OUT + 1, :HEAD])[:, 0:1]
    gain_row = jnp.sum(jnp.where(mine, gain_column, 0.0), axis=0, keepdims=True)
    block = jnp.concatenate(
        [small_terms[:ROW_OUT, :], gain_row, jnp.zeros((1, width), F32),
         dot_tn(d_beta[...], attn_low[...]), jnp.zeros((HEAD - SMALL_ROWS, width), F32)], axis=0,
    )
    small_out[...] = block.T.reshape(flat + (HEAD,))
    for t in range(pieces, pieces + 1 + SCATTER_TICKS[-1]):
        run_tick(tail_scatters, SCATTER_TICKS, t)
    for g in attn_gather + out_gather:
        g.finish()

    def finish(i, carry):
        for g in feed_gather(i):
            g.finish()
        return carry

    lax.fori_loop(0, steps, finish, 0)
    store_result.wait()
    for m in range(micro):
        tokens_back(m).wait()


EARLY = 3


def block_call(tokens, take, back, grad, small_shard, qkv_shard, out_shard, feed_shard, micro):
    rows, width = grad.shape
    length, blocks = rows // micro, rows // SPAN
    n = lax.axis_size("fsdp")
    dims = grid_of(n)
    k = hops(dims)
    share = width // n
    steps = feed_shard.shape[1] // WIDE
    pieces = 3 * width // WIDE
    token_rows = tokens.shape[1] // n
    flat = dims + (share,)
    shape = jax.ShapeDtypeStruct
    outs = [
        shape((rows, width), BF16), shape(tokens.shape, BF16),
        shape(feed_shard.shape, F32), shape(qkv_shard.shape, F32), shape(out_shard.shape, F32), shape((share, HEAD), F32),
        shape(dims + small_shard.shape, BF16), shape(dims + qkv_shard.shape, BF16), shape(dims + out_shard.shape, BF16),
        shape(dims + feed_shard.shape, BF16),
    ]
    wide, full = pltpu.VMEM((rows, width), BF16), pltpu.VMEM((rows, width), F32)
    square = pltpu.VMEM((blocks, HEADS, SPAN, SPAN), BF16)
    gathers = 2 * steps + 1 + 2 * pieces + 2
    scatters = 2 * steps + 4 + 2 * pieces + 1
    dma = pltpu.SemaphoreType.DMA
    scratch = [
        wide, wide, pltpu.VMEM((rows, 3 * width), BF16), pltpu.VMEM((rows, 3 * width), BF16),
        pltpu.VMEM((rows, 16), F32), pltpu.VMEM((blocks, HEADS, HEAD, HEAD), BF16), square, square, wide, wide, wide,
        full, full, full, wide, wide, pltpu.VMEM((pieces,) + flat + (WIDE,), BF16), pltpu.VMEM(flat + (width,), BF16),
        pltpu.VMEM((HEADS, HEAD, HEAD), F32), pltpu.VMEM((SPAN, width), F32), pltpu.VMEM(tokens.shape, BF16),
        pltpu.VMEM(flat + (HEAD,), BF16), pltpu.VMEM((SMALL_ROWS, width), F32), pltpu.VMEM((SMALL_ROWS // 2, width), F32),
        pltpu.VMEM((1, HEAD), F32), pltpu.VMEM((rows, 16), BF16),
        pltpu.VMEM(flat + (HEAD,), F32),
        dma((gathers, k)), dma((gathers, k)), dma((gathers,)), dma((scatters, k)), dma((scatters, k)),
        dma((2 * micro, n)), dma((2 * micro, n)), dma((2 * micro,)), dma((pieces + 5,)), pltpu.SemaphoreType.REGULAR,
    ]
    for order in (CXYZ, CYXZ):
        scratch += scatter_scratch(dims, share, HALF, order, BF16, SLOTS)
    scratch += scatter_scratch(dims, share, HEAD, CXYZ, F32)
    return pl.pallas_call(
        functools.partial(block_kernel, dims, micro, length, steps, token_rows),
        out_shape=outs,
        in_specs=[any_spec(), vmem_spec(), vmem_spec()] + [any_spec()] * 5,
        out_specs=[any_spec()] * 2 + [vmem_spec()] * 4 + [any_spec()] * 4,
        scratch_shapes=scratch,
        compiler_params=pltpu.CompilerParams(
            collective_id=1, has_side_effects=True, vmem_limit_bytes=VMEM_LIMIT
        ),
    )(tokens, take, back, grad, small_shard, qkv_shard, out_shard, feed_shard)[:6]


def picked(index, source):
    hot_rows = index[:, None] == jnp.arange(source.shape[0], dtype=jnp.int32)[None, :]
    return jnp.dot(low(hot_rows), source, preferred_element_type=F32).astype(BF16)


def split_rows(values, parts):
    cut = values.reshape(values.shape[:-1] + (parts, values.shape[-1] // parts))
    return jnp.moveaxis(cut, -2, 0)


def spans(width, size):
    at = 0
    while at < width:
        yield at, min(size, width - at)
        at += size


def local(
    inputs, cotangent, lengths, owners, attn_gain, query_weight, key_weight, value_weight, beta_weight,
    query_conv, key_conv, value_conv, out_gain, out_weight, mlp_gain, gate_weight, up_weight, down_weight,
):
    n = lax.axis_size("fsdp")
    me = lax.axis_index("fsdp")
    micro, _, length, width = inputs.shape
    hidden_units = gate_weight.shape[1]
    share = width // n
    if share % 16:
        return local_thin(
            inputs, cotangent, lengths, owners, attn_gain, query_weight, key_weight, value_weight, beta_weight,
            query_conv, key_conv, value_conv, out_gain, out_weight, mlp_gain, gate_weight, up_weight, down_weight,
        )
    slots = length // n
    parts = 16 // math.gcd(slots, 16)
    thin = width // parts
    token_rows = parts * slots
    i32 = jnp.int32
    devices = jnp.arange(n, dtype=i32)
    slot_ids = jnp.arange(slots, dtype=i32)
    row_ids = jnp.arange(length, dtype=i32)
    part_ids = jnp.arange(parts, dtype=i32)

    before = devices[:, None] < devices[None, :]
    starts = jnp.sum(jnp.where(before[None], lengths[:, :, None], 0), axis=1)
    match = owners[:, None, :] == devices[None, :, None]
    own_start = jnp.sum(jnp.where(match, starts[:, None, :], 0), axis=2)
    own_len = jnp.sum(jnp.where(match, lengths[:, None, :], 0), axis=2)
    mine = devices == me
    my_start = jnp.sum(jnp.where(mine, own_start, 0), axis=1)
    my_len = jnp.sum(jnp.where(mine, own_len, 0), axis=1)

    first = own_start + (me - own_start) % n
    pos = first[:, :, None] + n * slot_ids
    live = pos < (own_start + own_len)[:, :, None]
    send = jnp.where(live, pos // n, -1)[:, :, None, :]
    send = jnp.where(send >= 0, send + (part_ids * length)[:, None], -1)
    outgoing = jnp.stack(
        [picked(send[m].reshape(-1), split_rows(inputs[m, 0], parts).reshape(-1, thin)) for m in range(micro)]
    )

    active = row_ids[None] < my_len[:, None]
    block = (my_start[:, None] + row_ids) % n
    take = jnp.where(active, block * token_rows + row_ids // n, -1).astype(F32).reshape(-1, HEAD)
    grad = jnp.where(active.reshape(-1, 1), cotangent[:, 0].reshape(-1, width), jnp.zeros((), BF16))

    back = slot_ids * n + (devices[:, None] - my_start[:, None, None]) % n
    back = jnp.where(back < my_len[:, None, None], back, -1)[:, :, None, :]
    back = (back + jnp.zeros((parts, 1), i32)).astype(F32).reshape(-1, HEAD)

    def fill(v):
        return jnp.pad(v, ((0, 0), (0, share - v.shape[1])))

    small_shard = jnp.concatenate([
        query_conv, key_conv, value_conv, attn_gain[None], mlp_gain[None], fill(out_gain[None]),
        jnp.zeros((1, share), BF16), beta_weight.T, jnp.zeros((HEAD - 16 - HEADS, share), BF16),
    ]).T
    pieces = width // (2 * HEAD)
    qkv_shard = jnp.stack(
        [w.reshape(share, pieces, 2 * HEAD) for w in (query_weight, key_weight, value_weight)], axis=2
    ).reshape(share, 3 * width)
    steps = hidden_units // FFW
    feed_shard = jnp.stack(
        [w.reshape(share, steps, FFW) for w in (gate_weight, up_weight, down_weight.T)], axis=2
    ).reshape(share, 3 * hidden_units)

    result, returned, feed_grad, qkv_grad, out_grad, small_grad = block_call(
        outgoing, take, back, grad, small_shard, qkv_shard, out_weight.T, feed_shard, micro
    )
    result = jnp.where(active.reshape(-1, 1), result, jnp.zeros((), BF16))

    at_row = row_ids * n + me
    inside = (at_row[None, :, None] >= own_start[:, None, :]) & (
        at_row[None, :, None] < (own_start + own_len)[:, None, :]
    )
    at = devices * token_rows + (at_row[None, :, None] - first[:, None, :]) // n
    put = jnp.sum(jnp.where(inside, at + 1, 0), axis=2) - 1
    input_rows = jnp.stack([
        jnp.concatenate(
            [picked(jnp.where(put[m] >= 0, put[m] + p * slots, -1), returned[m]) for p in range(parts)], axis=1
        )
        for m in range(micro)
    ])

    small_grad = small_grad.T
    feed_grad = feed_grad.reshape(share, steps, 3, FFW)
    gate_grad, up_grad, down_grad = (
        feed_grad[:, :, i].reshape(share, hidden_units) for i in range(3)
    )
    qkv_grad = qkv_grad.reshape(share, pieces, 3, 2 * HEAD)
    query_grad, key_grad, value_grad = (qkv_grad[:, :, i].reshape(share, width) for i in range(3))
    return (
        result.reshape(micro, 1, length, width),
        input_rows.reshape(micro, 1, length, width),
        small_grad[ROW_ATTN],
        query_grad,
        key_grad,
        value_grad,
        small_grad[ROW_BETA : ROW_BETA + HEADS].T,
        small_grad[0:4],
        small_grad[4:8],
        small_grad[8:12],
        small_grad[ROW_OUT, : HEAD // n],
        out_grad.T,
        small_grad[ROW_MLP],
        gate_grad,
        up_grad,
        down_grad.T,
    )


class GatherThin:
    def __init__(self, dims, cs, shard, out, low, width, order, sems):
        self.dims, self.cs, self.order = dims, cs, order
        self.columns = pl.ds(low, width)
        self.shard, self.out = shard.at[:, self.columns], out
        self.send, self.recv, self.local_thin = sems

    def slot(self, stage, delta):
        return sum(self.dims[a] - 1 for a in self.order[:stage]) + delta - 1

    def region(self, stage, cs):
        done = self.order[:stage]
        lead = tuple(slice(None) if k in done else cs[k] for k in range(4))
        return self.out.at[lead + (slice(None), self.columns)]

    def copies(self, stage, incoming):
        axis = self.order[stage]
        for delta in range(1, self.dims[axis]):
            frm = along(self.dims, self.cs, axis, -delta) if incoming else self.cs
            to = along(self.dims, self.cs, axis, delta)
            k = self.slot(stage, delta)
            yield pltpu.make_async_remote_copy(
                src_ref=self.shard if stage == 0 else self.region(stage, self.cs),
                dst_ref=self.region(stage, frm),
                send_sem=self.send.at[k],
                recv_sem=self.recv.at[k],
                device_id=(index_of(self.dims, to),),
                device_id_type=MESH,
            )

    def keep(self):
        return pltpu.make_async_copy(self.shard, self.region(0, self.cs), self.local_thin)

    def step(self, stage):
        if stage == 0:
            self.keep().start()
        if stage == 1:
            self.keep().wait()
        if stage >= 1:
            for c in self.copies(stage - 1, True):
                c.wait_recv()
        if stage < 4:
            for c in self.copies(stage, False):
                c.start()

    def finish(self):
        for stage in range(4):
            for c in self.copies(stage, False):
                c.wait_send()


def pipelined_thin(jobs, stages, lag):
    for tick in range(len(jobs) + (stages - 1) * lag):
        for stage in range(stages):
            i = tick - stage * lag
            if 0 <= i < len(jobs):
                jobs[i].step(stage)


class TokensThin:
    def __init__(self, n, me, a, b, send, recv, local_thin):
        self.n, self.me, self.a, self.b = n, me, a, b
        self.send, self.recv, self.local_thin = send, recv, local_thin

    def copy(self, d, incoming):
        to = lax.rem(self.me + d, self.n)
        frm = lax.rem(self.me - d + self.n, self.n)
        return pltpu.make_async_remote_copy(
            src_ref=self.a.at[to],
            dst_ref=self.b.at[frm if incoming else self.me],
            send_sem=self.send.at[d],
            recv_sem=self.recv.at[d],
            device_id=(to,),
            device_id_type=MESH,
        )

    def keep(self):
        return pltpu.make_async_copy(self.a.at[self.me], self.b.at[self.me], self.local_thin)

    def each(self, act):
        def body(d, carry):
            act(d)
            return carry

        lax.fori_loop(1, self.n, body, 0)

    def start(self):
        self.keep().start()
        self.each(lambda d: self.copy(d, False).start())

    def wait(self):
        self.keep().wait()
        self.each(lambda d: self.copy(d, True).wait_recv())
        self.each(lambda d: self.copy(d, False).wait_send())


def gather_kernel_thin(dims, plan, lag, count, with_tokens, *refs):
    n = math.prod(dims)
    t = 1 if with_tokens else 0
    ins, outs, scr = refs[: count + t], refs[count + t : 2 * (count + t)], refs[2 * (count + t) :]
    send, recv, local_thin = scr[:3]
    me = lax.axis_index("fsdp")
    cs = coords_of(dims, me)
    if with_tokens:
        greet_all(n, me)
        tokens = TokensThin(n, me, ins[count], outs[count], *scr[3:])
        tokens.start()
    else:
        greet_axes(dims, cs)
    jobs = [
        GatherThin(dims, cs, ins[a], outs[a], low, width, order, (send.at[i], recv.at[i], local_thin.at[i]))
        for i, (a, low, width, order) in enumerate(plan)
    ]
    pipelined_thin(jobs, 5, lag)
    for j in jobs:
        j.finish()
    if with_tokens:
        tokens.wait()


def token_sems_thin(n):
    return [
        pltpu.SemaphoreType.DMA((n,)),
        pltpu.SemaphoreType.DMA((n,)),
        pltpu.SemaphoreType.DMA,
    ]


def gather_call_thin(shards, tokens, plan, lag, collective_id):
    n = lax.axis_size("fsdp")
    dims = grid_of(n)
    k = hops(dims)
    ins = list(shards) + ([] if tokens is None else [tokens])
    outs = [jax.ShapeDtypeStruct(dims + s.shape, s.dtype) for s in shards]
    if tokens is not None:
        outs.append(jax.ShapeDtypeStruct(tokens.shape, tokens.dtype))
    m = len(plan)
    return pl.pallas_call(
        functools.partial(gather_kernel_thin, dims, plan, lag, len(shards), tokens is not None),
        out_shape=outs,
        in_specs=[any_spec()] * len(ins),
        out_specs=[any_spec()] * len(outs),
        scratch_shapes=[
            pltpu.SemaphoreType.DMA((m, k)),
            pltpu.SemaphoreType.DMA((m, k)),
            pltpu.SemaphoreType.DMA((m,)),
        ]
        + ([] if tokens is None else token_sems_thin(n)),
        compiler_params=pltpu.CompilerParams(
            collective_id=collective_id, has_side_effects=True, vmem_limit_bytes=VMEM_LIMIT
        ),
    )(*ins)


class ScatterThin:
    def __init__(self, dims, cs, terms, result, low, width, order, scratch, sems):
        self.dims, self.cs, self.order = dims, cs, order
        self.columns = pl.ds(low, width)
        self.terms, self.result = terms, result
        self.own, self.got = scratch[0], scratch[1:]
        self.send, self.recv, self.local_thin = sems

    def slot(self, stage, delta):
        return sum(self.dims[a] - 1 for a in self.order[:stage]) + delta - 1

    def part(self, stage, at):
        axis = self.order[stage]
        if stage == 0:
            lead = tuple(at if k == axis else slice(None) for k in range(4))
            return self.terms.at[lead + (slice(None), self.columns)]
        left = [k for k in range(4) if k not in self.order[:stage]]
        return self.got[stage - 1].at[(0,) + tuple(at if k == axis else slice(None) for k in left)]

    def copies(self, stage):
        axis = self.order[stage]
        for delta in range(1, self.dims[axis]):
            to = along(self.dims, self.cs, axis, delta)
            k = self.slot(stage, delta)
            yield pltpu.make_async_remote_copy(
                src_ref=self.part(stage, to[axis]),
                dst_ref=self.got[stage].at[delta - 1],
                send_sem=self.send.at[k],
                recv_sem=self.recv.at[k],
                device_id=(index_of(self.dims, to),),
                device_id_type=MESH,
            )

    def keep(self):
        return pltpu.make_async_copy(self.part(0, self.cs[self.order[0]]), self.own, self.local_thin)

    def total(self, stage):
        axis = self.order[stage]
        left = [k for k in range(4) if k not in self.order[: stage + 1]]
        shape = [self.dims[k] for k in left]
        got = self.got[stage]
        mine = self.own if stage == 0 else self.part(stage, self.cs[axis])

        def one(i, carry):
            at = tuple(coords_of(shape, i)) if shape else ()
            total = mine[at + (slice(None), slice(None))].astype(F32)
            for delta in range(1, self.dims[axis]):
                total += got[(delta - 1,) + at + (slice(None), slice(None))].astype(F32)
            if left:
                got[(0,) + at + (slice(None), slice(None))] = total.astype(got.dtype)
            else:
                self.result[:, self.columns] = total
            return carry

        lax.fori_loop(0, math.prod(shape), one, 0)

    def step(self, stage):
        if stage == 0:
            self.keep().start()
        if stage == 1:
            self.keep().wait()
        if stage >= 1:
            for c in self.copies(stage - 1):
                c.wait_recv()
            self.total(stage - 1)
        if stage < 4:
            for c in self.copies(stage):
                c.start()

    def finish(self):
        for stage in range(4):
            for c in self.copies(stage):
                c.wait_send()


def scatter_scratch_thin(dims, rows, width, order, dtype):
    left = list(dims)
    out = [pltpu.VMEM(tuple(d for k, d in enumerate(dims) if k != order[0]) + (rows, width), dtype)]
    for s, axis in enumerate(order):
        rest = tuple(dims[k] for k in range(4) if k not in order[: s + 1])
        out.append(pltpu.VMEM((dims[axis] - 1,) + rest + (rows, width), dtype))
    return out


def scatter_kernel_thin(dims, plan, lag, count, with_tokens, *refs):
    n = math.prod(dims)
    t = 1 if with_tokens else 0
    ins, outs, scr = refs[: count + t], refs[count + t : 2 * (count + t)], refs[2 * (count + t) :]
    send, recv, local_thin = scr[:3]
    scr = scr[3:]
    me = lax.axis_index("fsdp")
    cs = coords_of(dims, me)
    if with_tokens:
        greet_all(n, me)
        tokens = TokensThin(n, me, ins[count], outs[count], *scr[:3])
        tokens.start()
        scr = scr[3:]
    else:
        greet_axes(dims, cs)
    jobs = [
        ScatterThin(
            dims, cs, ins[a], outs[a], low, width, order, scr[5 * i : 5 * i + 5],
            (send.at[i], recv.at[i], local_thin.at[i]),
        )
        for i, (a, low, width, order) in enumerate(plan)
    ]
    pipelined_thin(jobs, 5, lag)
    for j in jobs:
        j.finish()
    if with_tokens:
        tokens.wait()


def scatter_call_thin(terms, tokens, plan, lag, collective_id):
    n = lax.axis_size("fsdp")
    dims = grid_of(n)
    k = hops(dims)
    ins = list(terms) + ([] if tokens is None else [tokens])
    outs = [jax.ShapeDtypeStruct(s.shape[4:], F32) for s in terms]
    out_specs = [vmem_spec()] * len(terms)
    if tokens is not None:
        outs.append(jax.ShapeDtypeStruct(tokens.shape, tokens.dtype))
        out_specs.append(any_spec())
    m = len(plan)
    scratch = []
    for a, low, width, order in plan:
        scratch += scatter_scratch_thin(dims, terms[a].shape[4], width, order, terms[a].dtype)
    return pl.pallas_call(
        functools.partial(scatter_kernel_thin, dims, plan, lag, len(terms), tokens is not None),
        out_shape=outs,
        in_specs=[any_spec()] * len(ins),
        out_specs=out_specs,
        scratch_shapes=[
            pltpu.SemaphoreType.DMA((m, k)),
            pltpu.SemaphoreType.DMA((m, k)),
            pltpu.SemaphoreType.DMA((m,)),
        ]
        + ([] if tokens is None else token_sems_thin(n))
        + scratch,
        compiler_params=pltpu.CompilerParams(
            collective_id=collective_id, has_side_effects=True, vmem_limit_bytes=VMEM_LIMIT
        ),
    )(*ins)


def conv_thin(values, taps, row):
    total = values * taps[0:1]
    for c in range(1, taps.shape[0]):
        total += shifted(values, c, row) * taps[c : c + 1]
    return total


def project_thin(own, small, weights, attn_low, pre, queries, keys, values, beta, micro, length):
    width = own.shape[1]
    row = lax.broadcasted_iota(jnp.int32, (length, 2 * HEAD), 0)
    gain = small[ROW_ATTN : ROW_ATTN + 1, :]
    beta_rows = low(small[ROW_BETA : ROW_BETA + 16, :])

    def one(m, carry):
        rows = pl.ds(m * length, length)
        v = own[rows, :].astype(F32)
        r = lax.rsqrt(jnp.mean(v * v, axis=-1, keepdims=True) + NORM_EPS)
        attn_low[rows, :] = low(v * r * gain)
        a = attn_low[rows, :]
        beta[rows, :] = jax.nn.sigmoid(dot_nt(a, beta_rows))
        for kind, out in enumerate((queries, keys, values)):
            for b in range(width // (2 * HEAD)):
                cols = lanes(b, 2 * HEAD)
                wide = slice(kind * width + cols.start, kind * width + cols.stop)
                x = dot(a, weights[:, wide])
                pre[rows, wide] = low(x)
                c = conv_thin(x, small[4 * kind : 4 * kind + 4, cols], row)
                u = c * jax.nn.sigmoid(c)
                if kind == 2:
                    out[rows, cols] = low(u)
                    continue
                for h in range(2):
                    part = u[:, lanes(h)]
                    n = lax.rsqrt(head_sum(part * part) + UNIT_EPS)
                    out[rows, slice(cols.start + h * HEAD, cols.start + (h + 1) * HEAD)] = low(part * n)
        return carry

    lax.fori_loop(0, micro, one, 0)


def delta_block_thin(base, first, refs, gain):
    queries, keys, values, beta, state, states, inverses, scores, fresh, mix, mixed, at = refs
    rows = pl.ds(base, SPAN)
    i, j = iotas((SPAN, SPAN))
    masks = level_masks()
    eye = jnp.where(i == j, 1.0, 0.0).astype(F32)
    heads = range(HEADS)

    @pl.when(first)
    def _():
        state[...] = jnp.zeros_like(state)

    strength = beta[rows, :]
    k = [keys[rows, lanes(h)] for h in heads]
    q = [queries[rows, lanes(h)] for h in heads]
    b = [strength[:, h : h + 1] for h in heads]
    strict = [low(jnp.where(i > j, dot_nt(k[h], k[h]) * b[h], 0.0)) for h in heads]
    for h in heads:
        scores[at, h] = low(jnp.where(i >= j, dot_nt(q[h], k[h]), 0.0))
    zero = jnp.zeros((), BF16)
    inv = [eye - jnp.where(masks[0], strict[h], zero).astype(F32) for h in heads]
    for level in range(1, len(masks)):
        t = [low(inv[h]) for h in heads]
        f = [low(dot(jnp.where(masks[level], strict[h], zero), t[h])) for h in heads]
        inv = [inv[h] - dot(t[h], f[h]) for h in heads]
    for h in heads:
        inverses[at, h] = low(inv[h])
    s = [low(state[h]) for h in heads]
    for h in heads:
        states[at, h] = s[h]
    rest = [low((values[rows, lanes(h)].astype(F32) - dot(k[h], s[h])) * b[h]) for h in heads]
    new = [low(dot(inverses[at, h], rest[h])) for h in heads]
    out = [dot(q[h], s[h]) + dot(scores[at, h], new[h]) for h in heads]
    for h in heads:
        fresh[rows, lanes(h)] = new[h]
        state[h] += dot_tn(k[h], new[h])
        r = lax.rsqrt(jnp.mean(out[h] * out[h], axis=-1, keepdims=True) + NORM_EPS)
        mix[rows, lanes(h)] = low(out[h])
        mixed[rows, lanes(h)] = low(out[h] * r * gain)


def forward_kernel_thin(micro, length, *refs):
    (own, small, weights, out_weight, hidden, attn_low, pre, queries, keys, values, beta,
     states, inverses, scores, fresh, mix, mixed, state) = refs
    project_thin(own, small, weights, attn_low, pre, queries, keys, values, beta, micro, length)
    gain = small[ROW_OUT : ROW_OUT + 1, :HEAD]
    blocks = length // SPAN

    def one(t, carry):
        delta_block_thin(
            pl.multiple_of(t * SPAN, SPAN), lax.rem(t, blocks) == 0,
            (queries, keys, values, beta, state, states, inverses, scores, fresh, mix, mixed, t), gain,
        )
        rows = pl.ds(pl.multiple_of(t * SPAN, SPAN), SPAN)
        hidden[rows, :] = own[rows, :].astype(F32) + dot_nt(mixed[rows, :], out_weight[...])
        return carry

    lax.fori_loop(0, micro * blocks, one, 0)


def forward_call_thin(own, small, weights, out_weight, micro):
    rows, width = own.shape
    length = rows // micro
    blocks = rows // SPAN
    square = jax.ShapeDtypeStruct((blocks, HEADS, SPAN, SPAN), BF16)
    wide = jax.ShapeDtypeStruct((rows, width), BF16)
    outs = [
        jax.ShapeDtypeStruct((rows, width), F32), wide, jax.ShapeDtypeStruct((rows, 3 * width), BF16),
        wide, wide, wide, jax.ShapeDtypeStruct((rows, 16), F32),
        jax.ShapeDtypeStruct((blocks, HEADS, HEAD, HEAD), BF16), square, square, wide, wide, wide,
    ]
    return pl.pallas_call(
        functools.partial(forward_kernel_thin, micro, length),
        out_shape=outs,
        in_specs=[vmem_spec()] * 4,
        out_specs=[vmem_spec()] * len(outs),
        scratch_shapes=[pltpu.VMEM((HEADS, HEAD, HEAD), F32)],
        compiler_params=pltpu.CompilerParams(vmem_limit_bytes=VMEM_LIMIT),
    )(own, small, weights, out_weight)


def feed_kernel_thin(steps, hidden, grad, small, active, w_ref, result, terms, d_hidden, gain_grad, norm, total, d_norm):
    t = pl.program_id(0)
    gain = small[ROW_MLP : ROW_MLP + 1, :]

    @pl.when(t == 0)
    def _():
        v = hidden[...]
        r = lax.rsqrt(jnp.mean(v * v, axis=-1, keepdims=True) + NORM_EPS)
        norm[...] = low(v * r * gain)
        total[...] = v
        d_norm[...] = jnp.zeros_like(d_norm)

    x, g = norm[...], grad[...]
    gw, uw, dw = (w_ref[:, lanes(i, FFW)] for i in range(3))
    gate, up = dot(x, gw), dot(x, uw)
    d_act = dot(g, dw)
    s = jax.nn.sigmoid(gate)
    silu = gate * s
    act = low(silu * up)
    d_gate = low(d_act * up * (s + silu * (1.0 - s)))
    d_up = low(d_act * silu)
    total[...] += dot_nt(act, dw)
    d_norm[...] += dot_nt(d_gate, gw) + dot_nt(d_up, uw)
    terms[:, lanes(0, FFW)] = low(dot_tn(x, d_gate))
    terms[:, lanes(1, FFW)] = low(dot_tn(x, d_up))
    terms[:, lanes(2, FFW)] = low(dot_tn(g, act))

    @pl.when(t == steps - 1)
    def _():
        result[...] = low(jnp.where(active[...] > 0.0, total[...], 0.0))
        v, d = hidden[...], d_norm[...]
        n = v.shape[1]
        r = lax.rsqrt(jnp.mean(v * v, axis=-1, keepdims=True) + NORM_EPS)
        vr = v * r
        gain_grad[...] = jnp.sum(d * vr, axis=0, keepdims=True)
        gd = d * gain
        d_hidden[...] = g.astype(F32) + r * (gd - vr * (jnp.sum(vr * gd, axis=-1, keepdims=True) / n))


def feed_call_thin(hidden, grad, small, active, weights):
    rows, width = hidden.shape
    steps = weights.shape[1] // (3 * FFW)
    whole = lambda *shape: pl.BlockSpec(shape, lambda t: (0,) * len(shape))
    block = pl.BlockSpec((width, 3 * FFW), lambda t: (0, t))
    return pl.pallas_call(
        functools.partial(feed_kernel_thin, steps),
        grid=(steps,),
        out_shape=[
            jax.ShapeDtypeStruct((rows, width), BF16),
            jax.ShapeDtypeStruct(weights.shape, BF16),
            jax.ShapeDtypeStruct((rows, width), F32),
            jax.ShapeDtypeStruct((1, width), F32),
        ],
        in_specs=[whole(rows, width), whole(rows, width), whole(*small.shape), whole(rows, 1), block],
        out_specs=[whole(rows, width), block, whole(rows, width), whole(1, width)],
        scratch_shapes=[
            pltpu.VMEM((rows, width), BF16),
            pltpu.VMEM((rows, width), F32),
            pltpu.VMEM((rows, width), F32),
        ],
        compiler_params=pltpu.CompilerParams(
            vmem_limit_bytes=VMEM_LIMIT, dimension_semantics=("arbitrary",)
        ),
    )(hidden, grad, small, active, weights)


def delta_back_thin(base, last, refs, gain):
    (queries, keys, values, beta, states, inverses, scores, fresh, mix, d_mixed,
     d_state, d_out, d_q, d_k, d_v, d_beta, gain_grad, at) = refs
    rows = pl.ds(base, SPAN)
    i, j = iotas((SPAN, SPAN))
    lane = lax.broadcasted_iota(jnp.int32, (SPAN, 16), 1)
    heads = range(HEADS)

    @pl.when(last)
    def _():
        d_state[...] = jnp.zeros_like(d_state)

    strength = beta[rows, :]
    k = [keys[rows, lanes(h)] for h in heads]
    q = [queries[rows, lanes(h)] for h in heads]
    e = [fresh[rows, lanes(h)] for h in heads]
    b = [strength[:, h : h + 1] for h in heads]
    kb = [low(k[h].astype(F32) * b[h]) for h in heads]
    do = []
    for h in heads:
        v, d = mix[rows, lanes(h)].astype(F32), d_mixed[:, lanes(h)]
        r = lax.rsqrt(jnp.mean(v * v, axis=-1, keepdims=True) + NORM_EPS)
        vr, gd = v * r, d * gain
        gain_grad[...] += jnp.sum(d * vr, axis=0, keepdims=True)
        do.append(low(r * (gd - vr * jnp.mean(vr * gd, axis=-1, keepdims=True))))
    s = [states[at, h] for h in heads]
    p = [scores[at, h] for h in heads]
    ds = [low(d_state[h]) for h in heads]
    de = [low(dot_tn(p[h], do[h]) + dot(k[h], ds[h])) for h in heads]
    dx = [dot_tn(inverses[at, h], de[h]) for h in heads]
    dxl = [low(dx[h]) for h in heads]
    dp = [low(jnp.where(i >= j, dot_nt(do[h], e[h]), 0.0)) for h in heads]
    da = [low(jnp.where(i > j, -dot_nt(dxl[h], e[h]), 0.0)) for h in heads]
    dkb = [dot(da[h], k[h]) - dot_nt(dxl[h], s[h]) for h in heads]
    beta_grad = jnp.zeros((SPAN, 16), F32)
    for h in heads:
        d_q[rows, lanes(h)] = low(dot_nt(do[h], s[h]) + dot(dp[h], k[h]))
        d_k[rows, lanes(h)] = low(
            dkb[h] * b[h] + dot_tn(da[h], kb[h]) + dot_tn(dp[h], q[h]) + dot_nt(e[h], ds[h])
        )
        d_v[rows, lanes(h)] = low(dx[h] * b[h])
        d_state[h] += dot_tn(q[h], do[h]) - dot_tn(kb[h], dxl[h])
        db = head_sum(dkb[h] * k[h].astype(F32) + dx[h] * values[rows, lanes(h)].astype(F32))
        beta_grad += jnp.where(lane == h, db, 0.0)
    d_beta[rows, :] = low(beta_grad * strength * (1.0 - strength))


def backward_kernel_thin(micro, length, *refs):
    (d_hidden, own, small, weights, out_weight, attn_low, pre, queries, keys, values, beta,
     states, inverses, scores, fresh, mix, mixed,
     d_own, qkv_grad, out_grad, small_grad,
     d_state, d_out, d_q, d_k, d_v, d_beta, d_pre, d_attn, gain_grad) = refs
    width = own.shape[1]
    blocks = length // SPAN
    total = micro * blocks
    gain = small[ROW_OUT : ROW_OUT + 1, :HEAD]
    gain_grad[...] = jnp.zeros_like(gain_grad)
    small_grad[...] = jnp.zeros_like(small_grad)
    d_attn[...] = low(d_hidden[...])

    def one(step, carry):
        t = total - 1 - step
        base = pl.multiple_of(t * SPAN, SPAN)
        d_out[...] = dot(d_attn[pl.ds(base, SPAN), :], out_weight[...])
        delta_back_thin(
            base, lax.rem(step, blocks) == 0,
            (queries, keys, values, beta, states, inverses, scores, fresh, mix, d_out,
             d_state, None, d_q, d_k, d_v, d_beta, gain_grad, t), gain,
        )
        return carry

    lax.fori_loop(0, total, one, 0)
    row = lax.broadcasted_iota(jnp.int32, (length, HEAD), 0)

    def conv_back(m, carry):
        rows = pl.ds(m * length, length)
        for kind, grads in enumerate((d_q, d_k, d_v)):
            for h in range(width // HEAD):
                cols = lanes(h)
                wide = slice(kind * width + cols.start, kind * width + cols.stop)
                taps = small[4 * kind : 4 * kind + 4, cols]
                x = pre[rows, wide].astype(F32)
                moved = [shifted(x, c, row) for c in range(4)]
                c = moved[0] * taps[0:1]
                for o in range(1, 4):
                    c += moved[o] * taps[o : o + 1]
                s = jax.nn.sigmoid(c)
                u = c * s
                d = grads[rows, cols].astype(F32)
                if kind < 2:
                    n = lax.rsqrt(head_sum(u * u) + UNIT_EPS)
                    un = u * n
                    d = (d - un * head_sum(un * d)) * n
                d = d * (s + u * (1.0 - s))
                for o in range(4):
                    at = slice(4 * kind + o, 4 * kind + o + 1)
                    small_grad[at, cols] += jnp.sum(moved[o] * d, axis=0, keepdims=True)
                back = d * taps[0:1]
                for o in range(1, 4):
                    back += shifted(d, -o, row) * taps[o : o + 1]
                d_pre[rows, wide] = low(back)
        return carry

    lax.fori_loop(0, micro, conv_back, 0)
    for b in range(width // 256):
        cols = lanes(b, 256)
        out_grad[:, cols] = low(dot_tn(d_attn[...], mixed[:, cols]))
    for b in range(3 * width // 256):
        cols = lanes(b, 256)
        qkv_grad[:, cols] = low(dot_tn(attn_low[...], d_pre[:, cols]))
    beta_rows = low(small[ROW_BETA : ROW_BETA + 16, :])
    small_grad[ROW_BETA : ROW_BETA + 16, :] = dot_tn(d_beta[...], attn_low[...])
    small_grad[ROW_OUT : ROW_OUT + 1, :HEAD] = gain_grad[...]
    attn_gain = small[ROW_ATTN : ROW_ATTN + 1, :]

    def finish(t, carry):
        rows = pl.ds(pl.multiple_of(t * SPAN, SPAN), SPAN)
        d = dot_nt(d_pre[rows, :], weights[...]) + dot(d_beta[rows, :], beta_rows)
        v = own[rows, :].astype(F32)
        r = lax.rsqrt(jnp.mean(v * v, axis=-1, keepdims=True) + NORM_EPS)
        vr, gd = v * r, d * attn_gain
        small_grad[ROW_ATTN : ROW_ATTN + 1, :] += jnp.sum(d * vr, axis=0, keepdims=True)
        d_own[rows, :] = low(d_hidden[rows, :] + r * (gd - vr * jnp.mean(vr * gd, axis=-1, keepdims=True)))
        return carry

    lax.fori_loop(0, total, finish, 0)


def backward_call_thin(d_hidden, own, small, weights, out_weight, saved, micro):
    rows, width = own.shape
    length = rows // micro
    return pl.pallas_call(
        functools.partial(backward_kernel_thin, micro, length),
        out_shape=[
            jax.ShapeDtypeStruct((rows, width), BF16),
            jax.ShapeDtypeStruct((width, 3 * width), BF16),
            jax.ShapeDtypeStruct((width, width), BF16),
            jax.ShapeDtypeStruct((SMALL_ROWS, width), F32),
        ],
        in_specs=[vmem_spec()] * (5 + len(saved)),
        out_specs=[vmem_spec()] * 4,
        scratch_shapes=[
            pltpu.VMEM((HEADS, HEAD, HEAD), F32),
            pltpu.VMEM((SPAN, width), F32),
            pltpu.VMEM((rows, width), BF16),
            pltpu.VMEM((rows, width), BF16),
            pltpu.VMEM((rows, width), BF16),
            pltpu.VMEM((rows, 16), BF16),
            pltpu.VMEM((rows, 3 * width), BF16),
            pltpu.VMEM((rows, width), BF16),
            pltpu.VMEM((1, HEAD), F32),
        ],
        compiler_params=pltpu.CompilerParams(vmem_limit_bytes=VMEM_LIMIT),
    )(d_hidden, own, small, weights, out_weight, *saved)


def local_thin(
    inputs, cotangent, lengths, owners, attn_gain, query_weight, key_weight, value_weight, beta_weight,
    query_conv, key_conv, value_conv, out_gain, out_weight, mlp_gain, gate_weight, up_weight, down_weight,
):
    n = lax.axis_size("fsdp")
    dims = grid_of(n)
    me = lax.axis_index("fsdp")
    micro, _, length, width = inputs.shape
    hidden_units = gate_weight.shape[1]
    share = width // n
    slots = length // n
    per = micro * slots
    parts = 16 // math.gcd(per, 16)
    thin = width // parts
    i32 = jnp.int32
    devices = jnp.arange(n, dtype=i32)
    slot_ids = jnp.arange(slots, dtype=i32)
    row_ids = jnp.arange(length, dtype=i32)
    micros = jnp.arange(micro, dtype=i32)
    part_ids = jnp.arange(parts, dtype=i32)

    before = devices[:, None] < devices[None, :]
    starts = jnp.sum(jnp.where(before[None], lengths[:, :, None], 0), axis=1)
    match = owners[:, None, :] == devices[None, :, None]
    own_start = jnp.sum(jnp.where(match, starts[:, None, :], 0), axis=2)
    own_len = jnp.sum(jnp.where(match, lengths[:, None, :], 0), axis=2)
    mine = devices == me
    my_start = jnp.sum(jnp.where(mine, own_start, 0), axis=1)
    my_len = jnp.sum(jnp.where(mine, own_len, 0), axis=1)

    first = own_start + (me - own_start) % n
    pos = first[:, :, None] + n * slot_ids
    live = pos < (own_start + own_len)[:, :, None]
    send = jnp.where(live, micros[:, None, None] * length + pos // n, -1)
    send = jnp.moveaxis(send, 0, 1)[:, None] + jnp.zeros((1, parts, 1, 1), i32)
    send = jnp.where(send >= 0, send + (part_ids * micro * length)[None, :, None, None], -1)
    rows_in = split_rows(inputs[:, 0].reshape(micro * length, width), parts).reshape(-1, thin)
    outgoing = picked(send.reshape(-1), rows_in).reshape(n, parts * per, thin)

    def row_of(v):
        return jnp.pad(v, ((0, 0), (0, share - v.shape[1])))

    packed = jnp.concatenate([
        query_conv, key_conv, value_conv, attn_gain[None], mlp_gain[None], row_of(out_gain[None]),
        jnp.zeros((1, share), BF16), beta_weight.T, jnp.zeros((SMALL_ROWS - 16 - HEADS, share), BF16),
    ])
    count = SMALL_ROWS * share // HEAD
    packed = jnp.pad(packed.reshape(count, HEAD), ((0, -count % 16), (0, 0)))

    attn_shard = jnp.concatenate([query_weight, key_weight, value_weight, out_weight.T], axis=1)
    steps = hidden_units // FFW
    feed_shard = jnp.stack(
        [w.reshape(share, steps, FFW) for w in (gate_weight, up_weight, down_weight.T)], axis=2
    ).reshape(share, 3 * hidden_units)

    plan = [(0, 0, HEAD, ZXY)]
    for a, (w, size) in enumerate(((4 * width, 512), (3 * hidden_units, 768)), 1):
        for at, wide in spans(w, size):
            plan.append((a, at, wide, (ZXY, ZYX)[len(plan) % 2]))
    small_all, attn_all, feed_all, incoming = gather_call_thin(
        [packed, attn_shard, feed_shard], outgoing, tuple(plan), 2, 1
    )
    small = small_all.reshape(n, -1)[:, : SMALL_ROWS * share].reshape(n, SMALL_ROWS, share)
    small = jnp.moveaxis(small, 1, 0)
    gain_row = small[ROW_OUT, :, : HEAD // n].reshape(1, HEAD)
    small = small.reshape(SMALL_ROWS, width).astype(F32)
    small = lax.dynamic_update_slice(small, gain_row.astype(F32), (ROW_OUT, 0))
    attn_all = attn_all.reshape(width, 4 * width)
    feed_all = feed_all.reshape(width, 3 * hidden_units)
    qkv, out_t = attn_all[:, : 3 * width], attn_all[:, 3 * width :]

    active = row_ids[None] < my_len[:, None]
    block = (my_start[:, None] + row_ids) % n
    at = block * (parts * per) + micros[:, None] * slots + row_ids // n
    take = jnp.where(active, at, -1).reshape(-1)
    flat = incoming.reshape(n * parts * per, thin)
    own = jnp.concatenate(
        [picked(jnp.where(take >= 0, take + p * per, -1), flat) for p in range(parts)], axis=1
    )
    active = active.reshape(-1, 1)
    grad = jnp.where(active, cotangent[:, 0].reshape(-1, width), jnp.zeros((), BF16))

    hidden, *saved = forward_call_thin(own, small, qkv, out_t, micro)
    result, feed_terms, d_hidden, mlp_gain_grad = feed_call_thin(
        hidden, grad, small, active.astype(F32), feed_all
    )
    d_own, qkv_terms, out_terms, small_terms = backward_call_thin(
        d_hidden, own, small, qkv, out_t, saved, micro
    )

    back = slot_ids * n + (devices[:, None, None] - my_start[None, :, None]) % n
    back = jnp.where(back < my_len[None, :, None], back + (micros * length)[None, :, None], -1)
    back = back[:, None] + jnp.zeros((1, parts, 1, 1), i32)
    back = jnp.where(back >= 0, back + (part_ids * micro * length)[None, :, None, None], -1)
    returning = picked(back.reshape(-1), split_rows(d_own, parts).reshape(-1, thin))
    returning = returning.reshape(n, parts * per, thin)

    small_terms = lax.dynamic_update_slice(small_terms, mlp_gain_grad, (ROW_MLP, 0))
    out_gain_terms = jnp.pad(small_terms[ROW_OUT, :HEAD].reshape(n, -1), ((0, 0), (0, share - HEAD // n)))
    small_terms = jnp.concatenate(
        [small_terms[:ROW_OUT].reshape(ROW_OUT, n, share), out_gain_terms[None],
         small_terms[ROW_OUT + 1 :].reshape(SMALL_ROWS - ROW_OUT - 1, n, share)]
    )
    small_terms = jnp.moveaxis(small_terms, 1, 0).reshape(n, count, HEAD)
    small_terms = jnp.pad(small_terms, ((0, 0), (0, -count % 16), (0, 0)))
    terms = [
        small_terms.reshape(dims + small_terms.shape[1:]),
        qkv_terms.reshape(dims + (share, 3 * width)),
        out_terms.reshape(dims + (share, width)),
        feed_terms.reshape(dims + (share, 3 * hidden_units)),
    ]
    plan = []
    for a, size in ((3, 768), (2, 512), (1, 512), (0, HEAD)):
        for lo, wide in spans(terms[a].shape[5], size):
            plan.append((a, lo, wide, (CXYZ, CYXZ)[len(plan) % 2]))
    small_grad, qkv_grad, out_grad, feed_grad, returned = scatter_call_thin(
        terms, returning, tuple(plan), 2, 2
    )

    place = row_ids * n + me
    inside = (place[None, :, None] >= own_start[:, None, :]) & (
        place[None, :, None] < (own_start + own_len)[:, None, :]
    )
    at = devices * (parts * per) + micros[:, None, None] * slots + (place[None, :, None] - first[:, None, :]) // n
    take = (jnp.sum(jnp.where(inside, at + 1, 0), axis=2) - 1).reshape(-1)
    flat = returned.reshape(n * parts * per, thin)
    input_rows = jnp.concatenate(
        [picked(jnp.where(take >= 0, take + p * per, -1), flat) for p in range(parts)], axis=1
    )

    small_grad = small_grad.reshape(-1)[: SMALL_ROWS * share].reshape(SMALL_ROWS, share)
    feed_grad = feed_grad.reshape(share, steps, 3, FFW)
    gate_grad, up_grad, down_grad = (
        feed_grad[:, :, i].reshape(share, hidden_units) for i in range(3)
    )
    return (
        result.reshape(micro, 1, length, width),
        input_rows.reshape(micro, 1, length, width),
        small_grad[ROW_ATTN],
        qkv_grad[:, :width],
        qkv_grad[:, width : 2 * width],
        qkv_grad[:, 2 * width :],
        small_grad[ROW_BETA : ROW_BETA + HEADS].T,
        small_grad[0:4],
        small_grad[4:8],
        small_grad[8:12],
        small_grad[ROW_OUT, : HEAD // n],
        out_grad.T,
        small_grad[ROW_MLP],
        gate_grad,
        up_grad,
        down_grad.T,
    )


def solution(mesh):
    rows, cols, flat = P("fsdp", None), P(None, "fsdp"), P("fsdp")
    data = P(None, "fsdp", None, None)
    return jax.shard_map(
        local,
        mesh=mesh,
        in_specs=(
            data, data, P(), P(), flat, rows, rows, rows, rows, cols, cols, cols, flat, cols, flat, rows, rows, cols,
        ),
        out_specs=(
            data, data, flat, rows, rows, rows, rows, cols, cols, cols, flat, cols, flat, rows, rows, cols,
        ),
        check_vma=False,
    )
```

```python
import functools
import math

import jax
import jax.numpy as jnp
from jax import lax
from jax.experimental import pallas as pl
from jax.experimental.pallas import tpu as pltpu
from jax.sharding import PartitionSpec as P

HEADS = 8
HEAD = 128
SPAN = 128
NORM_EPS = 1e-05
UNIT_EPS = 1e-06
MESH = pl.DeviceIdType.MESH
F32, BF16 = jnp.float32, jnp.bfloat16
VMEM_LIMIT = 62 * 1024 * 1024
FFW = 256
WIDE = 3 * FFW
HALF = WIDE // 2
Z, Y, X, C = 0, 1, 2, 3
ZXY, ZYX = (Z, X, Y, C), (Z, Y, X, C)
CXYZ, CYXZ = (C, X, Y, Z), (C, Y, X, Z)
GATHER_TICKS = (0, 2, 4, 6, 8)
FEED_TICKS = (0, 2, 4, 6, 7)
SCATTER_TICKS = (0, 1, 3, 5, 7)
SLOTS = (4, 6, 6, 4)

ROW_CONV, ROW_ATTN, ROW_MLP, ROW_OUT, ROW_BETA, SMALL_ROWS = 0, 12, 13, 14, 16, 32


def grid_of(n):
    chips = n // 2
    a = 4 if chips % 4 == 0 else 1
    rest = chips // a
    b = 1
    while b * b < rest:
        b *= 2
    return (a, b, rest // b, 2)


def coords_of(dims, index):
    out = []
    for size in reversed(dims):
        out.append(lax.rem(index, size))
        index = index // size
    return out[::-1]


def index_of(dims, cs):
    total = 0
    for size, c in zip(dims, cs):
        total = total * size + c
    return total


def along(dims, cs, axis, delta):
    moved = list(cs)
    moved[axis] = lax.rem(cs[axis] + delta + dims[axis], dims[axis])
    return moved


def axis_peers(dims, cs):
    return [index_of(dims, along(dims, cs, a, d)) for a in range(4) for d in range(1, dims[a])]


def greet_all(n, me):
    barrier = pltpu.get_barrier_semaphore()

    def hello(d, carry):
        pl.semaphore_signal(
            barrier, inc=1, device_id=(lax.rem(me + d, n),), device_id_type=MESH
        )
        return carry

    lax.fori_loop(1, n, hello, 0)
    pl.semaphore_wait(barrier, n - 1)


def hops(dims):
    return sum(d - 1 for d in dims)


def guard(condition, act):
    if isinstance(condition, bool):
        if condition:
            act()
    else:
        pl.when(condition)(act)


def run_tick(segments, ticks, tick):
    for stage in reversed(range(len(ticks))):
        i = tick - ticks[stage]
        for make, first, end in segments:
            inside = (first <= i < end) if isinstance(i, int) else (i >= first) & (i < end)

            def act(make=make, i=i, stage=stage):
                for job in make(i):
                    job.step(stage)

            guard(inside, act)


class Gather:
    def __init__(self, dims, cs, shard, out, columns, order, sems):
        self.dims, self.cs, self.order, self.columns = dims, cs, order, columns
        self.shard, self.out = shard.at[:, columns], out
        self.send, self.recv, self.local = sems

    def slot(self, stage, delta):
        return sum(self.dims[a] - 1 for a in self.order[:stage]) + delta - 1

    def region(self, stage, cs):
        done = self.order[:stage]
        lead = tuple(slice(None) if k in done else cs[k] for k in range(4))
        return self.out.at[lead + (slice(None), self.columns)]

    def copies(self, stage, incoming):
        axis = self.order[stage]
        for delta in range(1, self.dims[axis]):
            frm = along(self.dims, self.cs, axis, -delta) if incoming else self.cs
            to = along(self.dims, self.cs, axis, delta)
            k = self.slot(stage, delta)
            yield pltpu.make_async_remote_copy(
                src_ref=self.shard if stage == 0 else self.region(stage, self.cs),
                dst_ref=self.region(stage, frm),
                send_sem=self.send.at[k],
                recv_sem=self.recv.at[k],
                device_id=(index_of(self.dims, to),),
                device_id_type=MESH,
            )

    def keep(self):
        return pltpu.make_async_copy(self.shard, self.region(0, self.cs), self.local)

    def step(self, stage):
        if stage == 0:
            self.keep().start()
        if stage == 1:
            self.keep().wait()
        if stage >= 1:
            for c in self.copies(stage - 1, True):
                c.wait_recv()
        if stage < 4:
            for c in self.copies(stage, False):
                c.start()

    def finish(self):
        for stage in range(4):
            for c in self.copies(stage, False):
                c.wait_send()


class Scatter:
    def __init__(self, dims, cs, terms, term_columns, result, columns, order, got, sems):
        self.dims, self.cs, self.order = dims, cs, order
        self.term_columns, self.columns = term_columns, columns
        self.terms, self.result, self.got = terms, result, got
        self.send, self.recv = sems

    def slot(self, stage, delta):
        return sum(self.dims[a] - 1 for a in self.order[:stage]) + delta - 1

    def part(self, stage, at):
        axis = self.order[stage]
        if stage == 0:
            lead = tuple(at if k == axis else slice(None) for k in range(4))
            return self.terms.at[lead + (slice(None), self.term_columns)]
        left = [k for k in range(4) if k not in self.order[:stage]]
        return self.got[stage - 1].at[(0,) + tuple(at if k == axis else slice(None) for k in left)]

    def copies(self, stage):
        axis = self.order[stage]
        for delta in range(1, self.dims[axis]):
            to = along(self.dims, self.cs, axis, delta)
            k = self.slot(stage, delta)
            yield pltpu.make_async_remote_copy(
                src_ref=self.part(stage, to[axis]),
                dst_ref=self.got[stage].at[delta - 1],
                send_sem=self.send.at[k],
                recv_sem=self.recv.at[k],
                device_id=(index_of(self.dims, to),),
                device_id_type=MESH,
            )

    def total(self, stage):
        axis = self.order[stage]
        left = [k for k in range(4) if k not in self.order[: stage + 1]]
        shape = [self.dims[k] for k in left]
        got = self.got[stage]
        mine = self.part(stage, self.cs[axis])

        def one(i, carry):
            at = tuple(coords_of(shape, i)) if shape else ()
            total = mine[at + (slice(None), slice(None))].astype(F32)
            for delta in range(1, self.dims[axis]):
                total += got[(delta - 1,) + at + (slice(None), slice(None))].astype(F32)
            if left:
                got[(0,) + at + (slice(None), slice(None))] = total.astype(got.dtype)
            else:
                self.result[:, self.columns] = total
            return carry

        lax.fori_loop(0, math.prod(shape), one, 0)

    def step(self, stage):
        if stage >= 1:
            for c in self.copies(stage - 1):
                c.wait()
            self.total(stage - 1)
        if stage < 4:
            for c in self.copies(stage):
                c.start()


def scatter_scratch(dims, rows, width, order, dtype, slots=None):
    out = []
    for s, axis in enumerate(order):
        rest = tuple(dims[k] for k in range(4) if k not in order[: s + 1])
        lead = () if slots is None else (slots[s],)
        out.append(pltpu.VMEM(lead + (dims[axis] - 1,) + rest + (rows, width), dtype))
    return out


class Tokens:
    def __init__(self, n, me, rows, a, b, send, recv, local):
        self.n, self.me, self.rows, self.a, self.b = n, me, rows, a, b
        self.send, self.recv, self.local = send, recv, local

    def block(self, d):
        return pl.ds(pl.multiple_of(d * self.rows, self.rows), self.rows)

    def copy(self, d, incoming):
        to = lax.rem(self.me + d, self.n)
        frm = lax.rem(self.me - d + self.n, self.n)
        return pltpu.make_async_remote_copy(
            src_ref=self.a.at[self.block(to)],
            dst_ref=self.b.at[self.block(frm if incoming else self.me)],
            send_sem=self.send.at[d],
            recv_sem=self.recv.at[d],
            device_id=(to,),
            device_id_type=MESH,
        )

    def keep(self):
        at = self.block(self.me)
        return pltpu.make_async_copy(self.a.at[at], self.b.at[at], self.local)

    def each(self, act):
        def body(d, carry):
            act(d)
            return carry

        lax.fori_loop(1, self.n, body, 0)

    def start(self):
        self.keep().start()
        self.each(lambda d: self.copy(d, False).start())

    def wait(self):
        self.keep().wait()
        self.each(lambda d: self.copy(d, True).wait_recv())
        self.each(lambda d: self.copy(d, False).wait_send())


def any_spec():
    return pl.BlockSpec(memory_space=pl.ANY)


def vmem_spec():
    return pl.BlockSpec(memory_space=pltpu.VMEM)


def dot(a, b):
    return lax.dot_general(a, b, (((1,), (0,)), ((), ())), preferred_element_type=F32)


def dot_nt(a, b):
    return lax.dot_general(a, b, (((1,), (1,)), ((), ())), preferred_element_type=F32)


def dot_tn(a, b):
    return lax.dot_general(a, b, (((0,), (0,)), ((), ())), preferred_element_type=F32)


def low(v):
    return v.astype(BF16)


def lanes(i, width=HEAD):
    return slice(i * width, (i + 1) * width)


def place(kind, h):
    at = (h // 2) * WIDE + kind * 2 * HEAD + (h % 2) * HEAD
    return slice(at, at + HEAD)


def shifted(values, by, row):
    if by == 0:
        return values
    rows = values.shape[0]
    moved = pltpu.roll(values, by % rows, 0)
    return jnp.where(row >= by if by > 0 else row < rows + by, moved, 0.0)


def head_sum(values):
    return jnp.sum(values, axis=-1, keepdims=True)


def rms(v):
    return lax.rsqrt(jnp.mean(v * v, axis=-1, keepdims=True) + NORM_EPS)


def rms_back(d, v, r, gain):
    vr, gd = v * r, d * gain
    return r * (gd - vr * jnp.mean(vr * gd, axis=-1, keepdims=True)), d * vr


def iotas(shape):
    return lax.broadcasted_iota(jnp.int32, shape, 0), lax.broadcasted_iota(jnp.int32, shape, 1)


def level_masks():
    i, j = iotas((SPAN, SPAN))
    found = []
    for level in range(SPAN.bit_length() - 1):
        a, b = i >> level, j >> level
        found.append(((a >> 1) == (b >> 1)) & ((a & 1) == 1) & ((b & 1) == 0))
    return found


def column(row):
    return jnp.broadcast_to(row, (HEAD, HEAD)).T


def hot(index, count):
    lane = lax.broadcasted_iota(jnp.int32, (HEAD, HEAD), 1).astype(F32)
    return jnp.concatenate(
        [low(jnp.where(lane + float(HEAD * b) == index, 1.0, 0.0)) for b in range(count // HEAD)], axis=1
    )


def prepare(x, taps, unit, row):
    c = x * taps[0:1]
    for o in range(1, taps.shape[0]):
        c += shifted(x, o, row) * taps[o : o + 1]
    u = c * jax.nn.sigmoid(c)
    if unit:
        u = jnp.concatenate(
            [
                u[:, lanes(h)] * lax.rsqrt(head_sum(u[:, lanes(h)] * u[:, lanes(h)]) + UNIT_EPS)
                for h in range(x.shape[1] // HEAD)
            ],
            axis=1,
        )
    return u


def prepare_back(x, d, taps, unit, row):
    moved = [shifted(x, o, row) for o in range(taps.shape[0])]
    c = moved[0] * taps[0:1]
    for o in range(1, taps.shape[0]):
        c += moved[o] * taps[o : o + 1]
    s = jax.nn.sigmoid(c)
    u = c * s
    if unit:
        n = lax.rsqrt(head_sum(u * u) + UNIT_EPS)
        un = u * n
        d = (d - un * head_sum(un * d)) * n
    d = d * (s + u * (1.0 - s))
    grads = [jnp.sum(m * d, axis=0, keepdims=True) for m in moved]
    back = d * taps[0:1]
    for o in range(1, taps.shape[0]):
        back += shifted(d, -o, row) * taps[o : o + 1]
    return back, grads


def delta_block(base, first, refs, gain):
    qkv, beta, state, states, inverses, scores, fresh, mix, mixed, at = refs
    rows = pl.ds(base, SPAN)
    i, j = iotas((SPAN, SPAN))
    masks = level_masks()
    eye = jnp.where(i == j, 1.0, 0.0).astype(F32)
    heads = range(HEADS)

    @pl.when(first)
    def _():
        state[...] = jnp.zeros_like(state)

    strength = beta[rows, :]
    q, k = ([qkv[rows, place(kind, h)] for h in heads] for kind in range(2))
    b = [strength[:, h : h + 1] for h in heads]
    strict = [low(jnp.where(i > j, dot_nt(k[h], k[h]) * b[h], 0.0)) for h in heads]
    for h in heads:
        scores[at, h] = low(jnp.where(i >= j, dot_nt(q[h], k[h]), 0.0))
    zero = jnp.zeros((), BF16)
    inv = [eye - jnp.where(masks[0], strict[h], zero).astype(F32) for h in heads]
    for level in range(1, len(masks)):
        t = [low(inv[h]) for h in heads]
        f = [low(dot(jnp.where(masks[level], strict[h], zero), t[h])) for h in heads]
        inv = [inv[h] - dot(t[h], f[h]) for h in heads]
    for h in heads:
        inverses[at, h] = low(inv[h])
    s = [low(state[h]) for h in heads]
    for h in heads:
        states[at, h] = s[h]
    rest = [low((qkv[rows, place(2, h)].astype(F32) - dot(k[h], s[h])) * b[h]) for h in heads]
    new = [low(dot(inverses[at, h], rest[h])) for h in heads]
    out = [dot(q[h], s[h]) + dot(scores[at, h], new[h]) for h in heads]
    for h in heads:
        fresh[rows, lanes(h)] = new[h]
        state[h] += dot_tn(k[h], new[h])
        mix[rows, lanes(h)] = low(out[h])
        mixed[rows, lanes(h)] = low(out[h] * rms(out[h]) * gain)


def delta_back(base, last, refs, gain):
    (qkv, beta, states, inverses, scores, fresh, mix, d_mixed,
     d_state, d_q, d_k, d_v, d_beta, gain_grad, at) = refs
    rows = pl.ds(base, SPAN)
    i, j = iotas((SPAN, SPAN))
    lane = lax.broadcasted_iota(jnp.int32, (SPAN, 16), 1)
    heads = range(HEADS)

    @pl.when(last)
    def _():
        d_state[...] = jnp.zeros_like(d_state)

    strength = beta[rows, :]
    q, k = ([qkv[rows, place(kind, h)] for h in heads] for kind in range(2))
    e = [fresh[rows, lanes(h)] for h in heads]
    b = [strength[:, h : h + 1] for h in heads]
    kb = [low(k[h].astype(F32) * b[h]) for h in heads]
    do = []
    for h in heads:
        v = mix[rows, lanes(h)].astype(F32)
        d, terms = rms_back(d_mixed[:, lanes(h)], v, rms(v), gain)
        gain_grad[...] += jnp.sum(terms, axis=0, keepdims=True)
        do.append(low(d))
    s = [states[at, h] for h in heads]
    p = [scores[at, h] for h in heads]
    ds = [low(d_state[h]) for h in heads]
    de = [low(dot_tn(p[h], do[h]) + dot(k[h], ds[h])) for h in heads]
    dx = [dot_tn(inverses[at, h], de[h]) for h in heads]
    dxl = [low(dx[h]) for h in heads]
    dp = [low(jnp.where(i >= j, dot_nt(do[h], e[h]), 0.0)) for h in heads]
    da = [low(jnp.where(i > j, -dot_nt(dxl[h], e[h]), 0.0)) for h in heads]
    dkb = [dot(da[h], k[h]) - dot_nt(dxl[h], s[h]) for h in heads]
    beta_grad = jnp.zeros((SPAN, 16), F32)
    for h in heads:
        d_q[rows, lanes(h)] = dot_nt(do[h], s[h]) + dot(dp[h], k[h])
        d_k[rows, lanes(h)] = (
            dkb[h] * b[h] + dot_tn(da[h], kb[h]) + dot_tn(dp[h], q[h]) + dot_nt(e[h], ds[h])
        )
        d_v[rows, lanes(h)] = low(dx[h] * b[h])
        d_state[h] += dot_tn(q[h], do[h]) - dot_tn(kb[h], dxl[h])
        v = qkv[rows, place(2, h)].astype(F32)
        db = head_sum(dkb[h] * k[h].astype(F32) + dx[h] * v)
        beta_grad += jnp.where(lane == h, db, 0.0)
    d_beta[rows, :] = low(beta_grad * strength * (1.0 - strength))


def block_kernel(dims, micro, length, steps, token_rows, *refs):
    (tokens_in, take, back, query_conv, key_conv, value_conv, attn_gain, mlp_gain, out_gain, beta_weight,
     grad_in, qkv_shard, out_shard, feed_shard,
     result, returned, feed_grad, qkv_grad, out_grad, small_grad,
     small_all, qkv_all, out_all, feed_all,
     own, attn_low, pre, qkv, beta, states, inverses, scores, fresh, mix, mixed,
     hidden, total, d_hidden, norm, grad, bufs, w_out, state, d_out, tok_buf, small_buf, small, small_terms,
     gain_out, d_beta, small_out, small_rows, small_shard,
     g_send, g_recv, g_local, s_send, s_recv, t_send, t_recv, t_local, load_sem, ready, *got) = refs
    n = math.prod(dims)
    me = lax.axis_index("fsdp")
    cs = coords_of(dims, me)
    width = own.shape[1]
    share = width // n
    thin = tok_buf.shape[2]
    parts = width // thin
    slots = token_rows // parts
    pieces = 3 * width // WIDE
    blocks = length // SPAN
    rows_total = micro * length
    flat = dims + (share,)

    def g_sems(i):
        return g_send.at[i], g_recv.at[i], g_local.at[i]

    def s_sems(i):
        return s_send.at[i], s_recv.at[i]

    def feed_columns(i, p=0, wide=WIDE):
        return pl.ds(pl.multiple_of(i * WIDE + p * HALF, HALF), wide)

    def feed_gather(i):
        for p, order in enumerate((ZXY, ZYX)):
            yield Gather(dims, cs, feed_shard, feed_all, feed_columns(i, p, HALF), order, g_sems(2 * i + p))

    first_gather = 2 * steps
    attn_gather = [Gather(dims, cs, small_shard, small_all, pl.ds(0, HEAD), ZXY, g_sems(first_gather))]
    for i in range(2 * pieces):
        attn_gather.append(Gather(
            dims, cs, qkv_shard, qkv_all, pl.ds(i * HALF, HALF), (ZXY, ZYX)[i % 2],
            g_sems(first_gather + 1 + i),
        ))
    half_out = width // 2
    out_gather = [
        Gather(dims, cs, out_shard, out_all, pl.ds(i * half_out, half_out), (ZXY, ZYX)[i],
               g_sems(first_gather + 1 + 2 * pieces + i))
        for i in range(2)
    ]
    gathers = [(feed_gather, 0, steps)]

    def slot_views(i, p, wide):
        for s in range(4):
            ref = got[4 * p + s]
            lead = (lax.rem(i, SLOTS[s]),) + (slice(None),) * (len(ref.shape) - 2)
            yield ref.at[lead + (pl.ds(0, wide),)]

    def scatter(i, source, source_at, target, at, wide, sem):
        for p, order in enumerate((CXYZ, CYXZ)):
            yield Scatter(
                dims, cs, source, pl.ds(source_at + p * wide, wide), target,
                pl.ds(pl.multiple_of(at + p * wide, HEAD), wide), order,
                list(slot_views(i, p, wide)), s_sems(sem + p),
            )

    def feed_scatter(i):
        return scatter(i, bufs.at[lax.rem(i, 2)], 0, feed_grad, i * WIDE, HALF, 2 * i)

    rest = width - WIDE
    first_out = 2 * steps

    def out_scatter(i):
        return scatter(steps, bufs.at[steps % 2], 0, out_grad, 0, HALF, first_out)

    def out_scatter_rest(i):
        return scatter(steps + 1, bufs.at[(steps + 1) % 2], 0, out_grad, WIDE, rest // 2, first_out + 2)

    scatters = [
        (feed_scatter, 0, steps), (out_scatter, steps, steps + 1), (out_scatter_rest, steps + 1, steps + 2)
    ]
    first_qkv = first_out + 4

    def qkv_scatter(i):
        yield from scatter(i, bufs.at[i], 0, qkv_grad, i * WIDE, HALF, first_qkv + 2 * i)

    def small_scatter(i):
        yield Scatter(
            dims, cs, small_out, pl.ds(0, HEAD), small_grad, pl.ds(0, HEAD), CXYZ, got[8:12],
            s_sems(first_qkv + 2 * pieces),
        )

    tail_scatters = [(qkv_scatter, 0, pieces), (small_scatter, pieces, pieces + 1)]

    def tokens_to(m):
        return Tokens(n, me, token_rows, tokens_in.at[m], tok_buf.at[m], t_send.at[m], t_recv.at[m], t_local.at[m])

    def tokens_back(m):
        k = micro + m
        return Tokens(n, me, token_rows, tok_buf.at[m], returned.at[m], t_send.at[k], t_recv.at[k], t_local.at[k])

    def load_qkv(i):
        return pltpu.make_async_copy(
            qkv_all.at[:, :, :, :, :, pl.ds(i * WIDE, WIDE)], bufs.at[i], load_sem.at[i]
        )

    load_out = pltpu.make_async_copy(out_all, w_out, load_sem.at[pieces])
    load_small = pltpu.make_async_copy(small_all, small_buf, load_sem.at[pieces + 1])
    load_grad = pltpu.make_async_copy(grad_in, grad, load_sem.at[pieces + 2])
    store_result = pltpu.make_async_copy(grad, result, load_sem.at[pieces + 2])

    def load_feed(t):
        slot = lax.rem(t, 2)
        return pltpu.make_async_copy(
            feed_all.at[:, :, :, :, :, feed_columns(t)], bufs.at[2 + slot], load_sem.at[pieces + 3 + slot]
        )

    load_grad.start()
    small_rows[...] = jnp.zeros_like(small_rows)
    for at, part in (
        (ROW_CONV, query_conv), (ROW_CONV + 4, key_conv), (ROW_CONV + 8, value_conv),
        (ROW_ATTN, attn_gain), (ROW_MLP, mlp_gain), (ROW_OUT, out_gain),
    ):
        small_rows[at : at + part.shape[0], : part.shape[1]] = part[...].astype(F32)
    turned = small_rows[...].T[:share]
    small_rows[:share, :] = turned
    small_rows[:share, ROW_BETA : ROW_BETA + HEADS] = beta_weight[...].astype(F32)
    small_shard[...] = low(small_rows[:share, :])
    greet_all(n, me)
    segment = [(lambda i: [attn_gather[i]], 0, len(attn_gather))]
    last = len(attn_gather) + GATHER_TICKS[-1]
    early = 0
    for t in range(last):
        run_tick(segment, GATHER_TICKS, t)
        if t == TOKENS_AT:
            tokens_to(0).start()
        if t >= len(attn_gather) and (last - 1 - t) % 2 == 0 and early < EARLY:
            run_tick(gathers, FEED_TICKS, early)
            early += 1
        if t == GATHER_TICKS[-1]:
            load_small.start()
        for i in range(pieces):
            if t == 2 * i + 2 + GATHER_TICKS[-1]:
                load_qkv(i).start()
    for m in range(1, micro):
        tokens_to(m).start()
    load_small.wait()
    blockwise = small_buf[...].reshape(width, HEAD).astype(F32)
    small[...] = blockwise.T[:SMALL_ROWS]
    i, j = iotas((width, HEAD))
    few = HEAD // n
    mine = (lax.rem(i, share) < few) & ((i // share) * few + lax.rem(i, share) == j)
    gain_out[...] = jnp.sum(
        jnp.where(mine, blockwise[:, ROW_OUT : ROW_OUT + 1], 0.0), axis=0, keepdims=True
    )
    for i in range(pieces):
        load_qkv(i).wait()

    gain_attn = small[ROW_ATTN : ROW_ATTN + 1, :]
    gain_mlp = small[ROW_MLP : ROW_MLP + 1, :]
    beta_rows = low(small[ROW_BETA : ROW_BETA + 16, :])
    row2 = lax.broadcasted_iota(jnp.int32, (length, 2 * HEAD), 0)
    row1 = lax.broadcasted_iota(jnp.int32, (length, HEAD), 0)

    def project(m, carry):
        run_tick(gathers, FEED_TICKS, early + m)
        tokens_to(m).wait()

        def arrive(t, carry):
            at = pl.ds(pl.multiple_of(t * SPAN, SPAN), SPAN)
            index = column(take[pl.ds(t, 1), :])
            for p in range(parts):
                cols = lanes(p, thin)
                pick = hot(jnp.where(index >= 0.0, index + float(p * slots), -1.0), n * token_rows)
                own[at, cols] = low(dot(pick, tok_buf[m]))
            v = own[at, :].astype(F32)
            attn_low[at, :] = low(v * rms(v) * gain_attn)
            return carry

        lax.fori_loop(m * blocks, (m + 1) * blocks, arrive, 0)
        rows = pl.ds(pl.multiple_of(m * length, SPAN), length)
        a = attn_low[rows, :]
        beta[rows, :] = jax.nn.sigmoid(dot_nt(a, beta_rows))
        for b in range(pieces):
            for kind in range(3):
                cols = lanes(kind, 2 * HEAD)
                wide = slice(b * WIDE + cols.start, b * WIDE + cols.stop)
                x = dot(a, bufs[b, :, :, :, :, :, cols].reshape(width, 2 * HEAD))
                pre[rows, wide] = low(x)
                taps = small[4 * kind : 4 * kind + 4, lanes(b, 2 * HEAD)]
                qkv[rows, wide] = low(prepare(x, taps, kind < 2, row2))
        return carry

    lax.fori_loop(0, micro, project, 0)

    def forward(t, carry):
        run_tick(gathers, FEED_TICKS, early + micro + t)
        for s in range(5):

            @pl.when(t == s)
            def _(s=s):
                for g in out_gather:
                    g.step(s)

        base = pl.multiple_of(t * SPAN, SPAN)
        delta_block(
            base, lax.rem(t, blocks) == 0,
            (qkv, beta, state, states, inverses, scores, fresh, mix, mixed, t), gain_out[...],
        )
        return carry

    lax.fori_loop(0, micro * blocks, forward, 0)
    load_out.start()
    begun = early + micro + micro * blocks
    load_feed(0).start()
    load_out.wait()

    load_grad.wait()

    def live(t):
        return column(take[pl.ds(t, 1), :])[:, 0:1] >= 0.0

    def enter(t, carry):
        at = pl.ds(pl.multiple_of(t * SPAN, SPAN), SPAN)
        v = own[at, :].astype(F32) + dot_nt(mixed[at, :], w_out[...].reshape(width, width))
        hidden[at, :] = v
        norm[at, :] = low(v * rms(v) * gain_mlp)
        grad[at, :] = jnp.where(live(t), grad[at, :], jnp.zeros((), BF16))
        return carry

    lax.fori_loop(0, micro * blocks, enter, 0)
    total[...] = jnp.zeros_like(total)
    d_hidden[...] = jnp.zeros_like(d_hidden)

    def feed(t, carry):
        run_tick(gathers, FEED_TICKS, begun + t)

        @pl.when(t + 1 < steps)
        def _():
            load_feed(t + 1).start()

        load_feed(t).wait()
        w = bufs.at[2 + lax.rem(t, 2)]
        terms = bufs.at[lax.rem(t, 2)]
        gw, uw, dw = (w[:, :, :, :, :, lanes(i, FFW)].reshape(width, FFW) for i in range(3))
        x, g = norm[...], grad[...]
        gate, up = dot(x, gw), dot(x, uw)
        d_act = dot(g, dw)
        s = jax.nn.sigmoid(gate)
        silu = gate * s
        act = low(silu * up)
        d_gate = low(d_act * up * (s + silu * (1.0 - s)))
        d_up = low(d_act * silu)
        for b in range(width // FFW):
            cols = lanes(b, FFW)
            total[:, cols] += dot_nt(act, dw[cols])
            d_hidden[:, cols] += dot_nt(d_gate, gw[cols]) + dot_nt(d_up, uw[cols])
        for i, (left, right) in enumerate(((x, d_gate), (x, d_up), (g, act))):
            terms[:, :, :, :, :, lanes(i, FFW)] = low(dot_tn(left, right)).reshape(flat + (FFW,))
        run_tick(scatters, SCATTER_TICKS, t)
        return carry

    lax.fori_loop(0, steps, feed, 0)
    small_terms[...] = jnp.zeros_like(small_terms)

    def leave(t, carry):
        at = pl.ds(pl.multiple_of(t * SPAN, SPAN), SPAN)
        v, g = hidden[at, :], grad[at, :].astype(F32)
        grad[at, :] = low(jnp.where(live(t), v + total[at, :], 0.0))
        d, terms = rms_back(d_hidden[at, :], v, rms(v), gain_mlp)
        small_terms[ROW_MLP : ROW_MLP + 1, :] += jnp.sum(terms, axis=0, keepdims=True)
        d_hidden[at, :] = g + d
        norm[at, :] = low(g + d)
        return carry

    lax.fori_loop(0, micro * blocks, leave, 0)
    store_result.start()
    d_attn = d_v = norm

    for b in range(width // 256):
        slot, at = (steps + b * 256 // WIDE) % 2, b * 256 % WIDE
        grads = low(dot_tn(d_attn[...], mixed[:, lanes(b, 256)]))
        bufs[slot, :, :, :, :, :, at : at + 256] = grads.reshape(flat + (256,))
        if b == WIDE // 256 - 1:
            run_tick(scatters, SCATTER_TICKS, steps)
    run_tick(scatters, SCATTER_TICKS, steps + 1)
    d_q, d_k = hidden, total
    begun_back = steps + 2

    def backward(turn, carry):
        m = micro - 1 - turn

        def one(b, carry):
            run_tick(scatters, SCATTER_TICKS, begun_back + turn * (blocks + 1) + b)
            t = m * blocks + blocks - 1 - b
            base = pl.multiple_of(t * SPAN, SPAN)
            d_out[...] = dot(d_attn[pl.ds(base, SPAN), :], w_out[...].reshape(width, width))
            delta_back(
                base, b == 0,
                (qkv, beta, states, inverses, scores, fresh, mix, d_out,
                 state, d_q, d_k, d_v, d_beta, small_terms.at[ROW_OUT : ROW_OUT + 1, 0:HEAD], t),
                gain_out[...],
            )
            return carry

        lax.fori_loop(0, blocks, one, 0)
        run_tick(scatters, SCATTER_TICKS, begun_back + turn * (blocks + 1) + blocks)

        @pl.when(turn == 0)
        def _():
            for i in range(pieces):
                load_qkv(i).start()

        rows = pl.ds(pl.multiple_of(m * length, SPAN), length)
        for kind, grads in enumerate((d_q, d_k, d_v)):
            for h in range(HEADS):
                at = place(kind, h)
                back_rows, taps = prepare_back(
                    pre[rows, at].astype(F32), grads[rows, lanes(h)].astype(F32),
                    small[4 * kind : 4 * kind + 4, lanes(h)], kind < 2, row1,
                )
                qkv[rows, at] = low(back_rows)
                for o, terms in enumerate(taps):
                    small_terms[4 * kind + o : 4 * kind + o + 1, lanes(h)] += terms

        @pl.when(turn == 0)
        def _():
            for i in range(pieces):
                load_qkv(i).wait()

        def depart(b, carry):
            at = pl.ds(pl.multiple_of(m * length + b * SPAN, SPAN), SPAN)
            d = dot(d_beta[at, :], beta_rows)
            for i in range(pieces):
                d += dot_nt(qkv[at, lanes(i, WIDE)], bufs[i].reshape(width, WIDE))
            v = own[at, :].astype(F32)
            d, terms = rms_back(d, v, rms(v), gain_attn)
            small_terms[ROW_ATTN : ROW_ATTN + 1, :] += jnp.sum(terms, axis=0, keepdims=True)
            own[at, :] = low(d_hidden[at, :] + d)
            return carry

        lax.fori_loop(0, blocks, depart, 0)
        line = lax.broadcasted_iota(jnp.int32, (HEAD, thin), 0)

        def pack(b, carry):
            pick = hot(column(back[pl.ds(m * (n * token_rows // HEAD) + b, 1), :]), length)
            part = lax.rem(line + b * HEAD, token_rows) // slots
            wide_rows = dot(pick, own[rows, :])
            held = wide_rows[:, lanes(0, thin)]
            for p in range(1, parts):
                held = jnp.where(part == p, wide_rows[:, lanes(p, thin)], held)
            tok_buf[m, pl.ds(pl.multiple_of(b * HEAD, HEAD), HEAD), :] = low(held)
            return carry

        lax.fori_loop(0, n * token_rows // HEAD, pack, 0)
        tokens_back(m).start()
        return carry

    lax.fori_loop(0, micro, backward, 0)

    for peer in axis_peers(dims, cs):
        pl.semaphore_signal(ready, inc=1, device_id=(peer,), device_id_type=MESH)
    for i in range(pieces):
        for kind in range(3):
            cols = lanes(kind, FFW)
            grads = low(dot_tn(attn_low[...], qkv[:, i * WIDE + cols.start : i * WIDE + cols.stop]))
            bufs[i, :, :, :, :, :, cols] = grads.reshape(flat + (FFW,))
        if i == 0:
            pl.semaphore_wait(ready, hops(dims))
        run_tick(tail_scatters, SCATTER_TICKS, i)
    i, j = iotas((HEAD, width))
    mine = (lax.rem(j, share) < few) & ((j // share) * few + lax.rem(j, share) == i)
    gain_column = column(small_terms[ROW_OUT : ROW_OUT + 1, :HEAD])[:, 0:1]
    gain_row = jnp.sum(jnp.where(mine, gain_column, 0.0), axis=0, keepdims=True)
    block = jnp.concatenate(
        [small_terms[:ROW_OUT, :], gain_row, jnp.zeros((1, width), F32),
         dot_tn(d_beta[...], attn_low[...]), jnp.zeros((HEAD - SMALL_ROWS, width), F32)], axis=0,
    )
    small_out[...] = block.T.reshape(flat + (HEAD,))
    for t in range(pieces, pieces + 1 + SCATTER_TICKS[-1]):
        run_tick(tail_scatters, SCATTER_TICKS, t)
    for g in attn_gather + out_gather:
        g.finish()

    def finish(i, carry):
        for g in feed_gather(i):
            g.finish()
        return carry

    lax.fori_loop(0, steps, finish, 0)
    store_result.wait()
    for m in range(micro):
        tokens_back(m).wait()


EARLY = 3
TOKENS_AT = 8


def block_call(tokens, take, back, smalls, grad, qkv_shard, out_shard, feed_shard, micro):
    rows, width = grad.shape
    length, blocks = rows // micro, rows // SPAN
    n = lax.axis_size("fsdp")
    dims = grid_of(n)
    k = hops(dims)
    share = width // n
    steps = feed_shard.shape[1] // WIDE
    pieces = 3 * width // WIDE
    token_rows = tokens.shape[1] // n
    flat = dims + (share,)
    shape = jax.ShapeDtypeStruct
    outs = [
        shape((rows, width), BF16), shape(tokens.shape, BF16),
        shape(feed_shard.shape, F32), shape(qkv_shard.shape, F32), shape(out_shard.shape, F32), shape((share, HEAD), F32),
        shape(flat + (HEAD,), BF16), shape(dims + qkv_shard.shape, BF16), shape(dims + out_shard.shape, BF16),
        shape(dims + feed_shard.shape, BF16),
    ]
    wide, full = pltpu.VMEM((rows, width), BF16), pltpu.VMEM((rows, width), F32)
    square = pltpu.VMEM((blocks, HEADS, SPAN, SPAN), BF16)
    gathers = 2 * steps + 1 + 2 * pieces + 2
    scatters = 2 * steps + 4 + 2 * pieces + 1
    dma = pltpu.SemaphoreType.DMA
    scratch = [
        wide, wide, pltpu.VMEM((rows, 3 * width), BF16), pltpu.VMEM((rows, 3 * width), BF16),
        pltpu.VMEM((rows, 16), F32), pltpu.VMEM((blocks, HEADS, HEAD, HEAD), BF16), square, square, wide, wide, wide,
        full, full, full, wide, wide, pltpu.VMEM((pieces,) + flat + (WIDE,), BF16), pltpu.VMEM(flat + (width,), BF16),
        pltpu.VMEM((HEADS, HEAD, HEAD), F32), pltpu.VMEM((SPAN, width), F32), pltpu.VMEM(tokens.shape, BF16),
        pltpu.VMEM(flat + (HEAD,), BF16), pltpu.VMEM((SMALL_ROWS, width), F32), pltpu.VMEM((SMALL_ROWS // 2, width), F32),
        pltpu.VMEM((1, HEAD), F32), pltpu.VMEM((rows, 16), BF16),
        pltpu.VMEM(flat + (HEAD,), F32), pltpu.VMEM((HEAD, HEAD), F32), pltpu.VMEM((share, HEAD), BF16),
        dma((gathers, k)), dma((gathers, k)), dma((gathers,)), dma((scatters, k)), dma((scatters, k)),
        dma((2 * micro, n)), dma((2 * micro, n)), dma((2 * micro,)), dma((pieces + 5,)), pltpu.SemaphoreType.REGULAR,
    ]
    for order in (CXYZ, CYXZ):
        scratch += scatter_scratch(dims, share, HALF, order, BF16, SLOTS)
    scratch += scatter_scratch(dims, share, HEAD, CXYZ, F32)
    return pl.pallas_call(
        functools.partial(block_kernel, dims, micro, length, steps, token_rows),
        out_shape=outs,
        in_specs=[any_spec()] + [vmem_spec()] * (2 + len(smalls)) + [any_spec()] * 4,
        out_specs=[any_spec()] * 2 + [vmem_spec()] * 4 + [any_spec()] * 4,
        scratch_shapes=scratch,
        compiler_params=pltpu.CompilerParams(
            collective_id=1, has_side_effects=True, vmem_limit_bytes=VMEM_LIMIT
        ),
    )(tokens, take, back, *smalls, grad, qkv_shard, out_shard, feed_shard)[:6]


def picked(index, source):
    hot_rows = index[:, None] == jnp.arange(source.shape[0], dtype=jnp.int32)[None, :]
    return jnp.dot(low(hot_rows), source, preferred_element_type=F32).astype(BF16)


def split_rows(values, parts):
    cut = values.reshape(values.shape[:-1] + (parts, values.shape[-1] // parts))
    return jnp.moveaxis(cut, -2, 0)


def spans(width, size):
    at = 0
    while at < width:
        yield at, min(size, width - at)
        at += size


def local(
    inputs, cotangent, lengths, owners, attn_gain, query_weight, key_weight, value_weight, beta_weight,
    query_conv, key_conv, value_conv, out_gain, out_weight, mlp_gain, gate_weight, up_weight, down_weight,
):
    n = lax.axis_size("fsdp")
    me = lax.axis_index("fsdp")
    micro, _, length, width = inputs.shape
    hidden_units = gate_weight.shape[1]
    share = width // n
    if share % 16:
        return local_thin(
            inputs, cotangent, lengths, owners, attn_gain, query_weight, key_weight, value_weight, beta_weight,
            query_conv, key_conv, value_conv, out_gain, out_weight, mlp_gain, gate_weight, up_weight, down_weight,
        )
    slots = length // n
    parts = 16 // math.gcd(slots, 16)
    thin = width // parts
    token_rows = parts * slots
    i32 = jnp.int32
    devices = jnp.arange(n, dtype=i32)
    slot_ids = jnp.arange(slots, dtype=i32)
    row_ids = jnp.arange(length, dtype=i32)
    part_ids = jnp.arange(parts, dtype=i32)

    before = devices[:, None] < devices[None, :]
    starts = jnp.sum(jnp.where(before[None], lengths[:, :, None], 0), axis=1)
    match = owners[:, None, :] == devices[None, :, None]
    own_start = jnp.sum(jnp.where(match, starts[:, None, :], 0), axis=2)
    own_len = jnp.sum(jnp.where(match, lengths[:, None, :], 0), axis=2)
    mine = devices == me
    my_start = jnp.sum(jnp.where(mine, own_start, 0), axis=1)
    my_len = jnp.sum(jnp.where(mine, own_len, 0), axis=1)

    first = own_start + (me - own_start) % n
    pos = first[:, :, None] + n * slot_ids
    live = pos < (own_start + own_len)[:, :, None]
    send = jnp.where(live, pos // n, -1)[:, :, None, :]
    send = jnp.where(send >= 0, send + (part_ids * length)[:, None], -1)
    outgoing = jnp.stack(
        [picked(send[m].reshape(-1), split_rows(inputs[m, 0], parts).reshape(-1, thin)) for m in range(micro)]
    )

    active = row_ids[None] < my_len[:, None]
    block = (my_start[:, None] + row_ids) % n
    take = jnp.where(active, block * token_rows + row_ids // n, -1).astype(F32).reshape(-1, HEAD)
    grad = cotangent[:, 0].reshape(-1, width)

    back = slot_ids * n + (devices[:, None] - my_start[:, None, None]) % n
    back = jnp.where(back < my_len[:, None, None], back, -1)[:, :, None, :]
    back = (back + jnp.zeros((parts, 1), i32)).astype(F32).reshape(-1, HEAD)

    smalls = (
        query_conv, key_conv, value_conv, attn_gain[None], mlp_gain[None], out_gain[None], beta_weight
    )
    pieces = width // (2 * HEAD)
    qkv_shard = jnp.stack(
        [w.reshape(share, pieces, 2 * HEAD) for w in (query_weight, key_weight, value_weight)], axis=2
    ).reshape(share, 3 * width)
    steps = hidden_units // FFW
    feed_shard = jnp.stack(
        [w.reshape(share, steps, FFW) for w in (gate_weight, up_weight, down_weight.T)], axis=2
    ).reshape(share, 3 * hidden_units)

    result, returned, feed_grad, qkv_grad, out_grad, small_grad = block_call(
        outgoing, take, back, smalls, grad, qkv_shard, out_weight.T, feed_shard, micro
    )

    at_row = row_ids * n + me
    inside = (at_row[None, :, None] >= own_start[:, None, :]) & (
        at_row[None, :, None] < (own_start + own_len)[:, None, :]
    )
    at = devices * token_rows + (at_row[None, :, None] - first[:, None, :]) // n
    put = jnp.sum(jnp.where(inside, at + 1, 0), axis=2) - 1
    sources = jnp.arange(n * token_rows, dtype=i32)
    input_rows = jnp.concatenate(
        [
            jnp.einsum(
                "mrs,msc->mrc", low(jnp.where(put >= 0, put + p * slots, -1)[:, :, None] == sources), returned,
                preferred_element_type=F32,
            ).astype(BF16)
            for p in range(parts)
        ],
        axis=2,
    )

    small_grad = small_grad.T
    feed_grad = feed_grad.reshape(share, steps, 3, FFW)
    gate_grad, up_grad, down_grad = (
        feed_grad[:, :, i].reshape(share, hidden_units) for i in range(3)
    )
    qkv_grad = qkv_grad.reshape(share, pieces, 3, 2 * HEAD)
    query_grad, key_grad, value_grad = (qkv_grad[:, :, i].reshape(share, width) for i in range(3))
    return (
        result.reshape(micro, 1, length, width),
        input_rows.reshape(micro, 1, length, width),
        small_grad[ROW_ATTN],
        query_grad,
        key_grad,
        value_grad,
        small_grad[ROW_BETA : ROW_BETA + HEADS].T,
        small_grad[0:4],
        small_grad[4:8],
        small_grad[8:12],
        small_grad[ROW_OUT, : HEAD // n],
        out_grad.T,
        small_grad[ROW_MLP],
        gate_grad,
        up_grad,
        down_grad.T,
    )


class GatherThin:
    def __init__(self, dims, cs, shard, out, low, width, order, sems):
        self.dims, self.cs, self.order = dims, cs, order
        self.columns = pl.ds(low, width)
        self.shard, self.out = shard.at[:, self.columns], out
        self.send, self.recv, self.local_thin = sems

    def slot(self, stage, delta):
        return sum(self.dims[a] - 1 for a in self.order[:stage]) + delta - 1

    def region(self, stage, cs):
        done = self.order[:stage]
        lead = tuple(slice(None) if k in done else cs[k] for k in range(4))
        return self.out.at[lead + (slice(None), self.columns)]

    def copies(self, stage, incoming):
        axis = self.order[stage]
        for delta in range(1, self.dims[axis]):
            frm = along(self.dims, self.cs, axis, -delta) if incoming else self.cs
            to = along(self.dims, self.cs, axis, delta)
            k = self.slot(stage, delta)
            yield pltpu.make_async_remote_copy(
                src_ref=self.shard if stage == 0 else self.region(stage, self.cs),
                dst_ref=self.region(stage, frm),
                send_sem=self.send.at[k],
                recv_sem=self.recv.at[k],
                device_id=(index_of(self.dims, to),),
                device_id_type=MESH,
            )

    def keep(self):
        return pltpu.make_async_copy(self.shard, self.region(0, self.cs), self.local_thin)

    def step(self, stage):
        if stage == 0:
            self.keep().start()
        if stage == 1:
            self.keep().wait()
        if stage >= 1:
            for c in self.copies(stage - 1, True):
                c.wait_recv()
        if stage < 4:
            for c in self.copies(stage, False):
                c.start()

    def finish(self):
        for stage in range(4):
            for c in self.copies(stage, False):
                c.wait_send()


def pipelined_thin(jobs, stages, lag):
    for tick in range(len(jobs) + (stages - 1) * lag):
        for stage in range(stages):
            i = tick - stage * lag
            if 0 <= i < len(jobs):
                jobs[i].step(stage)


class TokensThin:
    def __init__(self, n, me, a, b, send, recv, local_thin):
        self.n, self.me, self.a, self.b = n, me, a, b
        self.send, self.recv, self.local_thin = send, recv, local_thin

    def copy(self, d, incoming):
        to = lax.rem(self.me + d, self.n)
        frm = lax.rem(self.me - d + self.n, self.n)
        return pltpu.make_async_remote_copy(
            src_ref=self.a.at[to],
            dst_ref=self.b.at[frm if incoming else self.me],
            send_sem=self.send.at[d],
            recv_sem=self.recv.at[d],
            device_id=(to,),
            device_id_type=MESH,
        )

    def keep(self):
        return pltpu.make_async_copy(self.a.at[self.me], self.b.at[self.me], self.local_thin)

    def each(self, act):
        def body(d, carry):
            act(d)
            return carry

        lax.fori_loop(1, self.n, body, 0)

    def start(self):
        self.keep().start()
        self.each(lambda d: self.copy(d, False).start())

    def wait(self):
        self.keep().wait()
        self.each(lambda d: self.copy(d, True).wait_recv())
        self.each(lambda d: self.copy(d, False).wait_send())


def gather_kernel_thin(dims, plan, lag, count, with_tokens, *refs):
    n = math.prod(dims)
    t = 1 if with_tokens else 0
    ins, outs, scr = refs[: count + t], refs[count + t : 2 * (count + t)], refs[2 * (count + t) :]
    send, recv, local_thin = scr[:3]
    me = lax.axis_index("fsdp")
    cs = coords_of(dims, me)
    if with_tokens:
        greet_all(n, me)
        tokens = TokensThin(n, me, ins[count], outs[count], *scr[3:])
        tokens.start()
    else:
        greet_axes(dims, cs)
    jobs = [
        GatherThin(dims, cs, ins[a], outs[a], low, width, order, (send.at[i], recv.at[i], local_thin.at[i]))
        for i, (a, low, width, order) in enumerate(plan)
    ]
    pipelined_thin(jobs, 5, lag)
    for j in jobs:
        j.finish()
    if with_tokens:
        tokens.wait()


def token_sems_thin(n):
    return [
        pltpu.SemaphoreType.DMA((n,)),
        pltpu.SemaphoreType.DMA((n,)),
        pltpu.SemaphoreType.DMA,
    ]


def gather_call_thin(shards, tokens, plan, lag, collective_id):
    n = lax.axis_size("fsdp")
    dims = grid_of(n)
    k = hops(dims)
    ins = list(shards) + ([] if tokens is None else [tokens])
    outs = [jax.ShapeDtypeStruct(dims + s.shape, s.dtype) for s in shards]
    if tokens is not None:
        outs.append(jax.ShapeDtypeStruct(tokens.shape, tokens.dtype))
    m = len(plan)
    return pl.pallas_call(
        functools.partial(gather_kernel_thin, dims, plan, lag, len(shards), tokens is not None),
        out_shape=outs,
        in_specs=[any_spec()] * len(ins),
        out_specs=[any_spec()] * len(outs),
        scratch_shapes=[
            pltpu.SemaphoreType.DMA((m, k)),
            pltpu.SemaphoreType.DMA((m, k)),
            pltpu.SemaphoreType.DMA((m,)),
        ]
        + ([] if tokens is None else token_sems_thin(n)),
        compiler_params=pltpu.CompilerParams(
            collective_id=collective_id, has_side_effects=True, vmem_limit_bytes=VMEM_LIMIT
        ),
    )(*ins)


class ScatterThin:
    def __init__(self, dims, cs, terms, result, low, width, order, scratch, sems):
        self.dims, self.cs, self.order = dims, cs, order
        self.columns = pl.ds(low, width)
        self.terms, self.result = terms, result
        self.own, self.got = scratch[0], scratch[1:]
        self.send, self.recv, self.local_thin = sems

    def slot(self, stage, delta):
        return sum(self.dims[a] - 1 for a in self.order[:stage]) + delta - 1

    def part(self, stage, at):
        axis = self.order[stage]
        if stage == 0:
            lead = tuple(at if k == axis else slice(None) for k in range(4))
            return self.terms.at[lead + (slice(None), self.columns)]
        left = [k for k in range(4) if k not in self.order[:stage]]
        return self.got[stage - 1].at[(0,) + tuple(at if k == axis else slice(None) for k in left)]

    def copies(self, stage):
        axis = self.order[stage]
        for delta in range(1, self.dims[axis]):
            to = along(self.dims, self.cs, axis, delta)
            k = self.slot(stage, delta)
            yield pltpu.make_async_remote_copy(
                src_ref=self.part(stage, to[axis]),
                dst_ref=self.got[stage].at[delta - 1],
                send_sem=self.send.at[k],
                recv_sem=self.recv.at[k],
                device_id=(index_of(self.dims, to),),
                device_id_type=MESH,
            )

    def keep(self):
        return pltpu.make_async_copy(self.part(0, self.cs[self.order[0]]), self.own, self.local_thin)

    def total(self, stage):
        axis = self.order[stage]
        left = [k for k in range(4) if k not in self.order[: stage + 1]]
        shape = [self.dims[k] for k in left]
        got = self.got[stage]
        mine = self.own if stage == 0 else self.part(stage, self.cs[axis])

        def one(i, carry):
            at = tuple(coords_of(shape, i)) if shape else ()
            total = mine[at + (slice(None), slice(None))].astype(F32)
            for delta in range(1, self.dims[axis]):
                total += got[(delta - 1,) + at + (slice(None), slice(None))].astype(F32)
            if left:
                got[(0,) + at + (slice(None), slice(None))] = total.astype(got.dtype)
            else:
                self.result[:, self.columns] = total
            return carry

        lax.fori_loop(0, math.prod(shape), one, 0)

    def step(self, stage):
        if stage == 0:
            self.keep().start()
        if stage == 1:
            self.keep().wait()
        if stage >= 1:
            for c in self.copies(stage - 1):
                c.wait_recv()
            self.total(stage - 1)
        if stage < 4:
            for c in self.copies(stage):
                c.start()

    def finish(self):
        for stage in range(4):
            for c in self.copies(stage):
                c.wait_send()


def scatter_scratch_thin(dims, rows, width, order, dtype):
    left = list(dims)
    out = [pltpu.VMEM(tuple(d for k, d in enumerate(dims) if k != order[0]) + (rows, width), dtype)]
    for s, axis in enumerate(order):
        rest = tuple(dims[k] for k in range(4) if k not in order[: s + 1])
        out.append(pltpu.VMEM((dims[axis] - 1,) + rest + (rows, width), dtype))
    return out


def scatter_kernel_thin(dims, plan, lag, count, with_tokens, *refs):
    n = math.prod(dims)
    t = 1 if with_tokens else 0
    ins, outs, scr = refs[: count + t], refs[count + t : 2 * (count + t)], refs[2 * (count + t) :]
    send, recv, local_thin = scr[:3]
    scr = scr[3:]
    me = lax.axis_index("fsdp")
    cs = coords_of(dims, me)
    if with_tokens:
        greet_all(n, me)
        tokens = TokensThin(n, me, ins[count], outs[count], *scr[:3])
        tokens.start()
        scr = scr[3:]
    else:
        greet_axes(dims, cs)
    jobs = [
        ScatterThin(
            dims, cs, ins[a], outs[a], low, width, order, scr[5 * i : 5 * i + 5],
            (send.at[i], recv.at[i], local_thin.at[i]),
        )
        for i, (a, low, width, order) in enumerate(plan)
    ]
    pipelined_thin(jobs, 5, lag)
    for j in jobs:
        j.finish()
    if with_tokens:
        tokens.wait()


def scatter_call_thin(terms, tokens, plan, lag, collective_id):
    n = lax.axis_size("fsdp")
    dims = grid_of(n)
    k = hops(dims)
    ins = list(terms) + ([] if tokens is None else [tokens])
    outs = [jax.ShapeDtypeStruct(s.shape[4:], F32) for s in terms]
    out_specs = [vmem_spec()] * len(terms)
    if tokens is not None:
        outs.append(jax.ShapeDtypeStruct(tokens.shape, tokens.dtype))
        out_specs.append(any_spec())
    m = len(plan)
    scratch = []
    for a, low, width, order in plan:
        scratch += scatter_scratch_thin(dims, terms[a].shape[4], width, order, terms[a].dtype)
    return pl.pallas_call(
        functools.partial(scatter_kernel_thin, dims, plan, lag, len(terms), tokens is not None),
        out_shape=outs,
        in_specs=[any_spec()] * len(ins),
        out_specs=out_specs,
        scratch_shapes=[
            pltpu.SemaphoreType.DMA((m, k)),
            pltpu.SemaphoreType.DMA((m, k)),
            pltpu.SemaphoreType.DMA((m,)),
        ]
        + ([] if tokens is None else token_sems_thin(n))
        + scratch,
        compiler_params=pltpu.CompilerParams(
            collective_id=collective_id, has_side_effects=True, vmem_limit_bytes=VMEM_LIMIT
        ),
    )(*ins)


def conv_thin(values, taps, row):
    total = values * taps[0:1]
    for c in range(1, taps.shape[0]):
        total += shifted(values, c, row) * taps[c : c + 1]
    return total


def project_thin(own, small, weights, attn_low, pre, queries, keys, values, beta, micro, length):
    width = own.shape[1]
    row = lax.broadcasted_iota(jnp.int32, (length, 2 * HEAD), 0)
    gain = small[ROW_ATTN : ROW_ATTN + 1, :]
    beta_rows = low(small[ROW_BETA : ROW_BETA + 16, :])

    def one(m, carry):
        rows = pl.ds(m * length, length)
        v = own[rows, :].astype(F32)
        r = lax.rsqrt(jnp.mean(v * v, axis=-1, keepdims=True) + NORM_EPS)
        attn_low[rows, :] = low(v * r * gain)
        a = attn_low[rows, :]
        beta[rows, :] = jax.nn.sigmoid(dot_nt(a, beta_rows))
        for kind, out in enumerate((queries, keys, values)):
            for b in range(width // (2 * HEAD)):
                cols = lanes(b, 2 * HEAD)
                wide = slice(kind * width + cols.start, kind * width + cols.stop)
                x = dot(a, weights[:, wide])
                pre[rows, wide] = low(x)
                c = conv_thin(x, small[4 * kind : 4 * kind + 4, cols], row)
                u = c * jax.nn.sigmoid(c)
                if kind == 2:
                    out[rows, cols] = low(u)
                    continue
                for h in range(2):
                    part = u[:, lanes(h)]
                    n = lax.rsqrt(head_sum(part * part) + UNIT_EPS)
                    out[rows, slice(cols.start + h * HEAD, cols.start + (h + 1) * HEAD)] = low(part * n)
        return carry

    lax.fori_loop(0, micro, one, 0)


def delta_block_thin(base, first, refs, gain):
    queries, keys, values, beta, state, states, inverses, scores, fresh, mix, mixed, at = refs
    rows = pl.ds(base, SPAN)
    i, j = iotas((SPAN, SPAN))
    masks = level_masks()
    eye = jnp.where(i == j, 1.0, 0.0).astype(F32)
    heads = range(HEADS)

    @pl.when(first)
    def _():
        state[...] = jnp.zeros_like(state)

    strength = beta[rows, :]
    k = [keys[rows, lanes(h)] for h in heads]
    q = [queries[rows, lanes(h)] for h in heads]
    b = [strength[:, h : h + 1] for h in heads]
    strict = [low(jnp.where(i > j, dot_nt(k[h], k[h]) * b[h], 0.0)) for h in heads]
    for h in heads:
        scores[at, h] = low(jnp.where(i >= j, dot_nt(q[h], k[h]), 0.0))
    zero = jnp.zeros((), BF16)
    inv = [eye - jnp.where(masks[0], strict[h], zero).astype(F32) for h in heads]
    for level in range(1, len(masks)):
        t = [low(inv[h]) for h in heads]
        f = [low(dot(jnp.where(masks[level], strict[h], zero), t[h])) for h in heads]
        inv = [inv[h] - dot(t[h], f[h]) for h in heads]
    for h in heads:
        inverses[at, h] = low(inv[h])
    s = [low(state[h]) for h in heads]
    for h in heads:
        states[at, h] = s[h]
    rest = [low((values[rows, lanes(h)].astype(F32) - dot(k[h], s[h])) * b[h]) for h in heads]
    new = [low(dot(inverses[at, h], rest[h])) for h in heads]
    out = [dot(q[h], s[h]) + dot(scores[at, h], new[h]) for h in heads]
    for h in heads:
        fresh[rows, lanes(h)] = new[h]
        state[h] += dot_tn(k[h], new[h])
        r = lax.rsqrt(jnp.mean(out[h] * out[h], axis=-1, keepdims=True) + NORM_EPS)
        mix[rows, lanes(h)] = low(out[h])
        mixed[rows, lanes(h)] = low(out[h] * r * gain)


def forward_kernel_thin(micro, length, *refs):
    (own, small, weights, out_weight, hidden, attn_low, pre, queries, keys, values, beta,
     states, inverses, scores, fresh, mix, mixed, state) = refs
    project_thin(own, small, weights, attn_low, pre, queries, keys, values, beta, micro, length)
    gain = small[ROW_OUT : ROW_OUT + 1, :HEAD]
    blocks = length // SPAN

    def one(t, carry):
        delta_block_thin(
            pl.multiple_of(t * SPAN, SPAN), lax.rem(t, blocks) == 0,
            (queries, keys, values, beta, state, states, inverses, scores, fresh, mix, mixed, t), gain,
        )
        rows = pl.ds(pl.multiple_of(t * SPAN, SPAN), SPAN)
        hidden[rows, :] = own[rows, :].astype(F32) + dot_nt(mixed[rows, :], out_weight[...])
        return carry

    lax.fori_loop(0, micro * blocks, one, 0)


def forward_call_thin(own, small, weights, out_weight, micro):
    rows, width = own.shape
    length = rows // micro
    blocks = rows // SPAN
    square = jax.ShapeDtypeStruct((blocks, HEADS, SPAN, SPAN), BF16)
    wide = jax.ShapeDtypeStruct((rows, width), BF16)
    outs = [
        jax.ShapeDtypeStruct((rows, width), F32), wide, jax.ShapeDtypeStruct((rows, 3 * width), BF16),
        wide, wide, wide, jax.ShapeDtypeStruct((rows, 16), F32),
        jax.ShapeDtypeStruct((blocks, HEADS, HEAD, HEAD), BF16), square, square, wide, wide, wide,
    ]
    return pl.pallas_call(
        functools.partial(forward_kernel_thin, micro, length),
        out_shape=outs,
        in_specs=[vmem_spec()] * 4,
        out_specs=[vmem_spec()] * len(outs),
        scratch_shapes=[pltpu.VMEM((HEADS, HEAD, HEAD), F32)],
        compiler_params=pltpu.CompilerParams(vmem_limit_bytes=VMEM_LIMIT),
    )(own, small, weights, out_weight)


def feed_kernel_thin(steps, hidden, grad, small, active, w_ref, result, terms, d_hidden, gain_grad, norm, total, d_norm):
    t = pl.program_id(0)
    gain = small[ROW_MLP : ROW_MLP + 1, :]

    @pl.when(t == 0)
    def _():
        v = hidden[...]
        r = lax.rsqrt(jnp.mean(v * v, axis=-1, keepdims=True) + NORM_EPS)
        norm[...] = low(v * r * gain)
        total[...] = v
        d_norm[...] = jnp.zeros_like(d_norm)

    x, g = norm[...], grad[...]
    gw, uw, dw = (w_ref[:, lanes(i, FFW)] for i in range(3))
    gate, up = dot(x, gw), dot(x, uw)
    d_act = dot(g, dw)
    s = jax.nn.sigmoid(gate)
    silu = gate * s
    act = low(silu * up)
    d_gate = low(d_act * up * (s + silu * (1.0 - s)))
    d_up = low(d_act * silu)
    total[...] += dot_nt(act, dw)
    d_norm[...] += dot_nt(d_gate, gw) + dot_nt(d_up, uw)
    terms[:, lanes(0, FFW)] = low(dot_tn(x, d_gate))
    terms[:, lanes(1, FFW)] = low(dot_tn(x, d_up))
    terms[:, lanes(2, FFW)] = low(dot_tn(g, act))

    @pl.when(t == steps - 1)
    def _():
        result[...] = low(jnp.where(active[...] > 0.0, total[...], 0.0))
        v, d = hidden[...], d_norm[...]
        n = v.shape[1]
        r = lax.rsqrt(jnp.mean(v * v, axis=-1, keepdims=True) + NORM_EPS)
        vr = v * r
        gain_grad[...] = jnp.sum(d * vr, axis=0, keepdims=True)
        gd = d * gain
        d_hidden[...] = g.astype(F32) + r * (gd - vr * (jnp.sum(vr * gd, axis=-1, keepdims=True) / n))


def feed_call_thin(hidden, grad, small, active, weights):
    rows, width = hidden.shape
    steps = weights.shape[1] // (3 * FFW)
    whole = lambda *shape: pl.BlockSpec(shape, lambda t: (0,) * len(shape))
    block = pl.BlockSpec((width, 3 * FFW), lambda t: (0, t))
    return pl.pallas_call(
        functools.partial(feed_kernel_thin, steps),
        grid=(steps,),
        out_shape=[
            jax.ShapeDtypeStruct((rows, width), BF16),
            jax.ShapeDtypeStruct(weights.shape, BF16),
            jax.ShapeDtypeStruct((rows, width), F32),
            jax.ShapeDtypeStruct((1, width), F32),
        ],
        in_specs=[whole(rows, width), whole(rows, width), whole(*small.shape), whole(rows, 1), block],
        out_specs=[whole(rows, width), block, whole(rows, width), whole(1, width)],
        scratch_shapes=[
            pltpu.VMEM((rows, width), BF16),
            pltpu.VMEM((rows, width), F32),
            pltpu.VMEM((rows, width), F32),
        ],
        compiler_params=pltpu.CompilerParams(
            vmem_limit_bytes=VMEM_LIMIT, dimension_semantics=("arbitrary",)
        ),
    )(hidden, grad, small, active, weights)


def delta_back_thin(base, last, refs, gain):
    (queries, keys, values, beta, states, inverses, scores, fresh, mix, d_mixed,
     d_state, d_out, d_q, d_k, d_v, d_beta, gain_grad, at) = refs
    rows = pl.ds(base, SPAN)
    i, j = iotas((SPAN, SPAN))
    lane = lax.broadcasted_iota(jnp.int32, (SPAN, 16), 1)
    heads = range(HEADS)

    @pl.when(last)
    def _():
        d_state[...] = jnp.zeros_like(d_state)

    strength = beta[rows, :]
    k = [keys[rows, lanes(h)] for h in heads]
    q = [queries[rows, lanes(h)] for h in heads]
    e = [fresh[rows, lanes(h)] for h in heads]
    b = [strength[:, h : h + 1] for h in heads]
    kb = [low(k[h].astype(F32) * b[h]) for h in heads]
    do = []
    for h in heads:
        v, d = mix[rows, lanes(h)].astype(F32), d_mixed[:, lanes(h)]
        r = lax.rsqrt(jnp.mean(v * v, axis=-1, keepdims=True) + NORM_EPS)
        vr, gd = v * r, d * gain
        gain_grad[...] += jnp.sum(d * vr, axis=0, keepdims=True)
        do.append(low(r * (gd - vr * jnp.mean(vr * gd, axis=-1, keepdims=True))))
    s = [states[at, h] for h in heads]
    p = [scores[at, h] for h in heads]
    ds = [low(d_state[h]) for h in heads]
    de = [low(dot_tn(p[h], do[h]) + dot(k[h], ds[h])) for h in heads]
    dx = [dot_tn(inverses[at, h], de[h]) for h in heads]
    dxl = [low(dx[h]) for h in heads]
    dp = [low(jnp.where(i >= j, dot_nt(do[h], e[h]), 0.0)) for h in heads]
    da = [low(jnp.where(i > j, -dot_nt(dxl[h], e[h]), 0.0)) for h in heads]
    dkb = [dot(da[h], k[h]) - dot_nt(dxl[h], s[h]) for h in heads]
    beta_grad = jnp.zeros((SPAN, 16), F32)
    for h in heads:
        d_q[rows, lanes(h)] = low(dot_nt(do[h], s[h]) + dot(dp[h], k[h]))
        d_k[rows, lanes(h)] = low(
            dkb[h] * b[h] + dot_tn(da[h], kb[h]) + dot_tn(dp[h], q[h]) + dot_nt(e[h], ds[h])
        )
        d_v[rows, lanes(h)] = low(dx[h] * b[h])
        d_state[h] += dot_tn(q[h], do[h]) - dot_tn(kb[h], dxl[h])
        db = head_sum(dkb[h] * k[h].astype(F32) + dx[h] * values[rows, lanes(h)].astype(F32))
        beta_grad += jnp.where(lane == h, db, 0.0)
    d_beta[rows, :] = low(beta_grad * strength * (1.0 - strength))


def backward_kernel_thin(micro, length, *refs):
    (d_hidden, own, small, weights, out_weight, attn_low, pre, queries, keys, values, beta,
     states, inverses, scores, fresh, mix, mixed,
     d_own, qkv_grad, out_grad, small_grad,
     d_state, d_out, d_q, d_k, d_v, d_beta, d_pre, d_attn, gain_grad) = refs
    width = own.shape[1]
    blocks = length // SPAN
    total = micro * blocks
    gain = small[ROW_OUT : ROW_OUT + 1, :HEAD]
    gain_grad[...] = jnp.zeros_like(gain_grad)
    small_grad[...] = jnp.zeros_like(small_grad)
    d_attn[...] = low(d_hidden[...])

    def one(step, carry):
        t = total - 1 - step
        base = pl.multiple_of(t * SPAN, SPAN)
        d_out[...] = dot(d_attn[pl.ds(base, SPAN), :], out_weight[...])
        delta_back_thin(
            base, lax.rem(step, blocks) == 0,
            (queries, keys, values, beta, states, inverses, scores, fresh, mix, d_out,
             d_state, None, d_q, d_k, d_v, d_beta, gain_grad, t), gain,
        )
        return carry

    lax.fori_loop(0, total, one, 0)
    row = lax.broadcasted_iota(jnp.int32, (length, HEAD), 0)

    def conv_back(m, carry):
        rows = pl.ds(m * length, length)
        for kind, grads in enumerate((d_q, d_k, d_v)):
            for h in range(width // HEAD):
                cols = lanes(h)
                wide = slice(kind * width + cols.start, kind * width + cols.stop)
                taps = small[4 * kind : 4 * kind + 4, cols]
                x = pre[rows, wide].astype(F32)
                moved = [shifted(x, c, row) for c in range(4)]
                c = moved[0] * taps[0:1]
                for o in range(1, 4):
                    c += moved[o] * taps[o : o + 1]
                s = jax.nn.sigmoid(c)
                u = c * s
                d = grads[rows, cols].astype(F32)
                if kind < 2:
                    n = lax.rsqrt(head_sum(u * u) + UNIT_EPS)
                    un = u * n
                    d = (d - un * head_sum(un * d)) * n
                d = d * (s + u * (1.0 - s))
                for o in range(4):
                    at = slice(4 * kind + o, 4 * kind + o + 1)
                    small_grad[at, cols] += jnp.sum(moved[o] * d, axis=0, keepdims=True)
                back = d * taps[0:1]
                for o in range(1, 4):
                    back += shifted(d, -o, row) * taps[o : o + 1]
                d_pre[rows, wide] = low(back)
        return carry

    lax.fori_loop(0, micro, conv_back, 0)
    for b in range(width // 256):
        cols = lanes(b, 256)
        out_grad[:, cols] = low(dot_tn(d_attn[...], mixed[:, cols]))
    for b in range(3 * width // 256):
        cols = lanes(b, 256)
        qkv_grad[:, cols] = low(dot_tn(attn_low[...], d_pre[:, cols]))
    beta_rows = low(small[ROW_BETA : ROW_BETA + 16, :])
    small_grad[ROW_BETA : ROW_BETA + 16, :] = dot_tn(d_beta[...], attn_low[...])
    small_grad[ROW_OUT : ROW_OUT + 1, :HEAD] = gain_grad[...]
    attn_gain = small[ROW_ATTN : ROW_ATTN + 1, :]

    def finish(t, carry):
        rows = pl.ds(pl.multiple_of(t * SPAN, SPAN), SPAN)
        d = dot_nt(d_pre[rows, :], weights[...]) + dot(d_beta[rows, :], beta_rows)
        v = own[rows, :].astype(F32)
        r = lax.rsqrt(jnp.mean(v * v, axis=-1, keepdims=True) + NORM_EPS)
        vr, gd = v * r, d * attn_gain
        small_grad[ROW_ATTN : ROW_ATTN + 1, :] += jnp.sum(d * vr, axis=0, keepdims=True)
        d_own[rows, :] = low(d_hidden[rows, :] + r * (gd - vr * jnp.mean(vr * gd, axis=-1, keepdims=True)))
        return carry

    lax.fori_loop(0, total, finish, 0)


def backward_call_thin(d_hidden, own, small, weights, out_weight, saved, micro):
    rows, width = own.shape
    length = rows // micro
    return pl.pallas_call(
        functools.partial(backward_kernel_thin, micro, length),
        out_shape=[
            jax.ShapeDtypeStruct((rows, width), BF16),
            jax.ShapeDtypeStruct((width, 3 * width), BF16),
            jax.ShapeDtypeStruct((width, width), BF16),
            jax.ShapeDtypeStruct((SMALL_ROWS, width), F32),
        ],
        in_specs=[vmem_spec()] * (5 + len(saved)),
        out_specs=[vmem_spec()] * 4,
        scratch_shapes=[
            pltpu.VMEM((HEADS, HEAD, HEAD), F32),
            pltpu.VMEM((SPAN, width), F32),
            pltpu.VMEM((rows, width), BF16),
            pltpu.VMEM((rows, width), BF16),
            pltpu.VMEM((rows, width), BF16),
            pltpu.VMEM((rows, 16), BF16),
            pltpu.VMEM((rows, 3 * width), BF16),
            pltpu.VMEM((rows, width), BF16),
            pltpu.VMEM((1, HEAD), F32),
        ],
        compiler_params=pltpu.CompilerParams(vmem_limit_bytes=VMEM_LIMIT),
    )(d_hidden, own, small, weights, out_weight, *saved)


def local_thin(
    inputs, cotangent, lengths, owners, attn_gain, query_weight, key_weight, value_weight, beta_weight,
    query_conv, key_conv, value_conv, out_gain, out_weight, mlp_gain, gate_weight, up_weight, down_weight,
):
    n = lax.axis_size("fsdp")
    dims = grid_of(n)
    me = lax.axis_index("fsdp")
    micro, _, length, width = inputs.shape
    hidden_units = gate_weight.shape[1]
    share = width // n
    slots = length // n
    per = micro * slots
    parts = 16 // math.gcd(per, 16)
    thin = width // parts
    i32 = jnp.int32
    devices = jnp.arange(n, dtype=i32)
    slot_ids = jnp.arange(slots, dtype=i32)
    row_ids = jnp.arange(length, dtype=i32)
    micros = jnp.arange(micro, dtype=i32)
    part_ids = jnp.arange(parts, dtype=i32)

    before = devices[:, None] < devices[None, :]
    starts = jnp.sum(jnp.where(before[None], lengths[:, :, None], 0), axis=1)
    match = owners[:, None, :] == devices[None, :, None]
    own_start = jnp.sum(jnp.where(match, starts[:, None, :], 0), axis=2)
    own_len = jnp.sum(jnp.where(match, lengths[:, None, :], 0), axis=2)
    mine = devices == me
    my_start = jnp.sum(jnp.where(mine, own_start, 0), axis=1)
    my_len = jnp.sum(jnp.where(mine, own_len, 0), axis=1)

    first = own_start + (me - own_start) % n
    pos = first[:, :, None] + n * slot_ids
    live = pos < (own_start + own_len)[:, :, None]
    send = jnp.where(live, micros[:, None, None] * length + pos // n, -1)
    send = jnp.moveaxis(send, 0, 1)[:, None] + jnp.zeros((1, parts, 1, 1), i32)
    send = jnp.where(send >= 0, send + (part_ids * micro * length)[None, :, None, None], -1)
    rows_in = split_rows(inputs[:, 0].reshape(micro * length, width), parts).reshape(-1, thin)
    outgoing = picked(send.reshape(-1), rows_in).reshape(n, parts * per, thin)

    def row_of(v):
        return jnp.pad(v, ((0, 0), (0, share - v.shape[1])))

    packed = jnp.concatenate([
        query_conv, key_conv, value_conv, attn_gain[None], mlp_gain[None], row_of(out_gain[None]),
        jnp.zeros((1, share), BF16), beta_weight.T, jnp.zeros((SMALL_ROWS - 16 - HEADS, share), BF16),
    ])
    count = SMALL_ROWS * share // HEAD
    packed = jnp.pad(packed.reshape(count, HEAD), ((0, -count % 16), (0, 0)))

    attn_shard = jnp.concatenate([query_weight, key_weight, value_weight, out_weight.T], axis=1)
    steps = hidden_units // FFW
    feed_shard = jnp.stack(
        [w.reshape(share, steps, FFW) for w in (gate_weight, up_weight, down_weight.T)], axis=2
    ).reshape(share, 3 * hidden_units)

    plan = [(0, 0, HEAD, ZXY)]
    for a, (w, size) in enumerate(((4 * width, 512), (3 * hidden_units, 768)), 1):
        for at, wide in spans(w, size):
            plan.append((a, at, wide, (ZXY, ZYX)[len(plan) % 2]))
    small_all, attn_all, feed_all, incoming = gather_call_thin(
        [packed, attn_shard, feed_shard], outgoing, tuple(plan), 2, 1
    )
    small = small_all.reshape(n, -1)[:, : SMALL_ROWS * share].reshape(n, SMALL_ROWS, share)
    small = jnp.moveaxis(small, 1, 0)
    gain_row = small[ROW_OUT, :, : HEAD // n].reshape(1, HEAD)
    small = small.reshape(SMALL_ROWS, width).astype(F32)
    small = lax.dynamic_update_slice(small, gain_row.astype(F32), (ROW_OUT, 0))
    attn_all = attn_all.reshape(width, 4 * width)
    feed_all = feed_all.reshape(width, 3 * hidden_units)
    qkv, out_t = attn_all[:, : 3 * width], attn_all[:, 3 * width :]

    active = row_ids[None] < my_len[:, None]
    block = (my_start[:, None] + row_ids) % n
    at = block * (parts * per) + micros[:, None] * slots + row_ids // n
    take = jnp.where(active, at, -1).reshape(-1)
    flat = incoming.reshape(n * parts * per, thin)
    own = jnp.concatenate(
        [picked(jnp.where(take >= 0, take + p * per, -1), flat) for p in range(parts)], axis=1
    )
    active = active.reshape(-1, 1)
    grad = jnp.where(active, cotangent[:, 0].reshape(-1, width), jnp.zeros((), BF16))

    hidden, *saved = forward_call_thin(own, small, qkv, out_t, micro)
    result, feed_terms, d_hidden, mlp_gain_grad = feed_call_thin(
        hidden, grad, small, active.astype(F32), feed_all
    )
    d_own, qkv_terms, out_terms, small_terms = backward_call_thin(
        d_hidden, own, small, qkv, out_t, saved, micro
    )

    back = slot_ids * n + (devices[:, None, None] - my_start[None, :, None]) % n
    back = jnp.where(back < my_len[None, :, None], back + (micros * length)[None, :, None], -1)
    back = back[:, None] + jnp.zeros((1, parts, 1, 1), i32)
    back = jnp.where(back >= 0, back + (part_ids * micro * length)[None, :, None, None], -1)
    returning = picked(back.reshape(-1), split_rows(d_own, parts).reshape(-1, thin))
    returning = returning.reshape(n, parts * per, thin)

    small_terms = lax.dynamic_update_slice(small_terms, mlp_gain_grad, (ROW_MLP, 0))
    out_gain_terms = jnp.pad(small_terms[ROW_OUT, :HEAD].reshape(n, -1), ((0, 0), (0, share - HEAD // n)))
    small_terms = jnp.concatenate(
        [small_terms[:ROW_OUT].reshape(ROW_OUT, n, share), out_gain_terms[None],
         small_terms[ROW_OUT + 1 :].reshape(SMALL_ROWS - ROW_OUT - 1, n, share)]
    )
    small_terms = jnp.moveaxis(small_terms, 1, 0).reshape(n, count, HEAD)
    small_terms = jnp.pad(small_terms, ((0, 0), (0, -count % 16), (0, 0)))
    terms = [
        small_terms.reshape(dims + small_terms.shape[1:]),
        qkv_terms.reshape(dims + (share, 3 * width)),
        out_terms.reshape(dims + (share, width)),
        feed_terms.reshape(dims + (share, 3 * hidden_units)),
    ]
    plan = []
    for a, size in ((3, 768), (2, 512), (1, 512), (0, HEAD)):
        for lo, wide in spans(terms[a].shape[5], size):
            plan.append((a, lo, wide, (CXYZ, CYXZ)[len(plan) % 2]))
    small_grad, qkv_grad, out_grad, feed_grad, returned = scatter_call_thin(
        terms, returning, tuple(plan), 2, 2
    )

    place = row_ids * n + me
    inside = (place[None, :, None] >= own_start[:, None, :]) & (
        place[None, :, None] < (own_start + own_len)[:, None, :]
    )
    at = devices * (parts * per) + micros[:, None, None] * slots + (place[None, :, None] - first[:, None, :]) // n
    take = (jnp.sum(jnp.where(inside, at + 1, 0), axis=2) - 1).reshape(-1)
    flat = returned.reshape(n * parts * per, thin)
    input_rows = jnp.concatenate(
        [picked(jnp.where(take >= 0, take + p * per, -1), flat) for p in range(parts)], axis=1
    )

    small_grad = small_grad.reshape(-1)[: SMALL_ROWS * share].reshape(SMALL_ROWS, share)
    feed_grad = feed_grad.reshape(share, steps, 3, FFW)
    gate_grad, up_grad, down_grad = (
        feed_grad[:, :, i].reshape(share, hidden_units) for i in range(3)
    )
    return (
        result.reshape(micro, 1, length, width),
        input_rows.reshape(micro, 1, length, width),
        small_grad[ROW_ATTN],
        qkv_grad[:, :width],
        qkv_grad[:, width : 2 * width],
        qkv_grad[:, 2 * width :],
        small_grad[ROW_BETA : ROW_BETA + HEADS].T,
        small_grad[0:4],
        small_grad[4:8],
        small_grad[8:12],
        small_grad[ROW_OUT, : HEAD // n],
        out_grad.T,
        small_grad[ROW_MLP],
        gate_grad,
        up_grad,
        down_grad.T,
    )


def solution(mesh):
    rows, cols, flat = P("fsdp", None), P(None, "fsdp"), P("fsdp")
    data = P(None, "fsdp", None, None)
    return jax.shard_map(
        local,
        mesh=mesh,
        in_specs=(
            data, data, P(), P(), flat, rows, rows, rows, rows, cols, cols, cols, flat, cols, flat, rows, rows, cols,
        ),
        out_specs=(
            data, data, flat, rows, rows, rows, rows, cols, cols, cols, flat, cols, flat, rows, rows, cols,
        ),
        check_vma=False,
    )
```

```python
import functools
import math

import jax
import jax.numpy as jnp
from jax import lax
from jax.experimental import pallas as pl
from jax.experimental.pallas import tpu as pltpu
from jax.sharding import PartitionSpec as P

HEADS = 8
HEAD = 128
SPAN = 128
NORM_EPS = 1e-05
UNIT_EPS = 1e-06
MESH = pl.DeviceIdType.MESH
F32, BF16 = jnp.float32, jnp.bfloat16
VMEM_LIMIT = 62 * 1024 * 1024
FFW = 256
WIDE = 3 * FFW
HALF = WIDE // 2
Z, Y, X, C = 0, 1, 2, 3
ZXY, ZYX = (Z, X, Y, C), (Z, Y, X, C)
CXYZ, CYXZ = (C, X, Y, Z), (C, Y, X, Z)
GATHER_TICKS = (0, 2, 4, 6, 8)
FEED_TICKS = (0, 2, 4, 6, 7)
SCATTER_TICKS = (0, 1, 3, 4, 5)
SLOTS = (4, 5, 3, 2)

ROW_CONV, ROW_ATTN, ROW_MLP, ROW_OUT, ROW_BETA, SMALL_ROWS = 0, 12, 13, 14, 16, 32


def grid_of(n):
    chips = n // 2
    a = 4 if chips % 4 == 0 else 1
    rest = chips // a
    b = 1
    while b * b < rest:
        b *= 2
    return (a, b, rest // b, 2)


def coords_of(dims, index):
    out = []
    for size in reversed(dims):
        out.append(lax.rem(index, size))
        index = index // size
    return out[::-1]


def index_of(dims, cs):
    total = 0
    for size, c in zip(dims, cs):
        total = total * size + c
    return total


def along(dims, cs, axis, delta):
    moved = list(cs)
    moved[axis] = lax.rem(cs[axis] + delta + dims[axis], dims[axis])
    return moved


def axis_peers(dims, cs):
    return [index_of(dims, along(dims, cs, a, d)) for a in range(4) for d in range(1, dims[a])]


def greet_all(n, me):
    barrier = pltpu.get_barrier_semaphore()

    def hello(d, carry):
        pl.semaphore_signal(
            barrier, inc=1, device_id=(lax.rem(me + d, n),), device_id_type=MESH
        )
        return carry

    lax.fori_loop(1, n, hello, 0)
    pl.semaphore_wait(barrier, n - 1)


def hops(dims):
    return sum(d - 1 for d in dims)


def guard(condition, act):
    if isinstance(condition, bool):
        if condition:
            act()
    else:
        pl.when(condition)(act)


def run_tick(segments, ticks, tick):
    for stage in reversed(range(len(ticks))):
        i = tick - ticks[stage]
        for make, first, end in segments:
            inside = (first <= i < end) if isinstance(i, int) else (i >= first) & (i < end)

            def act(make=make, i=i, stage=stage):
                for job in make(i):
                    job.step(stage)

            guard(inside, act)


class Gather:
    def __init__(self, dims, cs, shard, out, columns, order, sems):
        self.dims, self.cs, self.order, self.columns = dims, cs, order, columns
        self.shard, self.out = shard.at[:, columns], out
        self.send, self.recv, self.local = sems

    def slot(self, stage, delta):
        return sum(self.dims[a] - 1 for a in self.order[:stage]) + delta - 1

    def region(self, stage, cs):
        done = self.order[:stage]
        lead = tuple(slice(None) if k in done else cs[k] for k in range(4))
        return self.out.at[lead + (slice(None), self.columns)]

    def copies(self, stage, incoming):
        axis = self.order[stage]
        for delta in range(1, self.dims[axis]):
            frm = along(self.dims, self.cs, axis, -delta) if incoming else self.cs
            to = along(self.dims, self.cs, axis, delta)
            k = self.slot(stage, delta)
            yield pltpu.make_async_remote_copy(
                src_ref=self.shard if stage == 0 else self.region(stage, self.cs),
                dst_ref=self.region(stage, frm),
                send_sem=self.send.at[k],
                recv_sem=self.recv.at[k],
                device_id=(index_of(self.dims, to),),
                device_id_type=MESH,
            )

    def keep(self):
        return pltpu.make_async_copy(self.shard, self.region(0, self.cs), self.local)

    def step(self, stage):
        if stage == 0:
            self.keep().start()
        if stage == 1:
            self.keep().wait()
        if stage >= 1:
            for c in self.copies(stage - 1, True):
                c.wait_recv()
        if stage < 4:
            for c in self.copies(stage, False):
                c.start()

    def finish(self):
        for stage in range(4):
            for c in self.copies(stage, False):
                c.wait_send()


class Scatter:
    def __init__(self, dims, cs, terms, term_columns, result, columns, order, got, sems):
        self.dims, self.cs, self.order = dims, cs, order
        self.term_columns, self.columns = term_columns, columns
        self.terms, self.result, self.got = terms, result, got
        self.send, self.recv = sems

    def slot(self, stage, delta):
        return sum(self.dims[a] - 1 for a in self.order[:stage]) + delta - 1

    def part(self, stage, at):
        axis = self.order[stage]
        if stage == 0:
            lead = tuple(at if k == axis else slice(None) for k in range(4))
            return self.terms.at[lead + (slice(None), self.term_columns)]
        left = [k for k in range(4) if k not in self.order[:stage]]
        return self.got[stage - 1].at[(0,) + tuple(at if k == axis else slice(None) for k in left)]

    def copies(self, stage):
        axis = self.order[stage]
        for delta in range(1, self.dims[axis]):
            to = along(self.dims, self.cs, axis, delta)
            k = self.slot(stage, delta)
            yield pltpu.make_async_remote_copy(
                src_ref=self.part(stage, to[axis]),
                dst_ref=self.got[stage].at[delta - 1],
                send_sem=self.send.at[k],
                recv_sem=self.recv.at[k],
                device_id=(index_of(self.dims, to),),
                device_id_type=MESH,
            )

    def total(self, stage):
        axis = self.order[stage]
        left = [k for k in range(4) if k not in self.order[: stage + 1]]
        shape = [self.dims[k] for k in left]
        got = self.got[stage]
        mine = self.part(stage, self.cs[axis])

        def one(i, carry):
            at = tuple(coords_of(shape, i)) if shape else ()
            total = mine[at + (slice(None), slice(None))].astype(F32)
            for delta in range(1, self.dims[axis]):
                total += got[(delta - 1,) + at + (slice(None), slice(None))].astype(F32)
            if left:
                got[(0,) + at + (slice(None), slice(None))] = total.astype(got.dtype)
            else:
                self.result[:, self.columns] = total
            return carry

        lax.fori_loop(0, math.prod(shape), one, 0)

    def step(self, stage):
        if stage >= 1:
            for c in self.copies(stage - 1):
                c.wait()
            self.total(stage - 1)
        if stage < 4:
            for c in self.copies(stage):
                c.start()


def scatter_scratch(dims, rows, width, order, dtype, slots=None):
    out = []
    for s, axis in enumerate(order):
        rest = tuple(dims[k] for k in range(4) if k not in order[: s + 1])
        lead = () if slots is None else (slots[s],)
        out.append(pltpu.VMEM(lead + (dims[axis] - 1,) + rest + (rows, width), dtype))
    return out


class Tokens:
    def __init__(self, n, me, rows, a, b, send, recv, local):
        self.n, self.me, self.rows, self.a, self.b = n, me, rows, a, b
        self.send, self.recv, self.local = send, recv, local

    def block(self, d):
        return pl.ds(pl.multiple_of(d * self.rows, self.rows), self.rows)

    def copy(self, d, incoming):
        to = lax.rem(self.me + d, self.n)
        frm = lax.rem(self.me - d + self.n, self.n)
        return pltpu.make_async_remote_copy(
            src_ref=self.a.at[self.block(to)],
            dst_ref=self.b.at[self.block(frm if incoming else self.me)],
            send_sem=self.send.at[d],
            recv_sem=self.recv.at[d],
            device_id=(to,),
            device_id_type=MESH,
        )

    def keep(self):
        at = self.block(self.me)
        return pltpu.make_async_copy(self.a.at[at], self.b.at[at], self.local)

    def each(self, act):
        def body(d, carry):
            act(d)
            return carry

        lax.fori_loop(1, self.n, body, 0)

    def start(self):
        self.keep().start()
        self.each(lambda d: self.copy(d, False).start())

    def wait(self):
        self.keep().wait()
        self.each(lambda d: self.copy(d, True).wait_recv())
        self.each(lambda d: self.copy(d, False).wait_send())


def any_spec():
    return pl.BlockSpec(memory_space=pl.ANY)


def vmem_spec():
    return pl.BlockSpec(memory_space=pltpu.VMEM)


def dot(a, b):
    return lax.dot_general(a, b, (((1,), (0,)), ((), ())), preferred_element_type=F32)


def dot_nt(a, b):
    return lax.dot_general(a, b, (((1,), (1,)), ((), ())), preferred_element_type=F32)


def dot_tn(a, b):
    return lax.dot_general(a, b, (((0,), (0,)), ((), ())), preferred_element_type=F32)


def low(v):
    return v.astype(BF16)


def lanes(i, width=HEAD):
    return slice(i * width, (i + 1) * width)


def place(kind, h):
    at = (h // 2) * WIDE + kind * 2 * HEAD + (h % 2) * HEAD
    return slice(at, at + HEAD)


def shifted(values, by, row):
    if by == 0:
        return values
    rows = values.shape[0]
    moved = pltpu.roll(values, by % rows, 0)
    return jnp.where(row >= by if by > 0 else row < rows + by, moved, 0.0)


def head_sum(values):
    return jnp.sum(values, axis=-1, keepdims=True)


def rms(v):
    return lax.rsqrt(jnp.mean(v * v, axis=-1, keepdims=True) + NORM_EPS)


def rms_back(d, v, r, gain):
    vr, gd = v * r, d * gain
    return r * (gd - vr * jnp.mean(vr * gd, axis=-1, keepdims=True)), d * vr


def iotas(shape):
    return lax.broadcasted_iota(jnp.int32, shape, 0), lax.broadcasted_iota(jnp.int32, shape, 1)


def level_masks():
    i, j = iotas((SPAN, SPAN))
    found = []
    for level in range(SPAN.bit_length() - 1):
        a, b = i >> level, j >> level
        found.append(((a >> 1) == (b >> 1)) & ((a & 1) == 1) & ((b & 1) == 0))
    return found


def column(row):
    return jnp.broadcast_to(row, (HEAD, HEAD)).T


def hot(index, count):
    lane = lax.broadcasted_iota(jnp.int32, (HEAD, HEAD), 1).astype(F32)
    return jnp.concatenate(
        [low(jnp.where(lane + float(HEAD * b) == index, 1.0, 0.0)) for b in range(count // HEAD)], axis=1
    )


def prepare(x, taps, unit, row):
    c = x * taps[0:1]
    for o in range(1, taps.shape[0]):
        c += shifted(x, o, row) * taps[o : o + 1]
    u = c * jax.nn.sigmoid(c)
    if unit:
        u = jnp.concatenate(
            [
                u[:, lanes(h)] * lax.rsqrt(head_sum(u[:, lanes(h)] * u[:, lanes(h)]) + UNIT_EPS)
                for h in range(x.shape[1] // HEAD)
            ],
            axis=1,
        )
    return u


def prepare_back(x, d, taps, unit, row):
    moved = [shifted(x, o, row) for o in range(taps.shape[0])]
    c = moved[0] * taps[0:1]
    for o in range(1, taps.shape[0]):
        c += moved[o] * taps[o : o + 1]
    s = jax.nn.sigmoid(c)
    u = c * s
    if unit:
        n = lax.rsqrt(head_sum(u * u) + UNIT_EPS)
        un = u * n
        d = (d - un * head_sum(un * d)) * n
    d = d * (s + u * (1.0 - s))
    grads = [jnp.sum(m * d, axis=0, keepdims=True) for m in moved]
    back = d * taps[0:1]
    for o in range(1, taps.shape[0]):
        back += shifted(d, -o, row) * taps[o : o + 1]
    return back, grads


def delta_block(base, first, refs, gain):
    qkv, beta, state, states, inverses, scores, fresh, mix, mixed, at = refs
    rows = pl.ds(base, SPAN)
    i, j = iotas((SPAN, SPAN))
    masks = level_masks()
    eye = jnp.where(i == j, 1.0, 0.0).astype(F32)
    heads = range(HEADS)

    @pl.when(first)
    def _():
        state[...] = jnp.zeros_like(state)

    strength = beta[rows, :]
    q, k = ([qkv[rows, place(kind, h)] for h in heads] for kind in range(2))
    b = [strength[:, h : h + 1] for h in heads]
    strict = [low(jnp.where(i > j, dot_nt(k[h], k[h]) * b[h], 0.0)) for h in heads]
    for h in heads:
        scores[at, h] = low(jnp.where(i >= j, dot_nt(q[h], k[h]), 0.0))
    zero = jnp.zeros((), BF16)
    inv = [eye - jnp.where(masks[0], strict[h], zero).astype(F32) for h in heads]
    for level in range(1, len(masks)):
        t = [low(inv[h]) for h in heads]
        f = [low(dot(jnp.where(masks[level], strict[h], zero), t[h])) for h in heads]
        inv = [inv[h] - dot(t[h], f[h]) for h in heads]
    for h in heads:
        inverses[at, h] = low(inv[h])
    s = [low(state[h]) for h in heads]
    for h in heads:
        states[at, h] = s[h]
    rest = [low((qkv[rows, place(2, h)].astype(F32) - dot(k[h], s[h])) * b[h]) for h in heads]
    new = [low(dot(inverses[at, h], rest[h])) for h in heads]
    out = [dot(q[h], s[h]) + dot(scores[at, h], new[h]) for h in heads]
    for h in heads:
        fresh[rows, lanes(h)] = new[h]
        state[h] += dot_tn(k[h], new[h])
        mix[rows, lanes(h)] = low(out[h])
        mixed[rows, lanes(h)] = low(out[h] * rms(out[h]) * gain)


def delta_back(base, last, refs, gain):
    (qkv, beta, states, inverses, scores, fresh, mix, d_mixed,
     d_state, d_q, d_k, d_v, d_beta, gain_grad, at) = refs
    rows = pl.ds(base, SPAN)
    i, j = iotas((SPAN, SPAN))
    lane = lax.broadcasted_iota(jnp.int32, (SPAN, 16), 1)
    heads = range(HEADS)

    @pl.when(last)
    def _():
        d_state[...] = jnp.zeros_like(d_state)

    strength = beta[rows, :]
    q, k = ([qkv[rows, place(kind, h)] for h in heads] for kind in range(2))
    e = [fresh[rows, lanes(h)] for h in heads]
    b = [strength[:, h : h + 1] for h in heads]
    kb = [low(k[h].astype(F32) * b[h]) for h in heads]
    do = []
    for h in heads:
        v = mix[rows, lanes(h)].astype(F32)
        d, terms = rms_back(d_mixed[:, lanes(h)], v, rms(v), gain)
        gain_grad[...] += jnp.sum(terms, axis=0, keepdims=True)
        do.append(low(d))
    s = [states[at, h] for h in heads]
    p = [scores[at, h] for h in heads]
    ds = [low(d_state[h]) for h in heads]
    de = [low(dot_tn(p[h], do[h]) + dot(k[h], ds[h])) for h in heads]
    dx = [dot_tn(inverses[at, h], de[h]) for h in heads]
    dxl = [low(dx[h]) for h in heads]
    dp = [low(jnp.where(i >= j, dot_nt(do[h], e[h]), 0.0)) for h in heads]
    da = [low(jnp.where(i > j, -dot_nt(dxl[h], e[h]), 0.0)) for h in heads]
    dkb = [dot(da[h], k[h]) - dot_nt(dxl[h], s[h]) for h in heads]
    beta_grad = jnp.zeros((SPAN, 16), F32)
    for h in heads:
        d_q[rows, lanes(h)] = dot_nt(do[h], s[h]) + dot(dp[h], k[h])
        d_k[rows, lanes(h)] = (
            dkb[h] * b[h] + dot_tn(da[h], kb[h]) + dot_tn(dp[h], q[h]) + dot_nt(e[h], ds[h])
        )
        d_v[rows, lanes(h)] = low(dx[h] * b[h])
        d_state[h] += dot_tn(q[h], do[h]) - dot_tn(kb[h], dxl[h])
        v = qkv[rows, place(2, h)].astype(F32)
        db = head_sum(dkb[h] * k[h].astype(F32) + dx[h] * v)
        beta_grad += jnp.where(lane == h, db, 0.0)
    d_beta[rows, :] = low(beta_grad * strength * (1.0 - strength))


def block_kernel(dims, micro, length, steps, token_rows, *refs):
    (tokens_in, take, back, query_conv, key_conv, value_conv, attn_gain, mlp_gain, out_gain, beta_weight,
     grad_in, qkv_shard, out_shard, feed_shard,
     result, returned, feed_grad, qkv_grad, out_grad, small_grad,
     small_all, qkv_all, out_all, feed_all,
     own, attn_low, pre, qkv, beta, states, inverses, scores, fresh, mix, mixed,
     hidden, total, d_hidden, norm, grad, bufs, w_out, state, d_out, tok_buf, small_buf, small, small_terms,
     gain_out, d_beta, small_out, small_rows, small_shard,
     g_send, g_recv, g_local, s_send, s_recv, t_send, t_recv, t_local, load_sem, ready, *got) = refs
    n = math.prod(dims)
    me = lax.axis_index("fsdp")
    cs = coords_of(dims, me)
    width = own.shape[1]
    share = width // n
    thin = tok_buf.shape[2]
    parts = width // thin
    slots = token_rows // parts
    pieces = 3 * width // WIDE
    blocks = length // SPAN
    rows_total = micro * length
    flat = dims + (share,)

    def g_sems(i):
        return g_send.at[i], g_recv.at[i], g_local.at[i]

    def s_sems(i):
        return s_send.at[i], s_recv.at[i]

    def feed_columns(i, p=0, wide=WIDE):
        return pl.ds(pl.multiple_of(i * WIDE + p * HALF, HALF), wide)

    def feed_gather(i):
        for p, order in enumerate((ZXY, ZYX)):
            yield Gather(dims, cs, feed_shard, feed_all, feed_columns(i, p, HALF), order, g_sems(2 * i + p))

    first_gather = 2 * steps
    attn_gather = [Gather(dims, cs, small_shard, small_all, pl.ds(0, HEAD), ZXY, g_sems(first_gather))]
    for i in range(2 * pieces):
        attn_gather.append(Gather(
            dims, cs, qkv_shard, qkv_all, pl.ds(i * HALF, HALF), (ZXY, ZYX)[i % 2],
            g_sems(first_gather + 1 + i),
        ))
    half_out = width // 2
    out_gather = [
        Gather(dims, cs, out_shard, out_all, pl.ds(i * half_out, half_out), (ZXY, ZYX)[i],
               g_sems(first_gather + 1 + 2 * pieces + i))
        for i in range(2)
    ]
    gathers = [(feed_gather, 0, steps)]

    def slot_views(i, p, wide):
        for s in range(4):
            ref = got[4 * p + s]
            lead = (lax.rem(i, SLOTS[s]),) + (slice(None),) * (len(ref.shape) - 2)
            yield ref.at[lead + (pl.ds(0, wide),)]

    def scatter(i, source, source_at, target, at, wide, sem):
        for p, order in enumerate((CXYZ, CYXZ)):
            yield Scatter(
                dims, cs, source, pl.ds(source_at + p * wide, wide), target,
                pl.ds(pl.multiple_of(at + p * wide, HEAD), wide), order,
                list(slot_views(i, p, wide)), s_sems(sem + p),
            )

    def feed_scatter(i):
        return scatter(i, bufs.at[lax.rem(i, 2)], 0, feed_grad, i * WIDE, HALF, 2 * i)

    rest = width - WIDE
    first_out = 2 * steps

    def out_scatter(i):
        return scatter(steps, bufs.at[steps % 2], 0, out_grad, 0, HALF, first_out)

    def out_scatter_rest(i):
        return scatter(steps + 1, bufs.at[(steps + 1) % 2], 0, out_grad, WIDE, rest // 2, first_out + 2)

    scatters = [
        (feed_scatter, 0, steps), (out_scatter, steps, steps + 1), (out_scatter_rest, steps + 1, steps + 2)
    ]
    first_qkv = first_out + 4

    def qkv_scatter(i):
        yield from scatter(i, bufs.at[i], 0, qkv_grad, i * WIDE, HALF, first_qkv + 2 * i)

    def small_scatter(i):
        yield Scatter(
            dims, cs, small_out, pl.ds(0, HEAD), small_grad, pl.ds(0, HEAD), CXYZ, got[8:12],
            s_sems(first_qkv + 2 * pieces),
        )

    tail_scatters = [(qkv_scatter, 0, pieces), (small_scatter, pieces, pieces + 1)]

    def tokens_to(m):
        return Tokens(n, me, token_rows, tokens_in.at[m], tok_buf.at[m], t_send.at[m], t_recv.at[m], t_local.at[m])

    def tokens_back(m):
        k = micro + m
        return Tokens(n, me, token_rows, tok_buf.at[m], returned.at[m], t_send.at[k], t_recv.at[k], t_local.at[k])

    def load_qkv(i):
        return pltpu.make_async_copy(
            qkv_all.at[:, :, :, :, :, pl.ds(i * WIDE, WIDE)], bufs.at[i], load_sem.at[i]
        )

    load_out = pltpu.make_async_copy(out_all, w_out, load_sem.at[pieces])
    load_small = pltpu.make_async_copy(small_all, small_buf, load_sem.at[pieces + 1])
    load_grad = pltpu.make_async_copy(grad_in, grad, load_sem.at[pieces + 2])
    store_result = pltpu.make_async_copy(grad, result, load_sem.at[pieces + 2])

    def load_feed(t):
        slot = lax.rem(t, 2)
        return pltpu.make_async_copy(
            feed_all.at[:, :, :, :, :, feed_columns(t)], bufs.at[2 + slot], load_sem.at[pieces + 3 + slot]
        )

    load_grad.start()
    small_rows[...] = jnp.zeros_like(small_rows)
    for at, part in (
        (ROW_CONV, query_conv), (ROW_CONV + 4, key_conv), (ROW_CONV + 8, value_conv),
        (ROW_ATTN, attn_gain), (ROW_MLP, mlp_gain), (ROW_OUT, out_gain),
    ):
        small_rows[at : at + part.shape[0], : part.shape[1]] = part[...].astype(F32)
    turned = small_rows[...].T[:share]
    small_rows[:share, :] = turned
    small_rows[:share, ROW_BETA : ROW_BETA + HEADS] = beta_weight[...].astype(F32)
    small_shard[...] = low(small_rows[:share, :])
    greet_all(n, me)
    segment = [(lambda i: [attn_gather[i]], 0, len(attn_gather))]
    last = len(attn_gather) + GATHER_TICKS[-1]
    early = 0
    for t in range(last):
        run_tick(segment, GATHER_TICKS, t)
        if t == TOKENS_AT:
            tokens_to(0).start()
        if t >= len(attn_gather) and (last - 1 - t) % 2 == 0 and early < EARLY:
            run_tick(gathers, FEED_TICKS, early)
            early += 1
        if t == GATHER_TICKS[-1]:
            load_small.start()
        for i in range(pieces):
            if t == 2 * i + 2 + GATHER_TICKS[-1]:
                load_qkv(i).start()
    for m in range(1, micro):
        tokens_to(m).start()
    load_small.wait()
    blockwise = small_buf[...].reshape(width, HEAD).astype(F32)
    small[...] = blockwise.T[:SMALL_ROWS]
    i, j = iotas((width, HEAD))
    few = HEAD // n
    mine = (lax.rem(i, share) < few) & ((i // share) * few + lax.rem(i, share) == j)
    gain_out[...] = jnp.sum(
        jnp.where(mine, blockwise[:, ROW_OUT : ROW_OUT + 1], 0.0), axis=0, keepdims=True
    )
    for i in range(pieces):
        load_qkv(i).wait()

    gain_attn = small[ROW_ATTN : ROW_ATTN + 1, :]
    gain_mlp = small[ROW_MLP : ROW_MLP + 1, :]
    beta_rows = low(small[ROW_BETA : ROW_BETA + 16, :])
    row2 = lax.broadcasted_iota(jnp.int32, (length, 2 * HEAD), 0)
    row1 = lax.broadcasted_iota(jnp.int32, (length, HEAD), 0)

    def project(m, carry):
        run_tick(gathers, FEED_TICKS, early + m)
        tokens_to(m).wait()

        def arrive(t, carry):
            at = pl.ds(pl.multiple_of(t * SPAN, SPAN), SPAN)
            index = column(take[pl.ds(t, 1), :])
            for p in range(parts):
                cols = lanes(p, thin)
                pick = hot(jnp.where(index >= 0.0, index + float(p * slots), -1.0), n * token_rows)
                own[at, cols] = low(dot(pick, tok_buf[m]))
            v = own[at, :].astype(F32)
            attn_low[at, :] = low(v * rms(v) * gain_attn)
            return carry

        lax.fori_loop(m * blocks, (m + 1) * blocks, arrive, 0)
        rows = pl.ds(pl.multiple_of(m * length, SPAN), length)
        a = attn_low[rows, :]
        beta[rows, :] = jax.nn.sigmoid(dot_nt(a, beta_rows))
        for b in range(pieces):
            for kind in range(3):
                cols = lanes(kind, 2 * HEAD)
                wide = slice(b * WIDE + cols.start, b * WIDE + cols.stop)
                x = dot(a, bufs[b, :, :, :, :, :, cols].reshape(width, 2 * HEAD))
                pre[rows, wide] = low(x)
                taps = small[4 * kind : 4 * kind + 4, lanes(b, 2 * HEAD)]
                qkv[rows, wide] = low(prepare(x, taps, kind < 2, row2))
        return carry

    lax.fori_loop(0, micro, project, 0)

    def forward(t, carry):
        run_tick(gathers, FEED_TICKS, early + micro + t)
        for s in range(5):

            @pl.when(t == s)
            def _(s=s):
                for g in out_gather:
                    g.step(s)

        base = pl.multiple_of(t * SPAN, SPAN)
        delta_block(
            base, lax.rem(t, blocks) == 0,
            (qkv, beta, state, states, inverses, scores, fresh, mix, mixed, t), gain_out[...],
        )
        return carry

    lax.fori_loop(0, micro * blocks, forward, 0)
    load_out.start()
    begun = early + micro + micro * blocks
    load_feed(0).start()
    load_out.wait()

    load_grad.wait()

    def live(t):
        return column(take[pl.ds(t, 1), :])[:, 0:1] >= 0.0

    def enter(t, carry):
        at = pl.ds(pl.multiple_of(t * SPAN, SPAN), SPAN)
        v = own[at, :].astype(F32) + dot_nt(mixed[at, :], w_out[...].reshape(width, width))
        hidden[at, :] = v
        norm[at, :] = low(v * rms(v) * gain_mlp)
        grad[at, :] = jnp.where(live(t), grad[at, :], jnp.zeros((), BF16))
        return carry

    lax.fori_loop(0, micro * blocks, enter, 0)
    total[...] = jnp.zeros_like(total)
    d_hidden[...] = jnp.zeros_like(d_hidden)

    def feed(t, carry):
        run_tick(gathers, FEED_TICKS, begun + t)

        @pl.when(t + 1 < steps)
        def _():
            load_feed(t + 1).start()

        load_feed(t).wait()
        w = bufs.at[2 + lax.rem(t, 2)]
        terms = bufs.at[lax.rem(t, 2)]
        gw, uw, dw = (w[:, :, :, :, :, lanes(i, FFW)].reshape(width, FFW) for i in range(3))
        x, g = norm[...], grad[...]
        gate, up = dot(x, gw), dot(x, uw)
        d_act = dot(g, dw)
        s = jax.nn.sigmoid(gate)
        silu = gate * s
        act = low(silu * up)
        d_gate = low(d_act * up * (s + silu * (1.0 - s)))
        d_up = low(d_act * silu)
        for b in range(width // FFW):
            cols = lanes(b, FFW)
            total[:, cols] += dot_nt(act, dw[cols])
            d_hidden[:, cols] += dot_nt(d_gate, gw[cols]) + dot_nt(d_up, uw[cols])
        for i, (left, right) in enumerate(((x, d_gate), (x, d_up), (g, act))):
            terms[:, :, :, :, :, lanes(i, FFW)] = low(dot_tn(left, right)).reshape(flat + (FFW,))
        run_tick(scatters, SCATTER_TICKS, t)
        return carry

    lax.fori_loop(0, steps, feed, 0)
    small_terms[...] = jnp.zeros_like(small_terms)

    def leave(t, carry):
        at = pl.ds(pl.multiple_of(t * SPAN, SPAN), SPAN)
        v, g = hidden[at, :], grad[at, :].astype(F32)
        grad[at, :] = low(jnp.where(live(t), v + total[at, :], 0.0))
        d, terms = rms_back(d_hidden[at, :], v, rms(v), gain_mlp)
        small_terms[ROW_MLP : ROW_MLP + 1, :] += jnp.sum(terms, axis=0, keepdims=True)
        d_hidden[at, :] = g + d
        norm[at, :] = low(g + d)
        return carry

    lax.fori_loop(0, micro * blocks, leave, 0)
    store_result.start()
    d_attn = d_v = norm

    for b in range(width // 256):
        slot, at = (steps + b * 256 // WIDE) % 2, b * 256 % WIDE
        grads = low(dot_tn(d_attn[...], mixed[:, lanes(b, 256)]))
        bufs[slot, :, :, :, :, :, at : at + 256] = grads.reshape(flat + (256,))
        if b == WIDE // 256 - 1:
            run_tick(scatters, SCATTER_TICKS, steps)
    run_tick(scatters, SCATTER_TICKS, steps + 1)
    d_q, d_k = hidden, total
    begun_back = steps + 2

    def backward(turn, carry):
        m = micro - 1 - turn

        def one(b, carry):
            run_tick(scatters, SCATTER_TICKS, begun_back + turn * (blocks + 1) + b)
            t = m * blocks + blocks - 1 - b
            base = pl.multiple_of(t * SPAN, SPAN)
            d_out[...] = dot(d_attn[pl.ds(base, SPAN), :], w_out[...].reshape(width, width))
            delta_back(
                base, b == 0,
                (qkv, beta, states, inverses, scores, fresh, mix, d_out,
                 state, d_q, d_k, d_v, d_beta, small_terms.at[ROW_OUT : ROW_OUT + 1, 0:HEAD], t),
                gain_out[...],
            )
            return carry

        lax.fori_loop(0, blocks, one, 0)
        run_tick(scatters, SCATTER_TICKS, begun_back + turn * (blocks + 1) + blocks)

        @pl.when(turn == 0)
        def _():
            for i in range(pieces):
                load_qkv(i).start()

        rows = pl.ds(pl.multiple_of(m * length, SPAN), length)
        for kind, grads in enumerate((d_q, d_k, d_v)):
            for h in range(HEADS):
                at = place(kind, h)
                back_rows, taps = prepare_back(
                    pre[rows, at].astype(F32), grads[rows, lanes(h)].astype(F32),
                    small[4 * kind : 4 * kind + 4, lanes(h)], kind < 2, row1,
                )
                qkv[rows, at] = low(back_rows)
                for o, terms in enumerate(taps):
                    small_terms[4 * kind + o : 4 * kind + o + 1, lanes(h)] += terms

        @pl.when(turn == 0)
        def _():
            for i in range(pieces):
                load_qkv(i).wait()

        def depart(b, carry):
            at = pl.ds(pl.multiple_of(m * length + b * SPAN, SPAN), SPAN)
            d = dot(d_beta[at, :], beta_rows)
            for i in range(pieces):
                d += dot_nt(qkv[at, lanes(i, WIDE)], bufs[i].reshape(width, WIDE))
            v = own[at, :].astype(F32)
            d, terms = rms_back(d, v, rms(v), gain_attn)
            small_terms[ROW_ATTN : ROW_ATTN + 1, :] += jnp.sum(terms, axis=0, keepdims=True)
            own[at, :] = low(d_hidden[at, :] + d)
            return carry

        lax.fori_loop(0, blocks, depart, 0)
        line = lax.broadcasted_iota(jnp.int32, (HEAD, thin), 0)

        def pack(b, carry):
            pick = hot(column(back[pl.ds(m * (n * token_rows // HEAD) + b, 1), :]), length)
            part = lax.rem(line + b * HEAD, token_rows) // slots
            wide_rows = dot(pick, own[rows, :])
            held = wide_rows[:, lanes(0, thin)]
            for p in range(1, parts):
                held = jnp.where(part == p, wide_rows[:, lanes(p, thin)], held)
            tok_buf[m, pl.ds(pl.multiple_of(b * HEAD, HEAD), HEAD), :] = low(held)
            return carry

        lax.fori_loop(0, n * token_rows // HEAD, pack, 0)
        tokens_back(m).start()
        return carry

    lax.fori_loop(0, micro, backward, 0)

    for peer in axis_peers(dims, cs):
        pl.semaphore_signal(ready, inc=1, device_id=(peer,), device_id_type=MESH)
    for i in range(pieces):
        for kind in range(3):
            cols = lanes(kind, FFW)
            grads = low(dot_tn(attn_low[...], qkv[:, i * WIDE + cols.start : i * WIDE + cols.stop]))
            bufs[i, :, :, :, :, :, cols] = grads.reshape(flat + (FFW,))
        if i == 0:
            pl.semaphore_wait(ready, hops(dims))
        run_tick(tail_scatters, SCATTER_TICKS, i)
    i, j = iotas((HEAD, width))
    mine = (lax.rem(j, share) < few) & ((j // share) * few + lax.rem(j, share) == i)
    gain_column = column(small_terms[ROW_OUT : ROW_OUT + 1, :HEAD])[:, 0:1]
    gain_row = jnp.sum(jnp.where(mine, gain_column, 0.0), axis=0, keepdims=True)
    block = jnp.concatenate(
        [small_terms[:ROW_OUT, :], gain_row, jnp.zeros((1, width), F32),
         dot_tn(d_beta[...], attn_low[...]), jnp.zeros((HEAD - SMALL_ROWS, width), F32)], axis=0,
    )
    small_out[...] = block.T.reshape(flat + (HEAD,))
    for t in range(pieces, pieces + 1 + SCATTER_TICKS[-1]):
        run_tick(tail_scatters, SCATTER_TICKS, t)
    for g in attn_gather + out_gather:
        g.finish()

    def finish(i, carry):
        for g in feed_gather(i):
            g.finish()
        return carry

    lax.fori_loop(0, steps, finish, 0)
    store_result.wait()
    for m in range(micro):
        tokens_back(m).wait()


EARLY = 4
TOKENS_AT = 6


def block_call(tokens, take, back, smalls, grad, qkv_shard, out_shard, feed_shard, micro):
    rows, width = grad.shape
    length, blocks = rows // micro, rows // SPAN
    n = lax.axis_size("fsdp")
    dims = grid_of(n)
    k = hops(dims)
    share = width // n
    steps = feed_shard.shape[1] // WIDE
    pieces = 3 * width // WIDE
    token_rows = tokens.shape[1] // n
    flat = dims + (share,)
    shape = jax.ShapeDtypeStruct
    outs = [
        shape((rows, width), BF16), shape(tokens.shape, BF16),
        shape(feed_shard.shape, F32), shape(qkv_shard.shape, F32), shape(out_shard.shape, F32), shape((share, HEAD), F32),
        shape(flat + (HEAD,), BF16), shape(dims + qkv_shard.shape, BF16), shape(dims + out_shard.shape, BF16),
        shape(dims + feed_shard.shape, BF16),
    ]
    wide, full = pltpu.VMEM((rows, width), BF16), pltpu.VMEM((rows, width), F32)
    square = pltpu.VMEM((blocks, HEADS, SPAN, SPAN), BF16)
    gathers = 2 * steps + 1 + 2 * pieces + 2
    scatters = 2 * steps + 4 + 2 * pieces + 1
    dma = pltpu.SemaphoreType.DMA
    scratch = [
        wide, wide, pltpu.VMEM((rows, 3 * width), BF16), pltpu.VMEM((rows, 3 * width), BF16),
        pltpu.VMEM((rows, 16), F32), pltpu.VMEM((blocks, HEADS, HEAD, HEAD), BF16), square, square, wide, wide, wide,
        full, full, full, wide, wide, pltpu.VMEM((pieces,) + flat + (WIDE,), BF16), pltpu.VMEM(flat + (width,), BF16),
        pltpu.VMEM((HEADS, HEAD, HEAD), F32), pltpu.VMEM((SPAN, width), F32), pltpu.VMEM(tokens.shape, BF16),
        pltpu.VMEM(flat + (HEAD,), BF16), pltpu.VMEM((SMALL_ROWS, width), F32), pltpu.VMEM((SMALL_ROWS // 2, width), F32),
        pltpu.VMEM((1, HEAD), F32), pltpu.VMEM((rows, 16), BF16),
        pltpu.VMEM(flat + (HEAD,), F32), pltpu.VMEM((HEAD, HEAD), F32), pltpu.VMEM((share, HEAD), BF16),
        dma((gathers, k)), dma((gathers, k)), dma((gathers,)), dma((scatters, k)), dma((scatters, k)),
        dma((2 * micro, n)), dma((2 * micro, n)), dma((2 * micro,)), dma((pieces + 5,)), pltpu.SemaphoreType.REGULAR,
    ]
    for order in (CXYZ, CYXZ):
        scratch += scatter_scratch(dims, share, HALF, order, BF16, SLOTS)
    scratch += scatter_scratch(dims, share, HEAD, CXYZ, F32)
    return pl.pallas_call(
        functools.partial(block_kernel, dims, micro, length, steps, token_rows),
        out_shape=outs,
        in_specs=[any_spec()] + [vmem_spec()] * (2 + len(smalls)) + [any_spec()] * 4,
        out_specs=[any_spec()] * 2 + [vmem_spec()] * 4 + [any_spec()] * 4,
        scratch_shapes=scratch,
        compiler_params=pltpu.CompilerParams(
            collective_id=1, has_side_effects=True, vmem_limit_bytes=VMEM_LIMIT
        ),
    )(tokens, take, back, *smalls, grad, qkv_shard, out_shard, feed_shard)[:6]


def picked(index, source):
    hot_rows = index[:, None] == jnp.arange(source.shape[0], dtype=jnp.int32)[None, :]
    return jnp.dot(low(hot_rows), source, preferred_element_type=F32).astype(BF16)


def split_rows(values, parts):
    cut = values.reshape(values.shape[:-1] + (parts, values.shape[-1] // parts))
    return jnp.moveaxis(cut, -2, 0)


def spans(width, size):
    at = 0
    while at < width:
        yield at, min(size, width - at)
        at += size


def local(
    inputs, cotangent, lengths, owners, attn_gain, query_weight, key_weight, value_weight, beta_weight,
    query_conv, key_conv, value_conv, out_gain, out_weight, mlp_gain, gate_weight, up_weight, down_weight,
):
    n = lax.axis_size("fsdp")
    me = lax.axis_index("fsdp")
    micro, _, length, width = inputs.shape
    hidden_units = gate_weight.shape[1]
    share = width // n
    if share % 16:
        return local_thin(
            inputs, cotangent, lengths, owners, attn_gain, query_weight, key_weight, value_weight, beta_weight,
            query_conv, key_conv, value_conv, out_gain, out_weight, mlp_gain, gate_weight, up_weight, down_weight,
        )
    slots = length // n
    parts = 16 // math.gcd(slots, 16)
    thin = width // parts
    token_rows = parts * slots
    i32 = jnp.int32
    devices = jnp.arange(n, dtype=i32)
    slot_ids = jnp.arange(slots, dtype=i32)
    row_ids = jnp.arange(length, dtype=i32)
    part_ids = jnp.arange(parts, dtype=i32)

    before = devices[:, None] < devices[None, :]
    starts = jnp.sum(jnp.where(before[None], lengths[:, :, None], 0), axis=1)
    match = owners[:, None, :] == devices[None, :, None]
    own_start = jnp.sum(jnp.where(match, starts[:, None, :], 0), axis=2)
    own_len = jnp.sum(jnp.where(match, lengths[:, None, :], 0), axis=2)
    mine = devices == me
    my_start = jnp.sum(jnp.where(mine, own_start, 0), axis=1)
    my_len = jnp.sum(jnp.where(mine, own_len, 0), axis=1)

    first = own_start + (me - own_start) % n
    pos = first[:, :, None] + n * slot_ids
    live = pos < (own_start + own_len)[:, :, None]
    send = jnp.where(live, pos // n, -1)[:, :, None, :]
    send = jnp.where(send >= 0, send + (part_ids * length)[:, None], -1)
    outgoing = jnp.stack(
        [picked(send[m].reshape(-1), split_rows(inputs[m, 0], parts).reshape(-1, thin)) for m in range(micro)]
    )

    active = row_ids[None] < my_len[:, None]
    block = (my_start[:, None] + row_ids) % n
    take = jnp.where(active, block * token_rows + row_ids // n, -1).astype(F32).reshape(-1, HEAD)
    grad = cotangent[:, 0].reshape(-1, width)

    back = slot_ids * n + (devices[:, None] - my_start[:, None, None]) % n
    back = jnp.where(back < my_len[:, None, None], back, -1)[:, :, None, :]
    back = (back + jnp.zeros((parts, 1), i32)).astype(F32).reshape(-1, HEAD)

    smalls = (
        query_conv, key_conv, value_conv, attn_gain[None], mlp_gain[None], out_gain[None], beta_weight
    )
    pieces = width // (2 * HEAD)
    qkv_shard = jnp.stack(
        [w.reshape(share, pieces, 2 * HEAD) for w in (query_weight, key_weight, value_weight)], axis=2
    ).reshape(share, 3 * width)
    steps = hidden_units // FFW
    feed_shard = jnp.stack(
        [w.reshape(share, steps, FFW) for w in (gate_weight, up_weight, down_weight.T)], axis=2
    ).reshape(share, 3 * hidden_units)

    result, returned, feed_grad, qkv_grad, out_grad, small_grad = block_call(
        outgoing, take, back, smalls, grad, qkv_shard, out_weight.T, feed_shard, micro
    )

    at_row = row_ids * n + me
    inside = (at_row[None, :, None] >= own_start[:, None, :]) & (
        at_row[None, :, None] < (own_start + own_len)[:, None, :]
    )
    at = devices * token_rows + (at_row[None, :, None] - first[:, None, :]) // n
    put = jnp.sum(jnp.where(inside, at + 1, 0), axis=2) - 1
    sources = jnp.arange(n * token_rows, dtype=i32)
    input_rows = jnp.concatenate(
        [
            jnp.einsum(
                "mrs,msc->mrc", low(jnp.where(put >= 0, put + p * slots, -1)[:, :, None] == sources), returned,
                preferred_element_type=F32,
            ).astype(BF16)
            for p in range(parts)
        ],
        axis=2,
    )

    small_grad = small_grad.T
    feed_grad = feed_grad.reshape(share, steps, 3, FFW)
    gate_grad, up_grad, down_grad = (
        feed_grad[:, :, i].reshape(share, hidden_units) for i in range(3)
    )
    qkv_grad = qkv_grad.reshape(share, pieces, 3, 2 * HEAD)
    query_grad, key_grad, value_grad = (qkv_grad[:, :, i].reshape(share, width) for i in range(3))
    return (
        result.reshape(micro, 1, length, width),
        input_rows.reshape(micro, 1, length, width),
        small_grad[ROW_ATTN],
        query_grad,
        key_grad,
        value_grad,
        small_grad[ROW_BETA : ROW_BETA + HEADS].T,
        small_grad[0:4],
        small_grad[4:8],
        small_grad[8:12],
        small_grad[ROW_OUT, : HEAD // n],
        out_grad.T,
        small_grad[ROW_MLP],
        gate_grad,
        up_grad,
        down_grad.T,
    )


class GatherThin:
    def __init__(self, dims, cs, shard, out, low, width, order, sems):
        self.dims, self.cs, self.order = dims, cs, order
        self.columns = pl.ds(low, width)
        self.shard, self.out = shard.at[:, self.columns], out
        self.send, self.recv, self.local_thin = sems

    def slot(self, stage, delta):
        return sum(self.dims[a] - 1 for a in self.order[:stage]) + delta - 1

    def region(self, stage, cs):
        done = self.order[:stage]
        lead = tuple(slice(None) if k in done else cs[k] for k in range(4))
        return self.out.at[lead + (slice(None), self.columns)]

    def copies(self, stage, incoming):
        axis = self.order[stage]
        for delta in range(1, self.dims[axis]):
            frm = along(self.dims, self.cs, axis, -delta) if incoming else self.cs
            to = along(self.dims, self.cs, axis, delta)
            k = self.slot(stage, delta)
            yield pltpu.make_async_remote_copy(
                src_ref=self.shard if stage == 0 else self.region(stage, self.cs),
                dst_ref=self.region(stage, frm),
                send_sem=self.send.at[k],
                recv_sem=self.recv.at[k],
                device_id=(index_of(self.dims, to),),
                device_id_type=MESH,
            )

    def keep(self):
        return pltpu.make_async_copy(self.shard, self.region(0, self.cs), self.local_thin)

    def step(self, stage):
        if stage == 0:
            self.keep().start()
        if stage == 1:
            self.keep().wait()
        if stage >= 1:
            for c in self.copies(stage - 1, True):
                c.wait_recv()
        if stage < 4:
            for c in self.copies(stage, False):
                c.start()

    def finish(self):
        for stage in range(4):
            for c in self.copies(stage, False):
                c.wait_send()


def pipelined_thin(jobs, stages, lag):
    for tick in range(len(jobs) + (stages - 1) * lag):
        for stage in range(stages):
            i = tick - stage * lag
            if 0 <= i < len(jobs):
                jobs[i].step(stage)


class TokensThin:
    def __init__(self, n, me, a, b, send, recv, local_thin):
        self.n, self.me, self.a, self.b = n, me, a, b
        self.send, self.recv, self.local_thin = send, recv, local_thin

    def copy(self, d, incoming):
        to = lax.rem(self.me + d, self.n)
        frm = lax.rem(self.me - d + self.n, self.n)
        return pltpu.make_async_remote_copy(
            src_ref=self.a.at[to],
            dst_ref=self.b.at[frm if incoming else self.me],
            send_sem=self.send.at[d],
            recv_sem=self.recv.at[d],
            device_id=(to,),
            device_id_type=MESH,
        )

    def keep(self):
        return pltpu.make_async_copy(self.a.at[self.me], self.b.at[self.me], self.local_thin)

    def each(self, act):
        def body(d, carry):
            act(d)
            return carry

        lax.fori_loop(1, self.n, body, 0)

    def start(self):
        self.keep().start()
        self.each(lambda d: self.copy(d, False).start())

    def wait(self):
        self.keep().wait()
        self.each(lambda d: self.copy(d, True).wait_recv())
        self.each(lambda d: self.copy(d, False).wait_send())


def gather_kernel_thin(dims, plan, lag, count, with_tokens, *refs):
    n = math.prod(dims)
    t = 1 if with_tokens else 0
    ins, outs, scr = refs[: count + t], refs[count + t : 2 * (count + t)], refs[2 * (count + t) :]
    send, recv, local_thin = scr[:3]
    me = lax.axis_index("fsdp")
    cs = coords_of(dims, me)
    if with_tokens:
        greet_all(n, me)
        tokens = TokensThin(n, me, ins[count], outs[count], *scr[3:])
        tokens.start()
    else:
        greet_axes(dims, cs)
    jobs = [
        GatherThin(dims, cs, ins[a], outs[a], low, width, order, (send.at[i], recv.at[i], local_thin.at[i]))
        for i, (a, low, width, order) in enumerate(plan)
    ]
    pipelined_thin(jobs, 5, lag)
    for j in jobs:
        j.finish()
    if with_tokens:
        tokens.wait()


def token_sems_thin(n):
    return [
        pltpu.SemaphoreType.DMA((n,)),
        pltpu.SemaphoreType.DMA((n,)),
        pltpu.SemaphoreType.DMA,
    ]


def gather_call_thin(shards, tokens, plan, lag, collective_id):
    n = lax.axis_size("fsdp")
    dims = grid_of(n)
    k = hops(dims)
    ins = list(shards) + ([] if tokens is None else [tokens])
    outs = [jax.ShapeDtypeStruct(dims + s.shape, s.dtype) for s in shards]
    if tokens is not None:
        outs.append(jax.ShapeDtypeStruct(tokens.shape, tokens.dtype))
    m = len(plan)
    return pl.pallas_call(
        functools.partial(gather_kernel_thin, dims, plan, lag, len(shards), tokens is not None),
        out_shape=outs,
        in_specs=[any_spec()] * len(ins),
        out_specs=[any_spec()] * len(outs),
        scratch_shapes=[
            pltpu.SemaphoreType.DMA((m, k)),
            pltpu.SemaphoreType.DMA((m, k)),
            pltpu.SemaphoreType.DMA((m,)),
        ]
        + ([] if tokens is None else token_sems_thin(n)),
        compiler_params=pltpu.CompilerParams(
            collective_id=collective_id, has_side_effects=True, vmem_limit_bytes=VMEM_LIMIT
        ),
    )(*ins)


class ScatterThin:
    def __init__(self, dims, cs, terms, result, low, width, order, scratch, sems):
        self.dims, self.cs, self.order = dims, cs, order
        self.columns = pl.ds(low, width)
        self.terms, self.result = terms, result
        self.own, self.got = scratch[0], scratch[1:]
        self.send, self.recv, self.local_thin = sems

    def slot(self, stage, delta):
        return sum(self.dims[a] - 1 for a in self.order[:stage]) + delta - 1

    def part(self, stage, at):
        axis = self.order[stage]
        if stage == 0:
            lead = tuple(at if k == axis else slice(None) for k in range(4))
            return self.terms.at[lead + (slice(None), self.columns)]
        left = [k for k in range(4) if k not in self.order[:stage]]
        return self.got[stage - 1].at[(0,) + tuple(at if k == axis else slice(None) for k in left)]

    def copies(self, stage):
        axis = self.order[stage]
        for delta in range(1, self.dims[axis]):
            to = along(self.dims, self.cs, axis, delta)
            k = self.slot(stage, delta)
            yield pltpu.make_async_remote_copy(
                src_ref=self.part(stage, to[axis]),
                dst_ref=self.got[stage].at[delta - 1],
                send_sem=self.send.at[k],
                recv_sem=self.recv.at[k],
                device_id=(index_of(self.dims, to),),
                device_id_type=MESH,
            )

    def keep(self):
        return pltpu.make_async_copy(self.part(0, self.cs[self.order[0]]), self.own, self.local_thin)

    def total(self, stage):
        axis = self.order[stage]
        left = [k for k in range(4) if k not in self.order[: stage + 1]]
        shape = [self.dims[k] for k in left]
        got = self.got[stage]
        mine = self.own if stage == 0 else self.part(stage, self.cs[axis])

        def one(i, carry):
            at = tuple(coords_of(shape, i)) if shape else ()
            total = mine[at + (slice(None), slice(None))].astype(F32)
            for delta in range(1, self.dims[axis]):
                total += got[(delta - 1,) + at + (slice(None), slice(None))].astype(F32)
            if left:
                got[(0,) + at + (slice(None), slice(None))] = total.astype(got.dtype)
            else:
                self.result[:, self.columns] = total
            return carry

        lax.fori_loop(0, math.prod(shape), one, 0)

    def step(self, stage):
        if stage == 0:
            self.keep().start()
        if stage == 1:
            self.keep().wait()
        if stage >= 1:
            for c in self.copies(stage - 1):
                c.wait_recv()
            self.total(stage - 1)
        if stage < 4:
            for c in self.copies(stage):
                c.start()

    def finish(self):
        for stage in range(4):
            for c in self.copies(stage):
                c.wait_send()


def scatter_scratch_thin(dims, rows, width, order, dtype):
    left = list(dims)
    out = [pltpu.VMEM(tuple(d for k, d in enumerate(dims) if k != order[0]) + (rows, width), dtype)]
    for s, axis in enumerate(order):
        rest = tuple(dims[k] for k in range(4) if k not in order[: s + 1])
        out.append(pltpu.VMEM((dims[axis] - 1,) + rest + (rows, width), dtype))
    return out


def scatter_kernel_thin(dims, plan, lag, count, with_tokens, *refs):
    n = math.prod(dims)
    t = 1 if with_tokens else 0
    ins, outs, scr = refs[: count + t], refs[count + t : 2 * (count + t)], refs[2 * (count + t) :]
    send, recv, local_thin = scr[:3]
    scr = scr[3:]
    me = lax.axis_index("fsdp")
    cs = coords_of(dims, me)
    if with_tokens:
        greet_all(n, me)
        tokens = TokensThin(n, me, ins[count], outs[count], *scr[:3])
        tokens.start()
        scr = scr[3:]
    else:
        greet_axes(dims, cs)
    jobs = [
        ScatterThin(
            dims, cs, ins[a], outs[a], low, width, order, scr[5 * i : 5 * i + 5],
            (send.at[i], recv.at[i], local_thin.at[i]),
        )
        for i, (a, low, width, order) in enumerate(plan)
    ]
    pipelined_thin(jobs, 5, lag)
    for j in jobs:
        j.finish()
    if with_tokens:
        tokens.wait()


def scatter_call_thin(terms, tokens, plan, lag, collective_id):
    n = lax.axis_size("fsdp")
    dims = grid_of(n)
    k = hops(dims)
    ins = list(terms) + ([] if tokens is None else [tokens])
    outs = [jax.ShapeDtypeStruct(s.shape[4:], F32) for s in terms]
    out_specs = [vmem_spec()] * len(terms)
    if tokens is not None:
        outs.append(jax.ShapeDtypeStruct(tokens.shape, tokens.dtype))
        out_specs.append(any_spec())
    m = len(plan)
    scratch = []
    for a, low, width, order in plan:
        scratch += scatter_scratch_thin(dims, terms[a].shape[4], width, order, terms[a].dtype)
    return pl.pallas_call(
        functools.partial(scatter_kernel_thin, dims, plan, lag, len(terms), tokens is not None),
        out_shape=outs,
        in_specs=[any_spec()] * len(ins),
        out_specs=out_specs,
        scratch_shapes=[
            pltpu.SemaphoreType.DMA((m, k)),
            pltpu.SemaphoreType.DMA((m, k)),
            pltpu.SemaphoreType.DMA((m,)),
        ]
        + ([] if tokens is None else token_sems_thin(n))
        + scratch,
        compiler_params=pltpu.CompilerParams(
            collective_id=collective_id, has_side_effects=True, vmem_limit_bytes=VMEM_LIMIT
        ),
    )(*ins)


def conv_thin(values, taps, row):
    total = values * taps[0:1]
    for c in range(1, taps.shape[0]):
        total += shifted(values, c, row) * taps[c : c + 1]
    return total


def project_thin(own, small, weights, attn_low, pre, queries, keys, values, beta, micro, length):
    width = own.shape[1]
    row = lax.broadcasted_iota(jnp.int32, (length, 2 * HEAD), 0)
    gain = small[ROW_ATTN : ROW_ATTN + 1, :]
    beta_rows = low(small[ROW_BETA : ROW_BETA + 16, :])

    def one(m, carry):
        rows = pl.ds(m * length, length)
        v = own[rows, :].astype(F32)
        r = lax.rsqrt(jnp.mean(v * v, axis=-1, keepdims=True) + NORM_EPS)
        attn_low[rows, :] = low(v * r * gain)
        a = attn_low[rows, :]
        beta[rows, :] = jax.nn.sigmoid(dot_nt(a, beta_rows))
        for kind, out in enumerate((queries, keys, values)):
            for b in range(width // (2 * HEAD)):
                cols = lanes(b, 2 * HEAD)
                wide = slice(kind * width + cols.start, kind * width + cols.stop)
                x = dot(a, weights[:, wide])
                pre[rows, wide] = low(x)
                c = conv_thin(x, small[4 * kind : 4 * kind + 4, cols], row)
                u = c * jax.nn.sigmoid(c)
                if kind == 2:
                    out[rows, cols] = low(u)
                    continue
                for h in range(2):
                    part = u[:, lanes(h)]
                    n = lax.rsqrt(head_sum(part * part) + UNIT_EPS)
                    out[rows, slice(cols.start + h * HEAD, cols.start + (h + 1) * HEAD)] = low(part * n)
        return carry

    lax.fori_loop(0, micro, one, 0)


def delta_block_thin(base, first, refs, gain):
    queries, keys, values, beta, state, states, inverses, scores, fresh, mix, mixed, at = refs
    rows = pl.ds(base, SPAN)
    i, j = iotas((SPAN, SPAN))
    masks = level_masks()
    eye = jnp.where(i == j, 1.0, 0.0).astype(F32)
    heads = range(HEADS)

    @pl.when(first)
    def _():
        state[...] = jnp.zeros_like(state)

    strength = beta[rows, :]
    k = [keys[rows, lanes(h)] for h in heads]
    q = [queries[rows, lanes(h)] for h in heads]
    b = [strength[:, h : h + 1] for h in heads]
    strict = [low(jnp.where(i > j, dot_nt(k[h], k[h]) * b[h], 0.0)) for h in heads]
    for h in heads:
        scores[at, h] = low(jnp.where(i >= j, dot_nt(q[h], k[h]), 0.0))
    zero = jnp.zeros((), BF16)
    inv = [eye - jnp.where(masks[0], strict[h], zero).astype(F32) for h in heads]
    for level in range(1, len(masks)):
        t = [low(inv[h]) for h in heads]
        f = [low(dot(jnp.where(masks[level], strict[h], zero), t[h])) for h in heads]
        inv = [inv[h] - dot(t[h], f[h]) for h in heads]
    for h in heads:
        inverses[at, h] = low(inv[h])
    s = [low(state[h]) for h in heads]
    for h in heads:
        states[at, h] = s[h]
    rest = [low((values[rows, lanes(h)].astype(F32) - dot(k[h], s[h])) * b[h]) for h in heads]
    new = [low(dot(inverses[at, h], rest[h])) for h in heads]
    out = [dot(q[h], s[h]) + dot(scores[at, h], new[h]) for h in heads]
    for h in heads:
        fresh[rows, lanes(h)] = new[h]
        state[h] += dot_tn(k[h], new[h])
        r = lax.rsqrt(jnp.mean(out[h] * out[h], axis=-1, keepdims=True) + NORM_EPS)
        mix[rows, lanes(h)] = low(out[h])
        mixed[rows, lanes(h)] = low(out[h] * r * gain)


def forward_kernel_thin(micro, length, *refs):
    (own, small, weights, out_weight, hidden, attn_low, pre, queries, keys, values, beta,
     states, inverses, scores, fresh, mix, mixed, state) = refs
    project_thin(own, small, weights, attn_low, pre, queries, keys, values, beta, micro, length)
    gain = small[ROW_OUT : ROW_OUT + 1, :HEAD]
    blocks = length // SPAN

    def one(t, carry):
        delta_block_thin(
            pl.multiple_of(t * SPAN, SPAN), lax.rem(t, blocks) == 0,
            (queries, keys, values, beta, state, states, inverses, scores, fresh, mix, mixed, t), gain,
        )
        rows = pl.ds(pl.multiple_of(t * SPAN, SPAN), SPAN)
        hidden[rows, :] = own[rows, :].astype(F32) + dot_nt(mixed[rows, :], out_weight[...])
        return carry

    lax.fori_loop(0, micro * blocks, one, 0)


def forward_call_thin(own, small, weights, out_weight, micro):
    rows, width = own.shape
    length = rows // micro
    blocks = rows // SPAN
    square = jax.ShapeDtypeStruct((blocks, HEADS, SPAN, SPAN), BF16)
    wide = jax.ShapeDtypeStruct((rows, width), BF16)
    outs = [
        jax.ShapeDtypeStruct((rows, width), F32), wide, jax.ShapeDtypeStruct((rows, 3 * width), BF16),
        wide, wide, wide, jax.ShapeDtypeStruct((rows, 16), F32),
        jax.ShapeDtypeStruct((blocks, HEADS, HEAD, HEAD), BF16), square, square, wide, wide, wide,
    ]
    return pl.pallas_call(
        functools.partial(forward_kernel_thin, micro, length),
        out_shape=outs,
        in_specs=[vmem_spec()] * 4,
        out_specs=[vmem_spec()] * len(outs),
        scratch_shapes=[pltpu.VMEM((HEADS, HEAD, HEAD), F32)],
        compiler_params=pltpu.CompilerParams(vmem_limit_bytes=VMEM_LIMIT),
    )(own, small, weights, out_weight)


def feed_kernel_thin(steps, hidden, grad, small, active, w_ref, result, terms, d_hidden, gain_grad, norm, total, d_norm):
    t = pl.program_id(0)
    gain = small[ROW_MLP : ROW_MLP + 1, :]

    @pl.when(t == 0)
    def _():
        v = hidden[...]
        r = lax.rsqrt(jnp.mean(v * v, axis=-1, keepdims=True) + NORM_EPS)
        norm[...] = low(v * r * gain)
        total[...] = v
        d_norm[...] = jnp.zeros_like(d_norm)

    x, g = norm[...], grad[...]
    gw, uw, dw = (w_ref[:, lanes(i, FFW)] for i in range(3))
    gate, up = dot(x, gw), dot(x, uw)
    d_act = dot(g, dw)
    s = jax.nn.sigmoid(gate)
    silu = gate * s
    act = low(silu * up)
    d_gate = low(d_act * up * (s + silu * (1.0 - s)))
    d_up = low(d_act * silu)
    total[...] += dot_nt(act, dw)
    d_norm[...] += dot_nt(d_gate, gw) + dot_nt(d_up, uw)
    terms[:, lanes(0, FFW)] = low(dot_tn(x, d_gate))
    terms[:, lanes(1, FFW)] = low(dot_tn(x, d_up))
    terms[:, lanes(2, FFW)] = low(dot_tn(g, act))

    @pl.when(t == steps - 1)
    def _():
        result[...] = low(jnp.where(active[...] > 0.0, total[...], 0.0))
        v, d = hidden[...], d_norm[...]
        n = v.shape[1]
        r = lax.rsqrt(jnp.mean(v * v, axis=-1, keepdims=True) + NORM_EPS)
        vr = v * r
        gain_grad[...] = jnp.sum(d * vr, axis=0, keepdims=True)
        gd = d * gain
        d_hidden[...] = g.astype(F32) + r * (gd - vr * (jnp.sum(vr * gd, axis=-1, keepdims=True) / n))


def feed_call_thin(hidden, grad, small, active, weights):
    rows, width = hidden.shape
    steps = weights.shape[1] // (3 * FFW)
    whole = lambda *shape: pl.BlockSpec(shape, lambda t: (0,) * len(shape))
    block = pl.BlockSpec((width, 3 * FFW), lambda t: (0, t))
    return pl.pallas_call(
        functools.partial(feed_kernel_thin, steps),
        grid=(steps,),
        out_shape=[
            jax.ShapeDtypeStruct((rows, width), BF16),
            jax.ShapeDtypeStruct(weights.shape, BF16),
            jax.ShapeDtypeStruct((rows, width), F32),
            jax.ShapeDtypeStruct((1, width), F32),
        ],
        in_specs=[whole(rows, width), whole(rows, width), whole(*small.shape), whole(rows, 1), block],
        out_specs=[whole(rows, width), block, whole(rows, width), whole(1, width)],
        scratch_shapes=[
            pltpu.VMEM((rows, width), BF16),
            pltpu.VMEM((rows, width), F32),
            pltpu.VMEM((rows, width), F32),
        ],
        compiler_params=pltpu.CompilerParams(
            vmem_limit_bytes=VMEM_LIMIT, dimension_semantics=("arbitrary",)
        ),
    )(hidden, grad, small, active, weights)


def delta_back_thin(base, last, refs, gain):
    (queries, keys, values, beta, states, inverses, scores, fresh, mix, d_mixed,
     d_state, d_out, d_q, d_k, d_v, d_beta, gain_grad, at) = refs
    rows = pl.ds(base, SPAN)
    i, j = iotas((SPAN, SPAN))
    lane = lax.broadcasted_iota(jnp.int32, (SPAN, 16), 1)
    heads = range(HEADS)

    @pl.when(last)
    def _():
        d_state[...] = jnp.zeros_like(d_state)

    strength = beta[rows, :]
    k = [keys[rows, lanes(h)] for h in heads]
    q = [queries[rows, lanes(h)] for h in heads]
    e = [fresh[rows, lanes(h)] for h in heads]
    b = [strength[:, h : h + 1] for h in heads]
    kb = [low(k[h].astype(F32) * b[h]) for h in heads]
    do = []
    for h in heads:
        v, d = mix[rows, lanes(h)].astype(F32), d_mixed[:, lanes(h)]
        r = lax.rsqrt(jnp.mean(v * v, axis=-1, keepdims=True) + NORM_EPS)
        vr, gd = v * r, d * gain
        gain_grad[...] += jnp.sum(d * vr, axis=0, keepdims=True)
        do.append(low(r * (gd - vr * jnp.mean(vr * gd, axis=-1, keepdims=True))))
    s = [states[at, h] for h in heads]
    p = [scores[at, h] for h in heads]
    ds = [low(d_state[h]) for h in heads]
    de = [low(dot_tn(p[h], do[h]) + dot(k[h], ds[h])) for h in heads]
    dx = [dot_tn(inverses[at, h], de[h]) for h in heads]
    dxl = [low(dx[h]) for h in heads]
    dp = [low(jnp.where(i >= j, dot_nt(do[h], e[h]), 0.0)) for h in heads]
    da = [low(jnp.where(i > j, -dot_nt(dxl[h], e[h]), 0.0)) for h in heads]
    dkb = [dot(da[h], k[h]) - dot_nt(dxl[h], s[h]) for h in heads]
    beta_grad = jnp.zeros((SPAN, 16), F32)
    for h in heads:
        d_q[rows, lanes(h)] = low(dot_nt(do[h], s[h]) + dot(dp[h], k[h]))
        d_k[rows, lanes(h)] = low(
            dkb[h] * b[h] + dot_tn(da[h], kb[h]) + dot_tn(dp[h], q[h]) + dot_nt(e[h], ds[h])
        )
        d_v[rows, lanes(h)] = low(dx[h] * b[h])
        d_state[h] += dot_tn(q[h], do[h]) - dot_tn(kb[h], dxl[h])
        db = head_sum(dkb[h] * k[h].astype(F32) + dx[h] * values[rows, lanes(h)].astype(F32))
        beta_grad += jnp.where(lane == h, db, 0.0)
    d_beta[rows, :] = low(beta_grad * strength * (1.0 - strength))


def backward_kernel_thin(micro, length, *refs):
    (d_hidden, own, small, weights, out_weight, attn_low, pre, queries, keys, values, beta,
     states, inverses, scores, fresh, mix, mixed,
     d_own, qkv_grad, out_grad, small_grad,
     d_state, d_out, d_q, d_k, d_v, d_beta, d_pre, d_attn, gain_grad) = refs
    width = own.shape[1]
    blocks = length // SPAN
    total = micro * blocks
    gain = small[ROW_OUT : ROW_OUT + 1, :HEAD]
    gain_grad[...] = jnp.zeros_like(gain_grad)
    small_grad[...] = jnp.zeros_like(small_grad)
    d_attn[...] = low(d_hidden[...])

    def one(step, carry):
        t = total - 1 - step
        base = pl.multiple_of(t * SPAN, SPAN)
        d_out[...] = dot(d_attn[pl.ds(base, SPAN), :], out_weight[...])
        delta_back_thin(
            base, lax.rem(step, blocks) == 0,
            (queries, keys, values, beta, states, inverses, scores, fresh, mix, d_out,
             d_state, None, d_q, d_k, d_v, d_beta, gain_grad, t), gain,
        )
        return carry

    lax.fori_loop(0, total, one, 0)
    row = lax.broadcasted_iota(jnp.int32, (length, HEAD), 0)

    def conv_back(m, carry):
        rows = pl.ds(m * length, length)
        for kind, grads in enumerate((d_q, d_k, d_v)):
            for h in range(width // HEAD):
                cols = lanes(h)
                wide = slice(kind * width + cols.start, kind * width + cols.stop)
                taps = small[4 * kind : 4 * kind + 4, cols]
                x = pre[rows, wide].astype(F32)
                moved = [shifted(x, c, row) for c in range(4)]
                c = moved[0] * taps[0:1]
                for o in range(1, 4):
                    c += moved[o] * taps[o : o + 1]
                s = jax.nn.sigmoid(c)
                u = c * s
                d = grads[rows, cols].astype(F32)
                if kind < 2:
                    n = lax.rsqrt(head_sum(u * u) + UNIT_EPS)
                    un = u * n
                    d = (d - un * head_sum(un * d)) * n
                d = d * (s + u * (1.0 - s))
                for o in range(4):
                    at = slice(4 * kind + o, 4 * kind + o + 1)
                    small_grad[at, cols] += jnp.sum(moved[o] * d, axis=0, keepdims=True)
                back = d * taps[0:1]
                for o in range(1, 4):
                    back += shifted(d, -o, row) * taps[o : o + 1]
                d_pre[rows, wide] = low(back)
        return carry

    lax.fori_loop(0, micro, conv_back, 0)
    for b in range(width // 256):
        cols = lanes(b, 256)
        out_grad[:, cols] = low(dot_tn(d_attn[...], mixed[:, cols]))
    for b in range(3 * width // 256):
        cols = lanes(b, 256)
        qkv_grad[:, cols] = low(dot_tn(attn_low[...], d_pre[:, cols]))
    beta_rows = low(small[ROW_BETA : ROW_BETA + 16, :])
    small_grad[ROW_BETA : ROW_BETA + 16, :] = dot_tn(d_beta[...], attn_low[...])
    small_grad[ROW_OUT : ROW_OUT + 1, :HEAD] = gain_grad[...]
    attn_gain = small[ROW_ATTN : ROW_ATTN + 1, :]

    def finish(t, carry):
        rows = pl.ds(pl.multiple_of(t * SPAN, SPAN), SPAN)
        d = dot_nt(d_pre[rows, :], weights[...]) + dot(d_beta[rows, :], beta_rows)
        v = own[rows, :].astype(F32)
        r = lax.rsqrt(jnp.mean(v * v, axis=-1, keepdims=True) + NORM_EPS)
        vr, gd = v * r, d * attn_gain
        small_grad[ROW_ATTN : ROW_ATTN + 1, :] += jnp.sum(d * vr, axis=0, keepdims=True)
        d_own[rows, :] = low(d_hidden[rows, :] + r * (gd - vr * jnp.mean(vr * gd, axis=-1, keepdims=True)))
        return carry

    lax.fori_loop(0, total, finish, 0)


def backward_call_thin(d_hidden, own, small, weights, out_weight, saved, micro):
    rows, width = own.shape
    length = rows // micro
    return pl.pallas_call(
        functools.partial(backward_kernel_thin, micro, length),
        out_shape=[
            jax.ShapeDtypeStruct((rows, width), BF16),
            jax.ShapeDtypeStruct((width, 3 * width), BF16),
            jax.ShapeDtypeStruct((width, width), BF16),
            jax.ShapeDtypeStruct((SMALL_ROWS, width), F32),
        ],
        in_specs=[vmem_spec()] * (5 + len(saved)),
        out_specs=[vmem_spec()] * 4,
        scratch_shapes=[
            pltpu.VMEM((HEADS, HEAD, HEAD), F32),
            pltpu.VMEM((SPAN, width), F32),
            pltpu.VMEM((rows, width), BF16),
            pltpu.VMEM((rows, width), BF16),
            pltpu.VMEM((rows, width), BF16),
            pltpu.VMEM((rows, 16), BF16),
            pltpu.VMEM((rows, 3 * width), BF16),
            pltpu.VMEM((rows, width), BF16),
            pltpu.VMEM((1, HEAD), F32),
        ],
        compiler_params=pltpu.CompilerParams(vmem_limit_bytes=VMEM_LIMIT),
    )(d_hidden, own, small, weights, out_weight, *saved)


def local_thin(
    inputs, cotangent, lengths, owners, attn_gain, query_weight, key_weight, value_weight, beta_weight,
    query_conv, key_conv, value_conv, out_gain, out_weight, mlp_gain, gate_weight, up_weight, down_weight,
):
    n = lax.axis_size("fsdp")
    dims = grid_of(n)
    me = lax.axis_index("fsdp")
    micro, _, length, width = inputs.shape
    hidden_units = gate_weight.shape[1]
    share = width // n
    slots = length // n
    per = micro * slots
    parts = 16 // math.gcd(per, 16)
    thin = width // parts
    i32 = jnp.int32
    devices = jnp.arange(n, dtype=i32)
    slot_ids = jnp.arange(slots, dtype=i32)
    row_ids = jnp.arange(length, dtype=i32)
    micros = jnp.arange(micro, dtype=i32)
    part_ids = jnp.arange(parts, dtype=i32)

    before = devices[:, None] < devices[None, :]
    starts = jnp.sum(jnp.where(before[None], lengths[:, :, None], 0), axis=1)
    match = owners[:, None, :] == devices[None, :, None]
    own_start = jnp.sum(jnp.where(match, starts[:, None, :], 0), axis=2)
    own_len = jnp.sum(jnp.where(match, lengths[:, None, :], 0), axis=2)
    mine = devices == me
    my_start = jnp.sum(jnp.where(mine, own_start, 0), axis=1)
    my_len = jnp.sum(jnp.where(mine, own_len, 0), axis=1)

    first = own_start + (me - own_start) % n
    pos = first[:, :, None] + n * slot_ids
    live = pos < (own_start + own_len)[:, :, None]
    send = jnp.where(live, micros[:, None, None] * length + pos // n, -1)
    send = jnp.moveaxis(send, 0, 1)[:, None] + jnp.zeros((1, parts, 1, 1), i32)
    send = jnp.where(send >= 0, send + (part_ids * micro * length)[None, :, None, None], -1)
    rows_in = split_rows(inputs[:, 0].reshape(micro * length, width), parts).reshape(-1, thin)
    outgoing = picked(send.reshape(-1), rows_in).reshape(n, parts * per, thin)

    def row_of(v):
        return jnp.pad(v, ((0, 0), (0, share - v.shape[1])))

    packed = jnp.concatenate([
        query_conv, key_conv, value_conv, attn_gain[None], mlp_gain[None], row_of(out_gain[None]),
        jnp.zeros((1, share), BF16), beta_weight.T, jnp.zeros((SMALL_ROWS - 16 - HEADS, share), BF16),
    ])
    count = SMALL_ROWS * share // HEAD
    packed = jnp.pad(packed.reshape(count, HEAD), ((0, -count % 16), (0, 0)))

    attn_shard = jnp.concatenate([query_weight, key_weight, value_weight, out_weight.T], axis=1)
    steps = hidden_units // FFW
    feed_shard = jnp.stack(
        [w.reshape(share, steps, FFW) for w in (gate_weight, up_weight, down_weight.T)], axis=2
    ).reshape(share, 3 * hidden_units)

    plan = [(0, 0, HEAD, ZXY)]
    for a, (w, size) in enumerate(((4 * width, 512), (3 * hidden_units, 768)), 1):
        for at, wide in spans(w, size):
            plan.append((a, at, wide, (ZXY, ZYX)[len(plan) % 2]))
    small_all, attn_all, feed_all, incoming = gather_call_thin(
        [packed, attn_shard, feed_shard], outgoing, tuple(plan), 2, 1
    )
    small = small_all.reshape(n, -1)[:, : SMALL_ROWS * share].reshape(n, SMALL_ROWS, share)
    small = jnp.moveaxis(small, 1, 0)
    gain_row = small[ROW_OUT, :, : HEAD // n].reshape(1, HEAD)
    small = small.reshape(SMALL_ROWS, width).astype(F32)
    small = lax.dynamic_update_slice(small, gain_row.astype(F32), (ROW_OUT, 0))
    attn_all = attn_all.reshape(width, 4 * width)
    feed_all = feed_all.reshape(width, 3 * hidden_units)
    qkv, out_t = attn_all[:, : 3 * width], attn_all[:, 3 * width :]

    active = row_ids[None] < my_len[:, None]
    block = (my_start[:, None] + row_ids) % n
    at = block * (parts * per) + micros[:, None] * slots + row_ids // n
    take = jnp.where(active, at, -1).reshape(-1)
    flat = incoming.reshape(n * parts * per, thin)
    own = jnp.concatenate(
        [picked(jnp.where(take >= 0, take + p * per, -1), flat) for p in range(parts)], axis=1
    )
    active = active.reshape(-1, 1)
    grad = jnp.where(active, cotangent[:, 0].reshape(-1, width), jnp.zeros((), BF16))

    hidden, *saved = forward_call_thin(own, small, qkv, out_t, micro)
    result, feed_terms, d_hidden, mlp_gain_grad = feed_call_thin(
        hidden, grad, small, active.astype(F32), feed_all
    )
    d_own, qkv_terms, out_terms, small_terms = backward_call_thin(
        d_hidden, own, small, qkv, out_t, saved, micro
    )

    back = slot_ids * n + (devices[:, None, None] - my_start[None, :, None]) % n
    back = jnp.where(back < my_len[None, :, None], back + (micros * length)[None, :, None], -1)
    back = back[:, None] + jnp.zeros((1, parts, 1, 1), i32)
    back = jnp.where(back >= 0, back + (part_ids * micro * length)[None, :, None, None], -1)
    returning = picked(back.reshape(-1), split_rows(d_own, parts).reshape(-1, thin))
    returning = returning.reshape(n, parts * per, thin)

    small_terms = lax.dynamic_update_slice(small_terms, mlp_gain_grad, (ROW_MLP, 0))
    out_gain_terms = jnp.pad(small_terms[ROW_OUT, :HEAD].reshape(n, -1), ((0, 0), (0, share - HEAD // n)))
    small_terms = jnp.concatenate(
        [small_terms[:ROW_OUT].reshape(ROW_OUT, n, share), out_gain_terms[None],
         small_terms[ROW_OUT + 1 :].reshape(SMALL_ROWS - ROW_OUT - 1, n, share)]
    )
    small_terms = jnp.moveaxis(small_terms, 1, 0).reshape(n, count, HEAD)
    small_terms = jnp.pad(small_terms, ((0, 0), (0, -count % 16), (0, 0)))
    terms = [
        small_terms.reshape(dims + small_terms.shape[1:]),
        qkv_terms.reshape(dims + (share, 3 * width)),
        out_terms.reshape(dims + (share, width)),
        feed_terms.reshape(dims + (share, 3 * hidden_units)),
    ]
    plan = []
    for a, size in ((3, 768), (2, 512), (1, 512), (0, HEAD)):
        for lo, wide in spans(terms[a].shape[5], size):
            plan.append((a, lo, wide, (CXYZ, CYXZ)[len(plan) % 2]))
    small_grad, qkv_grad, out_grad, feed_grad, returned = scatter_call_thin(
        terms, returning, tuple(plan), 2, 2
    )

    place = row_ids * n + me
    inside = (place[None, :, None] >= own_start[:, None, :]) & (
        place[None, :, None] < (own_start + own_len)[:, None, :]
    )
    at = devices * (parts * per) + micros[:, None, None] * slots + (place[None, :, None] - first[:, None, :]) // n
    take = (jnp.sum(jnp.where(inside, at + 1, 0), axis=2) - 1).reshape(-1)
    flat = returned.reshape(n * parts * per, thin)
    input_rows = jnp.concatenate(
        [picked(jnp.where(take >= 0, take + p * per, -1), flat) for p in range(parts)], axis=1
    )

    small_grad = small_grad.reshape(-1)[: SMALL_ROWS * share].reshape(SMALL_ROWS, share)
    feed_grad = feed_grad.reshape(share, steps, 3, FFW)
    gate_grad, up_grad, down_grad = (
        feed_grad[:, :, i].reshape(share, hidden_units) for i in range(3)
    )
    return (
        result.reshape(micro, 1, length, width),
        input_rows.reshape(micro, 1, length, width),
        small_grad[ROW_ATTN],
        qkv_grad[:, :width],
        qkv_grad[:, width : 2 * width],
        qkv_grad[:, 2 * width :],
        small_grad[ROW_BETA : ROW_BETA + HEADS].T,
        small_grad[0:4],
        small_grad[4:8],
        small_grad[8:12],
        small_grad[ROW_OUT, : HEAD // n],
        out_grad.T,
        small_grad[ROW_MLP],
        gate_grad,
        up_grad,
        down_grad.T,
    )


def solution(mesh):
    rows, cols, flat = P("fsdp", None), P(None, "fsdp"), P("fsdp")
    data = P(None, "fsdp", None, None)
    return jax.shard_map(
        local,
        mesh=mesh,
        in_specs=(
            data, data, P(), P(), flat, rows, rows, rows, rows, cols, cols, cols, flat, cols, flat, rows, rows, cols,
        ),
        out_specs=(
            data, data, flat, rows, rows, rows, rows, cols, cols, cols, flat, cols, flat, rows, rows, cols,
        ),
        check_vma=False,
    )
```
